32 devices in a mesh: seq: 4 (over z), vocab: 8 (over y, x, core).
Axes of the slice: x: 2, y: 2, z: 4, core: 2. Of those that a mesh axis runs over, the one named last changes fastest.
Arguments:
- token_identifiers: int32 [2, 4096], P(None, 'seq'), may hold values from 0 to 32767
- targets: int32 [2, 4096], P(None, 'seq'), may hold values from 0 to 32767
- row_group_index: int32 [2, 2], replicated, may hold values from 1 to 3, as said below
- answer_length: int32 [2, 2], replicated, may hold values from 2560 to 3072
- embedding: float32 [2048, 32768], P('seq', 'vocab'), may hold values from -6 to 6
- embedding_first_moment: float32 [2048, 32768], P('seq', 'vocab'), may hold values from -0.00021362305 to 0.00021362305
- embedding_second_moment: float32 [2048, 32768], P('seq', 'vocab'), may hold values from 7.450581e-12 to 1.192093e-10
- output_head_table: bfloat16 [2048, 32768], P('seq', 'vocab'), may hold values from -0.333666012 to 0.333666012
- query_projection: bfloat16 [2048, 2, 1024], P('seq', None, 'vocab'), may hold values from -0.125 to 0.125
- keyval_projection: bfloat16 [2048, 512], P('seq'), may hold values from -0.125 to 0.125
- output_projection: bfloat16 [2048, 2, 1024], P('seq', None, 'vocab'), may hold values from -0.5 to 0.5
- gate_up_projection: bfloat16 [2048, 2, 5632], P('seq', None, 'vocab'), may hold values from -0.125 to 0.125
- down_projection: bfloat16 [2048, 5632], P('seq', 'vocab'), may hold values from -0.078125 to 0.078125
- gains: float32 [3, 2048], replicated, may hold values from 0.5 to 1.5
- gain_first_moment: float32 [3, 2048], replicated, may hold values from -0.00390625 to 0.00390625
- gain_second_moment: float32 [3, 2048], replicated, may hold values from 3.2552083e-09 to 5.2083333e-08
- adapter_input_maps: float32 [4, 2048, 8], replicated, may hold values from -0.125 to 0.125
- input_map_momentum: float32 [4, 2048, 8], replicated, may hold values from -0.015625 to 0.015625
- adapter_up_maps: float32 [2, 8, 2048], replicated, may hold values from -0.75 to 0.75
- up_momentum: float32 [2, 8, 2048], replicated, may hold values from -0.0234375 to 0.0234375
- adapter_keyval_maps: float32 [2, 8, 256], replicated, may hold values from -0.75 to 0.75
- keyval_momentum: float32 [2, 8, 256], replicated, may hold values from -0.0625 to 0.0625
Outputs:
- loss_total_sum: float32 [], replicated
- loss_token_count: float32 [], replicated
- gradient_norm: float32 [], replicated
- embedding_first_next: float32 [2048, 32768], P('seq', 'vocab')
- embedding_second_next: float32 [2048, 32768], P('seq', 'vocab')
- embedding_next: float32 [2048, 32768], P('seq', 'vocab')
- gain_first_next: float32 [3, 2048], replicated
- gain_second_next: float32 [3, 2048], replicated
- gains_next: float32 [3, 2048], replicated
- input_map_momentum_next: float32 [4, 2048, 8], replicated
- adapter_input_next: float32 [4, 2048, 8], replicated
- up_momentum_next: float32 [2, 8, 2048], replicated
- adapter_up_next: float32 [2, 8, 2048], replicated
- keyval_momentum_next: float32 [2, 8, 256], replicated
- adapter_keyval_next: float32 [2, 8, 256], replicated
The draws below stay inside these ranges and needn't reach their ends.
Inputs may be any that keep to these rules, and one draw needn't show every extreme that they name: Row r of micro-batch b holds row_group_index[b, r] groups of 1024 tokens after the rows before it; each micro-batch's rows fill all its groups; every micro-batch has a row of 3 groups and one of 1. The last answer_length[b, r] tokens of row r are counted, all of them where the row is shorter.
All inputs are finite; a program needn't handle non-finite values.
Results may differ from the reference program's by a relative error of at most 0.0078.
Values may be sent and summed in bfloat16 or wider, within the bound.
A program may use at most 256 MiB of HBM per device.

```python
import math
import jax
import jax.numpy as jnp
import numpy as np
from jax import lax

MODEL_WIDTH = 2048
QUERY_HEADS = 32
KEY_HEADS = 4
HEAD_SIZE = 64
FF = 5632
VOCAB = 32768
GROUP = 1024
ADAPTER_RANK = 8
MB = 2
STEP = 10
ROWS = 2
TOKENS = 4096
HL = 2
N_SEQ = 4


def draw_output_head_table(key, part):
    key = jax.random.fold_in(key, 11)
    base_key, block_key = jax.random.split(key)
    rising = 2.0
    base = jax.random.truncated_normal(base_key, -4.0, 4.0, (MODEL_WIDTH, VOCAB), jnp.float32)
    column = jnp.arange(VOCAB, dtype=jnp.float32) / VOCAB
    block_factor = jax.random.uniform(block_key, (64,), jnp.float32, 0.75, 1.25)
    per_column = jnp.repeat(block_factor, VOCAB // 64)
    return (base * ((1.0 + rising * column) * per_column)[None, :] / math.sqrt(MODEL_WIDTH)).astype(jnp.bfloat16)


def draw_row_group_index(key, part):
    key = jax.random.fold_in(key, 23)
    pick_key, order_key = jax.random.split(key)
    pick = jax.random.randint(pick_key, (MB,), min(1, ROWS - 2), max(ROWS - 2, 1))
    order = jax.random.randint(order_key, (MB,), 0, 2)
    index = jnp.arange(ROWS, dtype=jnp.int32)[None, :]
    first = jnp.where(order == 1, 3, 1)[:, None]
    second = 4 - first
    result = jnp.where(index == pick[:, None], first, jnp.where(index == pick[:, None] + 1, second, 2))
    return result.astype(jnp.int32)


def with_ends(values, rng, low, top_value):
    longest = values.shape.index(max(values.shape))
    spots = []
    for shift in (0, 1):
        where = [jax.random.randint(jax.random.fold_in(rng, axis), (), 0, length) for axis, length in enumerate(values.shape)]
        where[longest] = (where[longest] + shift) % values.shape[longest]
        spots.append(tuple(where))
    return values.at[spots[0]].set(low).at[spots[1]].set(top_value)


def shard_levels(own_key, extent, cuts, smallest, top_value):
    def one(axis_at, blocks):
        steps = jax.random.uniform(jax.random.fold_in(jax.random.fold_in(own_key, 6), axis_at), (blocks,), jnp.float32, smallest / len(cuts), top_value / len(cuts))
        return jnp.repeat(jnp.exp(steps), extent[axis_at] // blocks).reshape((-1,) + (1,) * (len(extent) - axis_at - 1))

    loudness = one(*cuts[0])
    for cut in cuts[1:]:
        loudness = loudness * one(*cut)
    return loudness


def rank_bounds(amount, skew):
    portions = [(1 << 20) // math.isqrt(rank ** skew) + 1 for rank in range(1, amount + 1)]
    deviation = 1 + sum(portions) // (1 << 30)
    return np.cumsum(np.array([max(1, weight // deviation) for weight in portions]))


def skewed_ids(stream_key, dims, count, skew):
    table = rank_bounds(count, skew)
    lot = jax.random.randint(jax.random.fold_in(stream_key, 1), dims, 0, int(table[count - 1]))
    rank = jnp.searchsorted(jnp.asarray(table, jnp.int32), lot, side="right")
    return jax.random.permutation(jax.random.fold_in(stream_key, 2), count)[rank].astype(jnp.int32)


def scatter_about(own_key, extent, spread, limit, pieces=(), kind=jnp.bfloat16):
    loudness = shard_levels(own_key, extent, pieces, -0.22, 0.18) if pieces else 1.0
    values = jax.random.normal(own_key, extent, jnp.float32) * spread * loudness
    return jnp.minimum(jnp.maximum(values, -limit), limit).astype(kind)


def setup_inputs(seed: int = 0) -> dict:
    seeds = jax.random.split(jax.random.key(seed), 23)
    return {
        "token_identifiers": with_ends(skewed_ids(seeds[0], (MB, TOKENS), VOCAB, 2), jax.random.fold_in(seeds[0], 3), 0, VOCAB - 1).astype(jnp.int32),
        "targets": with_ends(skewed_ids(seeds[1], (MB, TOKENS), VOCAB, 2), jax.random.fold_in(seeds[1], 3), 0, VOCAB - 1).astype(jnp.int32),
        "row_group_index": draw_row_group_index(jax.random.fold_in(seeds[22], 71), 0),
        "answer_length": with_ends(jax.random.randint(seeds[3], (MB, ROWS), 5 * GROUP // 2, 3 * GROUP + 1), jax.random.fold_in(seeds[3], 1), 5 * GROUP // 2, 3 * GROUP).astype(jnp.int32),
        "embedding": scatter_about(seeds[4], (MODEL_WIDTH, VOCAB), 1.0, 6.0, ((0, 4), (1, 8)), jnp.float32),
        "embedding_first_moment": scatter_about(seeds[5], (MODEL_WIDTH, VOCAB), (0.11 / (MODEL_WIDTH * VOCAB) ** 0.5), 0.00021362305, ((0, 4), (1, 8)), jnp.float32),
        "embedding_second_moment": jnp.clip(jnp.exp(math.log(1.1920929521291868e-10) - 2.7725887 * jax.random.uniform(seeds[6], (MODEL_WIDTH, VOCAB), jnp.float32) ** shard_levels(seeds[6], (MODEL_WIDTH, VOCAB), ((0, 4), (1, 8)), -0.2, 0.2)), 7.450580950807417e-12, 1.1920929521291868e-10),
        "output_head_table": draw_output_head_table(jax.random.fold_in(seeds[22], 71), 0),
        "query_projection": scatter_about(seeds[8], (MODEL_WIDTH, 2, QUERY_HEADS * HEAD_SIZE // 2), MODEL_WIDTH ** -0.5, 0.125, ((0, 4), (2, 8))),
        "keyval_projection": scatter_about(seeds[9], (MODEL_WIDTH, 2 * KEY_HEADS * HEAD_SIZE), MODEL_WIDTH ** -0.5, 0.125, ((0, 4),)),
        "output_projection": scatter_about(seeds[10], (MODEL_WIDTH, 2, QUERY_HEADS * HEAD_SIZE // 2), (MODEL_WIDTH // 16) ** -0.5, 0.5, ((0, 4), (2, 8))),
        "gate_up_projection": scatter_about(seeds[11], (MODEL_WIDTH, 2, FF), MODEL_WIDTH ** -0.5, 0.125, ((0, 4), (2, 8))),
        "down_projection": scatter_about(seeds[12], (MODEL_WIDTH, FF), FF ** -0.5, 0.078125, ((0, 4), (1, 8))),
        "gains": jnp.clip(1.0 + 0.1 * jax.random.normal(seeds[13], (3, MODEL_WIDTH), jnp.float32), 0.5, 1.5),
        "gain_first_moment": scatter_about(seeds[14], (3, MODEL_WIDTH), (0.02 / (3 * MODEL_WIDTH) ** 0.5), 0.00390625, (), jnp.float32),
        "gain_second_moment": jnp.clip(jnp.exp(jax.random.uniform(seeds[15], (3, MODEL_WIDTH), jnp.float32, math.log(3.2552083251147224e-09), math.log(5.208333320183556e-08))), 3.2552083251147224e-09, 5.208333320183556e-08),
        "adapter_input_maps": scatter_about(seeds[16], (4, MODEL_WIDTH, ADAPTER_RANK), MODEL_WIDTH ** -0.5, 0.125, (), jnp.float32),
        "input_map_momentum": scatter_about(seeds[17], (4, MODEL_WIDTH, ADAPTER_RANK), (0.3 / (4 * MODEL_WIDTH * ADAPTER_RANK) ** 0.5), 0.015625, (), jnp.float32),
        "adapter_up_maps": scatter_about(seeds[18], (2, ADAPTER_RANK, MODEL_WIDTH), 0.05, 0.75, (), jnp.float32),
        "up_momentum": scatter_about(seeds[19], (2, ADAPTER_RANK, MODEL_WIDTH), (0.3 / (2 * MODEL_WIDTH * ADAPTER_RANK) ** 0.5), 0.0234375, (), jnp.float32),
        "adapter_keyval_maps": scatter_about(seeds[20], (2, ADAPTER_RANK, KEY_HEADS * HEAD_SIZE), 0.05, 0.75, (), jnp.float32),
        "keyval_momentum": scatter_about(seeds[21], (2, ADAPTER_RANK, KEY_HEADS * HEAD_SIZE), (0.3 / (2 * KEY_HEADS * HEAD_SIZE * ADAPTER_RANK) ** 0.5), 0.0625, (), jnp.float32),
    }


ADAPTER_SCALE = 2.0
NORM_EPS = 1e-05
Z_WEIGHT = 0.0001
CLIP_NORM = 1.0
ROPE_BASE = 10000.0
MASKED = -1e+30
MUON_MOMENTUM = 0.95
MUON_RATE = 0.1
ADAM_RATE = 0.3
BETA_FIRST = 0.9
BETA_SECOND = 0.999
ADAM_EPS = 1e-08
DECAY_RATE = 0.01
SCHULZ = (3.4445, -4.775, 2.0315)
PRECISE = lax.Precision.HIGHEST

@jax.custom_vjp
def lowrank_input(v):
    return lax.optimization_barrier(v.astype(jnp.bfloat16)).astype(jnp.float32)

@jax.custom_vjp
def low_back(v):
    return v

def low_keep(v):
    return (lowrank_input(v), None)

def low_pass(kept, grad):
    return (grad,)

def back_keep(v):
    return (v, None)

def back_low(kept, grad):
    return (lowrank_input(grad),)
lowrank_input.defvjp(low_keep, low_pass)
low_back.defvjp(back_keep, back_low)

def precise_product(left, right):
    return jnp.dot(left, right, precision=PRECISE)

def rms_norm(values, gain):
    return values * lax.rsqrt(lax.optimization_barrier(jnp.mean(values * values, axis=-1, keepdims=True)) + NORM_EPS) * gain

def rotate(values, positions):
    half_width = values.shape[-1] // 2
    freqs = ROPE_BASE ** (-2.0 * jnp.arange(half_width, dtype=jnp.float32) / values.shape[-1])
    angles = positions.astype(jnp.float32)[:, None] * freqs[None, :]
    cosine = jnp.cos(angles)[:, None, :]
    sine = jnp.sin(angles)[:, None, :]
    first, second = (values[..., :half_width], values[..., half_width:])
    return jnp.concatenate([first * cosine - second * sine, second * cosine + first * sine], axis=-1)

def layout(groups, count):
    ends = jnp.cumsum(groups)
    index = jnp.arange(count, dtype=jnp.int32)
    row_of = lax.optimization_barrier(jnp.sum((ends[None, :] <= index[:, None]).astype(jnp.int32), axis=1))
    length = groups[row_of]
    row_start = ends[row_of] - length
    source = jnp.where(index > row_start, index - 1, row_start + length - 1)
    return (row_of, row_start, length, source)

def allowed_keys(shifted):
    half_group = GROUP // 2
    rows = jnp.arange(GROUP, dtype=jnp.int32)[:, None]
    slots = jnp.arange(GROUP + half_group, dtype=jnp.int32)[None, :] - half_group
    plain = (slots >= 0) & (slots <= rows)
    moved = jnp.where(rows < half_group, slots <= rows, (slots >= half_group) & (slots <= rows))
    return jnp.where(shifted, moved, plain)

def attend_copy(packed):
    queries, keys, values, shifted = packed
    scores = jnp.einsum('ihd,kd->hik', queries, keys, precision=PRECISE) * HEAD_SIZE ** (-0.5)
    scores = low_back(jnp.where(allowed_keys(shifted)[None], scores, MASKED))
    peak = lax.optimization_barrier(jnp.max(scores, axis=-1, keepdims=True))
    terms = jnp.exp(scores - peak)
    probs = terms / lax.optimization_barrier(jnp.sum(terms, axis=-1, keepdims=True))
    return jnp.einsum('hik,kd->ihd', lowrank_input(probs), values, precision=PRECISE)

def attend_group(packed):
    queries, keys, values = packed
    copies = queries.shape[1]
    shifted = jnp.arange(copies) >= copies // 2
    outputs = lax.map(jax.checkpoint(attend_copy), (jnp.moveaxis(queries, 1, 0), jnp.moveaxis(keys, 1, 0), jnp.moveaxis(values, 1, 0), shifted))
    return jnp.moveaxis(outputs, 0, 1)

def loss_block(packed, table):
    normalized_input, wanted, counted = packed
    logits = low_back(precise_product(normalized_input, table))
    peak = lax.optimization_barrier(jnp.max(logits, axis=-1, keepdims=True))
    log_total = peak[:, 0] + jnp.log(lax.optimization_barrier(jnp.sum(jnp.exp(logits - peak), axis=-1)))
    picked = jnp.take_along_axis(logits, wanted[:, None], axis=1)[:, 0]
    return jnp.sum(counted * (log_total - picked + Z_WEIGHT * log_total * log_total))

def micro_loss(parameters, frozen, token_identifiers, targets, row_group_index, answer_length):
    embedding, gains, adapter_input_maps, adapter_up_maps, adapter_keyval_maps = parameters
    output_head_table, query_projection, keyval_projection, output_projection, gate_up_projection, down_projection = frozen
    tokens = GROUP * N_SEQ
    copies = QUERY_HEADS // HL
    half_group = GROUP // 2
    row_of, row_start, length, source = layout(row_group_index, N_SEQ)
    offsets = (jnp.arange(N_SEQ, dtype=jnp.int32) - row_start)[:, None] * GROUP + jnp.arange(GROUP, dtype=jnp.int32)[None, :]
    positions = offsets.reshape(tokens)
    limits = (length * GROUP - answer_length[row_of])[:, None]
    counted = (offsets >= limits).astype(jnp.float32).reshape(tokens)
    lowrank_result = lowrank_input(adapter_input_maps)
    residual_in = low_back(lowrank_input(embedding)[:, token_identifiers].T)
    normalized_input = lowrank_input(rms_norm(residual_in, gains[0]))
    adapter_result = lowrank_input(jnp.einsum('td,kdr->tkr', normalized_input, lowrank_result[:3], precision=PRECISE))
    query_linear = precise_product(normalized_input, query_projection.reshape(MODEL_WIDTH, QUERY_HEADS * HEAD_SIZE)) + ADAPTER_SCALE * precise_product(adapter_result[:, 0], lowrank_input(adapter_up_maps[0]))
    keyval_linear = jnp.einsum('td,dkc->tkc', normalized_input, keyval_projection.reshape(MODEL_WIDTH, 2, KEY_HEADS * HEAD_SIZE), precision=PRECISE)
    key_linear = keyval_linear[:, 0] + ADAPTER_SCALE * precise_product(adapter_result[:, 1], lowrank_input(adapter_keyval_maps[0]))
    value_linear = keyval_linear[:, 1] + ADAPTER_SCALE * precise_product(adapter_result[:, 2], lowrank_input(adapter_keyval_maps[1]))
    kv_of = jnp.arange(copies, dtype=jnp.int32) * HL // (QUERY_HEADS // KEY_HEADS)
    queries = lowrank_input(rotate(low_back(query_linear).reshape(tokens, QUERY_HEADS, HEAD_SIZE), positions))
    keys = lowrank_input(rotate(low_back(key_linear.reshape(tokens, KEY_HEADS, HEAD_SIZE)[:, kv_of]), positions))
    values = lowrank_input(low_back(value_linear.reshape(tokens, KEY_HEADS, HEAD_SIZE)[:, kv_of]))
    group_keys = keys.reshape(N_SEQ, GROUP, copies, HEAD_SIZE)
    group_values = values.reshape(N_SEQ, GROUP, copies, HEAD_SIZE)
    full_keys = jnp.concatenate([group_keys[source, half_group:], group_keys], axis=1)
    full_values = jnp.concatenate([group_values[source, half_group:], group_values], axis=1)
    attended = lax.map(attend_group, (queries.reshape(N_SEQ, GROUP, copies, HL, HEAD_SIZE), full_keys, full_values))
    combined_heads = lowrank_input(low_back(attended.reshape(tokens, QUERY_HEADS * HEAD_SIZE)))
    side_branch = precise_product(combined_heads, output_projection.reshape(MODEL_WIDTH, QUERY_HEADS * HEAD_SIZE).T) + ADAPTER_SCALE * precise_product(lowrank_input(precise_product(combined_heads, lowrank_result[3])), lowrank_input(adapter_up_maps[1]))
    residual_mid = residual_in + low_back(side_branch)
    normed_mid = lowrank_input(rms_norm(residual_mid, gains[1]))
    gate_pre = low_back(precise_product(normed_mid, gate_up_projection.reshape(MODEL_WIDTH, 2 * FF)))
    hidden = lowrank_input(jax.nn.silu(gate_pre[:, :FF]) * gate_pre[:, FF:])
    residual_out = residual_mid + low_back(precise_product(hidden, down_projection.T))
    normed_out = lowrank_input(rms_norm(residual_out, gains[2]))
    blocks = lax.map(jax.checkpoint(lambda packed: loss_block(packed, output_head_table)), (normed_out.reshape(N_SEQ, GROUP, MODEL_WIDTH), targets.reshape(N_SEQ, GROUP), counted.reshape(N_SEQ, GROUP)))
    return (jnp.sum(blocks), jnp.sum(counted))

def orthogonalize(moment):
    wide = moment.shape[0] <= moment.shape[1]
    current = moment if wide else moment.T
    current = current / (jnp.sqrt(jnp.sum(current * current)) + 1e-07)
    for iteration in range(5):
        gram = precise_product(current, current.T)
        current = SCHULZ[0] * current + precise_product(SCHULZ[1] * gram + SCHULZ[2] * precise_product(gram, gram), current)
    current = current if wide else current.T
    return current * (0.2 * math.sqrt(max(moment.shape)))

def momentum_orthogonal_step(weight, moment, grad):
    fresh = MUON_MOMENTUM * moment + grad
    steps = jnp.stack([orthogonalize(fresh[index]) for index in range(fresh.shape[0])])
    return (fresh, weight * (1.0 - MUON_RATE * DECAY_RATE) - MUON_RATE * steps)

def adamw_step(weight, first, second, grad):
    first = BETA_FIRST * first + (1.0 - BETA_FIRST) * grad
    second = BETA_SECOND * second + (1.0 - BETA_SECOND) * grad * grad
    fixed_first = first / (1.0 - BETA_FIRST ** STEP)
    fixed_second = second / (1.0 - BETA_SECOND ** STEP)
    return (first, second, weight - ADAM_RATE * (fixed_first / (jnp.sqrt(fixed_second) + ADAM_EPS) + DECAY_RATE * weight))

def reference(token_identifiers, targets, row_group_index, answer_length, embedding, embedding_first_moment, embedding_second_moment, output_head_table, query_projection, keyval_projection, output_projection, gate_up_projection, down_projection, gains, gain_first_moment, gain_second_moment, adapter_input_maps, input_map_momentum, adapter_up_maps, up_momentum, adapter_keyval_maps, keyval_momentum):
    frozen = tuple((item.astype(jnp.float32) for item in (output_head_table, query_projection, keyval_projection, output_projection, gate_up_projection, down_projection)))
    parameters = (embedding, gains, adapter_input_maps, adapter_up_maps, adapter_keyval_maps)
    grads = tuple((jnp.zeros_like(item) for item in parameters))
    loss_total_sum = jnp.zeros((), jnp.float32)
    loss_token_count = jnp.zeros((), jnp.float32)
    for batch in range(MB):

        def objective(values, batch=batch):
            return micro_loss(values, frozen, token_identifiers[batch], targets[batch], row_group_index[batch], answer_length[batch])
        total, pull, counted = jax.vjp(objective, parameters, has_aux=True)
        fresh = pull(jnp.ones_like(total))[0]
        grads = tuple((old + new for old, new in zip(grads, fresh)))
        loss_total_sum = loss_total_sum + total
        loss_token_count = loss_token_count + counted
    squares = sum((jnp.sum(item * item) for item in grads))
    gradient_norm = jnp.sqrt(squares)
    multiplier = jnp.minimum(1.0, CLIP_NORM / (gradient_norm + 1e-06))
    table_grad, gain_grad, input_map_grad, up_map_grad, keyval_map_grad = tuple((item * multiplier for item in grads))
    embedding_first_next, embedding_second_next, embedding_next = adamw_step(embedding, embedding_first_moment, embedding_second_moment, table_grad)
    gain_first_next, gain_second_next, gains_next = adamw_step(gains, gain_first_moment, gain_second_moment, gain_grad)
    input_map_momentum_next, adapter_input_next = momentum_orthogonal_step(adapter_input_maps, input_map_momentum, input_map_grad)
    up_momentum_next, adapter_up_next = momentum_orthogonal_step(adapter_up_maps, up_momentum, up_map_grad)
    keyval_momentum_next, adapter_keyval_next = momentum_orthogonal_step(adapter_keyval_maps, keyval_momentum, keyval_map_grad)
    return (loss_total_sum, loss_token_count, gradient_norm, embedding_first_next, embedding_second_next, embedding_next, gain_first_next, gain_second_next, gains_next, input_map_momentum_next, adapter_input_next, up_momentum_next, adapter_up_next, keyval_momentum_next, adapter_keyval_next)
```

```python
import functools
import math

import jax
import jax.numpy as jnp
from jax import lax
from jax.experimental import pallas as pl
from jax.experimental.pallas import tpu as pltpu
from jax.sharding import PartitionSpec as P

MODEL_WIDTH = 2048
QUERY_HEADS = 32
KEY_HEADS = 4
HEAD_SIZE = 64
ADAPTER_RANK = 8
MB = 2
STEP = 10


ADAPTER_SCALE = 2.0
NORM_EPS = 1e-05
Z_WEIGHT = 0.0001
CLIP_NORM = 1.0
ROPE_BASE = 10000.0
MASKED = -1e30
MUON_MOMENTUM = 0.95
MUON_RATE = 0.1
ADAM_RATE = 0.3
BETA_FIRST = 0.9
BETA_SECOND = 0.999
ADAM_EPS = 1e-08
DECAY_RATE = 0.01
SCHULZ = (3.4445, -4.775, 2.0315)
PRECISE = lax.Precision.HIGHEST
MESH = pl.DeviceIdType.MESH
VMEM_BYTES = 56 * 2**20


def flip(index, mask):
    result = index
    bit = 1
    while bit <= mask:
        if mask & bit:
            result = result + bit * (1 - 2 * lax.rem(lax.div(index, jnp.int32(bit)), jnp.int32(2)))
        bit *= 2
    return result


def token_share(kind, owner, team, rows, width, start, count):
    if kind == "stack":
        return (pl.ds(pl.multiple_of(owner * rows + start, 16), count), slice(None))
    column = pl.ds(pl.multiple_of(lax.rem(owner, jnp.int32(team)) * width, 128), width)
    if kind == "team":
        return (pl.ds(start, count), column)
    first = lax.div(owner, jnp.int32(team)) * rows + start
    return (pl.ds(pl.multiple_of(first, 16), count), column)


def row_of_sums(values):
    column = jnp.sum(values, axis=1, keepdims=True)
    return jnp.broadcast_to(column, (values.shape[0], 128)).T[:8]


def column_of(row):
    return row.T[:, :1]


def token_kernel(
    team, layer, rows, width, reduce, reduce_layer, middle, added, gather, gather_layer, chunks, *refs
):
    refs = list(refs)
    take = lambda: refs.pop(0)
    part_ref = take() if reduce else None
    payload_in = take() if gather and not middle else None
    added_ref = take() if added else None
    values_ref, scale_in = (take(), take()) if middle == "backward" else (None, None)
    gain_ref = take() if middle else None
    new_ref = take() if middle else None
    scale_ref = take() if middle == "forward" else None
    gain_grad_ref = take() if middle == "backward" else None
    low_ref = take() if not gather else None
    full_ref = take() if gather else None
    if reduce:
        near_in, far_out, far_in = take(), take(), take()
        near_sent, near_got, far_sent, far_got = take(), take(), take(), take()
    if middle:
        total_ref, sums_out, sums_in, sums_sent, sums_got = take(), take(), take(), take(), take()
    if gather:
        out_sent, out_got, on_sent, on_got = take(), take(), take(), take()

    seq_index = lax.axis_index("seq")
    me = lax.axis_index("vocab")
    reduce_masks = list(range(0, layer if reduce_layer else team, 2)) if reduce else []
    gather_masks = list(range(0, layer if gather_layer else team, 2)) if gather else []
    team_masks = list(range(1, team)) if middle else []
    peers = sorted(set(reduce_masks + gather_masks + team_masks + [1]) - {0})
    barrier = pltpu.get_barrier_semaphore()
    for mask in peers:
        pl.semaphore_signal(
            barrier, inc=1, device_id=(seq_index, flip(me, mask)), device_id_type=MESH
        )
    pl.semaphore_wait(barrier, len(peers))

    count = rows // chunks
    started = []

    def send(source, target, sent, got, mask):
        copy = pltpu.make_async_remote_copy(
            src_ref=source,
            dst_ref=target,
            send_sem=sent,
            recv_sem=got,
            device_id=(seq_index, flip(me, mask)),
            device_id_type=MESH,
        )
        copy.start()
        started.append(copy)
        return copy

    def share(kind, mask, chunk):
        return token_share(kind, flip(me, mask), team, rows, width, chunk * count, count)

    def within(chunk):
        return pl.ds(chunk * count, count)

    near, far, sums, out, on = {}, {}, {}, {}, {}
    for chunk in range(chunks):
        for place, mask in enumerate(reduce_masks):
            near[place, chunk] = send(
                part_ref.at[share(reduce, mask ^ 1, chunk)],
                near_in.at[place, within(chunk)],
                near_sent.at[place, chunk],
                near_got.at[place, chunk],
                1,
            )
    for chunk in range(chunks):
        for place, mask in enumerate(reduce_masks):
            near[place, chunk].wait_recv()
            if mask:
                both = part_ref[share(reduce, mask, chunk)].astype(jnp.float32) + near_in[
                    place, within(chunk)
                ].astype(jnp.float32)
                far_out[place - 1, within(chunk)] = both.astype(jnp.bfloat16)
                far[place, chunk] = send(
                    far_out.at[place - 1, within(chunk)],
                    far_in.at[place - 1, within(chunk)],
                    far_sent.at[place - 1, chunk],
                    far_got.at[place - 1, chunk],
                    mask,
                )

    def finish_sum(chunk):
        total = None
        if reduce:
            total = part_ref[share(reduce, 0, chunk)].astype(jnp.float32) + near_in[
                0, within(chunk)
            ].astype(jnp.float32)
            for place, mask in enumerate(reduce_masks):
                if mask:
                    far[place, chunk].wait_recv()
                    total = total + far_in[place - 1, within(chunk)].astype(jnp.float32)
        if middle == "forward":
            fresh = added_ref[within(chunk), :]
            if reduce:
                fresh = fresh + total
            new_ref[within(chunk), :] = fresh
            squares = fresh * fresh
        elif middle == "backward":
            total_ref[within(chunk), :] = total
            squares = values_ref[within(chunk), :] * total * gain_ref[...]
        if middle:
            sums_out[chunk] = row_of_sums(squares)
            for place, mask in enumerate(team_masks):
                sums[place, chunk] = send(
                    sums_out.at[chunk],
                    sums_in.at[place, chunk],
                    sums_sent.at[place, chunk],
                    sums_got.at[place, chunk],
                    mask,
                )
        elif reduce:
            low_ref[within(chunk), :] = total.astype(jnp.bfloat16)

    def finish_middle(chunk):
        if middle:
            whole = sums_out[chunk]
            for place, mask in enumerate(team_masks):
                sums[place, chunk].wait_recv()
                whole = whole + sums_in[place, chunk]
        if middle == "forward":
            scale = lax.rsqrt(whole / MODEL_WIDTH + NORM_EPS)
            scale_ref[:, within(chunk)] = scale
            payload = new_ref[within(chunk), :] * column_of(scale) * gain_ref[...]
        elif middle == "backward":
            total = total_ref[within(chunk), :]
            values = values_ref[within(chunk), :]
            scale_row = scale_in[:, within(chunk)]
            scale = column_of(scale_row)
            pull = column_of(scale_row * scale_row * scale_row * whole / MODEL_WIDTH)
            result = scale * (total * gain_ref[...]) - values * pull
            gain_part = jnp.sum(total * values * scale, axis=0, keepdims=True)
            gain_part = jnp.broadcast_to(gain_part, gain_grad_ref.shape)
            gain_grad_ref[...] = gain_part if chunk == 0 else gain_grad_ref[...] + gain_part
            if added:
                result = result + added_ref[within(chunk), :]
            new_ref[within(chunk), :] = result
            payload = result
        if gather:
            here = share(gather, 0, chunk)
            if middle:
                full_ref[here] = payload.astype(jnp.bfloat16)
            else:
                full_ref[here] = payload_in[within(chunk), :]
            for place, mask in enumerate(gather_masks):
                out[place, chunk] = send(
                    full_ref.at[here],
                    full_ref.at[here],
                    out_sent.at[place, chunk],
                    out_got.at[place, chunk],
                    mask if mask else 1,
                )
        elif middle:
            low_ref[within(chunk), :] = payload.astype(jnp.bfloat16)

    for chunk in range(chunks):
        finish_sum(chunk)
        if chunk:
            finish_middle(chunk - 1)
    finish_middle(chunks - 1)
    for chunk in range(chunks):
        for place, mask in enumerate(gather_masks):
            out[place, chunk].wait_recv()
            if mask:
                there = share(gather, mask, chunk)
                on[place, chunk] = send(
                    full_ref.at[there],
                    full_ref.at[there],
                    on_sent.at[place - 1, chunk],
                    on_got.at[place - 1, chunk],
                    1,
                )
    for copy in on.values():
        copy.wait_recv()
    for copy in started:
        copy.wait_send()


def move_tokens(
    name, collective, team, layer, rows, width, *, part=None, reduce=None, payload=None, middle=None,
    added=None, values=None, scale=None, gain=None, gather=None, chunks=2
):
    reduce_layer, gather_layer = reduce in ("layer", "stack"), gather in ("layer", "stack")
    vmem = pl.BlockSpec(memory_space=pltpu.VMEM)
    operands = [item for item in (part, payload, added, values, scale, gain) if item is not None]
    wide = jax.ShapeDtypeStruct((rows, width), jnp.float32)
    results = []
    if middle:
        results.append(wide)
    if middle == "forward":
        results.append(jax.ShapeDtypeStruct((8, rows), jnp.float32))
    if middle == "backward":
        results.append(jax.ShapeDtypeStruct((8, width), jnp.float32))
    if gather is None:
        results.append(jax.ShapeDtypeStruct((rows, width), jnp.bfloat16))
    elif gather == "stack":
        results.append(jax.ShapeDtypeStruct((layer * rows, width), jnp.bfloat16))
    else:
        tall = rows * (layer // team if gather == "layer" else 1)
        results.append(jax.ShapeDtypeStruct((tall, team * width), jnp.bfloat16))
    scratch = []
    if reduce:
        places = (layer if reduce_layer else team) // 2
        scratch += [
            pltpu.VMEM((places, rows, width), jnp.bfloat16),
            pltpu.VMEM((places - 1, rows, width), jnp.bfloat16),
            pltpu.VMEM((places - 1, rows, width), jnp.bfloat16),
        ]
        scratch += [pltpu.SemaphoreType.DMA((places, chunks))] * 2
        scratch += [pltpu.SemaphoreType.DMA((places - 1, chunks))] * 2
    if middle:
        scratch += [
            pltpu.VMEM((rows, width) if middle == "backward" else (8, 128), jnp.float32),
            pltpu.VMEM((chunks, 8, rows // chunks), jnp.float32),
            pltpu.VMEM((team - 1, chunks, 8, rows // chunks), jnp.float32),
        ]
        scratch += [pltpu.SemaphoreType.DMA((team - 1, chunks))] * 2
    if gather:
        places = (layer if gather_layer else team) // 2
        scratch += [pltpu.SemaphoreType.DMA((places, chunks))] * 2
        scratch += [pltpu.SemaphoreType.DMA((places - 1, chunks))] * 2
    return pl.pallas_call(
        functools.partial(
            token_kernel, team, layer, rows, width, reduce, reduce_layer, middle,
            added is not None, gather, gather_layer, chunks,
        ),
        name=name,
        out_shape=results,
        in_specs=[vmem] * len(operands),
        out_specs=[vmem] * len(results),
        scratch_shapes=scratch,
        cost_estimate=pl.CostEstimate(flops=0, bytes_accessed=150_000_000, transcendentals=0),
        compiler_params=pltpu.CompilerParams(
            collective_id=collective, has_side_effects=True, vmem_limit_bytes=VMEM_BYTES
        ),
    )(*operands)


def spread_kernel(layer, item_ref, all_ref, sent, got):
    seq_index = lax.axis_index("seq")
    me = lax.axis_index("vocab")
    barrier = pltpu.get_barrier_semaphore()
    for mask in range(1, layer):
        pl.semaphore_signal(
            barrier, inc=1, device_id=(seq_index, flip(me, mask)), device_id_type=MESH
        )
    pl.semaphore_wait(barrier, layer - 1)
    all_ref[me] = item_ref[...]
    copies = []
    for mask in range(1, layer):
        copy = pltpu.make_async_remote_copy(
            src_ref=item_ref,
            dst_ref=all_ref.at[me],
            send_sem=sent.at[mask - 1],
            recv_sem=got.at[mask - 1],
            device_id=(seq_index, flip(me, mask)),
            device_id_type=MESH,
        )
        copy.start()
        copies.append(copy)
    for copy in copies:
        copy.wait()


def spread(name, collective, layer, item):
    vmem = pl.BlockSpec(memory_space=pltpu.VMEM)
    return pl.pallas_call(
        functools.partial(spread_kernel, layer),
        name=name,
        out_shape=jax.ShapeDtypeStruct((layer, *item.shape), item.dtype),
        in_specs=[vmem],
        out_specs=vmem,
        scratch_shapes=[pltpu.SemaphoreType.DMA((layer - 1,))] * 2,
        cost_estimate=pl.CostEstimate(flops=0, bytes_accessed=20_000_000, transcendentals=0),
        compiler_params=pltpu.CompilerParams(collective_id=collective, has_side_effects=True),
    )(item)


def total_kernel(seq_count, layer, item_ref, total_ref, layer_in, between, seq_in, sent, got, up_sent, up_got):
    seq_index = lax.axis_index("seq")
    me = lax.axis_index("vocab")
    others = [
        (lax.rem(seq_index + step, jnp.int32(seq_count)), me) for step in range(1, seq_count)
    ]
    barrier = pltpu.get_barrier_semaphore()
    for mask in range(1, layer):
        pl.semaphore_signal(
            barrier, inc=1, device_id=(seq_index, flip(me, mask)), device_id_type=MESH
        )
    for other in others:
        pl.semaphore_signal(barrier, inc=1, device_id=other, device_id_type=MESH)
    pl.semaphore_wait(barrier, layer - 1 + len(others))
    layer_in[me] = item_ref[...]
    copies = []
    for mask in range(1, layer):
        copy = pltpu.make_async_remote_copy(
            src_ref=item_ref,
            dst_ref=layer_in.at[me],
            send_sem=sent.at[mask - 1],
            recv_sem=got.at[mask - 1],
            device_id=(seq_index, flip(me, mask)),
            device_id_type=MESH,
        )
        copy.start()
        copies.append(copy)
    for copy in copies:
        copy.wait_recv()
    whole = layer_in[0]
    for place in range(1, layer):
        whole = whole + layer_in[place]
    between[...] = whole
    seq_in[seq_index] = whole
    ups = []
    for step, other in enumerate(others):
        copy = pltpu.make_async_remote_copy(
            src_ref=between,
            dst_ref=seq_in.at[seq_index],
            send_sem=up_sent.at[step],
            recv_sem=up_got.at[step],
            device_id=other,
            device_id_type=MESH,
        )
        copy.start()
        ups.append(copy)
    for copy in ups:
        copy.wait_recv()
    whole = seq_in[0]
    for place in range(1, seq_count):
        whole = whole + seq_in[place]
    total_ref[...] = whole
    for copy in copies + ups:
        copy.wait_send()


def total_over_all(name, collective, seq_count, layer, item):
    vmem = pl.BlockSpec(memory_space=pltpu.VMEM)
    return pl.pallas_call(
        functools.partial(total_kernel, seq_count, layer),
        name=name,
        out_shape=jax.ShapeDtypeStruct(item.shape, item.dtype),
        in_specs=[vmem],
        out_specs=vmem,
        scratch_shapes=[
            pltpu.VMEM((layer, *item.shape), item.dtype),
            pltpu.VMEM(item.shape, item.dtype),
            pltpu.VMEM((seq_count, *item.shape), item.dtype),
        ]
        + [pltpu.SemaphoreType.DMA((layer - 1,))] * 2
        + [pltpu.SemaphoreType.DMA((seq_count - 1,))] * 2,
        cost_estimate=pl.CostEstimate(flops=0, bytes_accessed=20_000_000, transcendentals=0),
        compiler_params=pltpu.CompilerParams(collective_id=collective, has_side_effects=True),
    )(item)


def precise_product(left, right):
    return jnp.dot(left, right, precision=PRECISE)


def rotate(values, positions):
    half_width = values.shape[-1] // 2
    freqs = ROPE_BASE ** (-2.0 * jnp.arange(half_width, dtype=jnp.float32) / values.shape[-1])
    angles = positions.astype(jnp.float32)[:, None] * freqs[None, :]
    cosine = jnp.cos(angles)[:, None, :]
    sine = jnp.sin(angles)[:, None, :]
    first, second = (values[..., :half_width], values[..., half_width:])
    return jnp.concatenate(
        [first * cosine - second * sine, second * cosine + first * sine], axis=-1
    )


def rotate_back(grads, positions):
    half_width = grads.shape[-1] // 2
    freqs = ROPE_BASE ** (-2.0 * jnp.arange(half_width, dtype=jnp.float32) / grads.shape[-1])
    angles = positions.astype(jnp.float32)[:, None] * freqs[None, :]
    cosine = jnp.cos(angles)[:, None, :]
    sine = jnp.sin(angles)[:, None, :]
    first, second = (grads[..., :half_width], grads[..., half_width:])
    return jnp.concatenate(
        [first * cosine + second * sine, second * cosine - first * sine], axis=-1
    )


def layout(groups, count):
    ends = jnp.cumsum(groups)
    index = jnp.arange(count, dtype=jnp.int32)
    row_of = jnp.sum((ends[None, :] <= index[:, None]).astype(jnp.int32), axis=1)
    length = groups[row_of]
    row_start = ends[row_of] - length
    source = jnp.where(index > row_start, index - 1, row_start + length - 1)
    return (row_of, row_start, length, source)


def orthogonalize(moment):
    wide = moment.shape[0] <= moment.shape[1]
    current = moment if wide else moment.T
    current = current / (jnp.sqrt(jnp.sum(current * current)) + 1e-07)
    for iteration in range(5):
        gram = precise_product(current, current.T)
        current = SCHULZ[0] * current + precise_product(
            SCHULZ[1] * gram + SCHULZ[2] * precise_product(gram, gram), current
        )
    current = current if wide else current.T
    return current * (0.2 * math.sqrt(max(moment.shape)))


def momentum_orthogonal_step(weight, moment, grad):
    fresh = MUON_MOMENTUM * moment + grad
    steps = jnp.stack([orthogonalize(fresh[index]) for index in range(fresh.shape[0])])
    return (fresh, weight * (1.0 - MUON_RATE * DECAY_RATE) - MUON_RATE * steps)


def adamw_step(weight, first, second, grad):
    first = BETA_FIRST * first + (1.0 - BETA_FIRST) * grad
    second = BETA_SECOND * second + (1.0 - BETA_SECOND) * grad * grad
    fixed_first = first / (1.0 - BETA_FIRST**STEP)
    fixed_second = second / (1.0 - BETA_SECOND**STEP)
    return (
        first,
        second,
        weight
        - ADAM_RATE * (fixed_first / (jnp.sqrt(fixed_second) + ADAM_EPS) + DECAY_RATE * weight),
    )


def plain_mask(rows, width):
    return jnp.arange(width)[None, :] <= rows[:, None]


def shifted_mask(rows, width):
    half_group = width // 3
    slots = jnp.arange(width)[None, :] - half_group
    early = rows[:, None] < half_group
    return jnp.where(
        early, slots <= rows[:, None], (slots >= half_group) & (slots <= rows[:, None])
    )


def score_block(queries, keys, rows, mask_fn):
    scores = jnp.einsum(
        "ihd,kd->hik", queries, keys, preferred_element_type=jnp.float32
    ) * HEAD_SIZE ** (-0.5)
    return jnp.where(mask_fn(rows, keys.shape[0])[None], scores, MASKED)


def attend(queries, keys, values, mask_fn):
    group_rows = queries.shape[0]
    block_rows = min(512, group_rows)
    count_blocks = group_rows // block_rows

    def one_block(packed):
        query_block, first_row = packed
        scores = score_block(query_block, keys, first_row + jnp.arange(block_rows), mask_fn)
        peak = jnp.max(scores, axis=-1, keepdims=True)
        terms = jnp.exp(scores - peak)
        summed = jnp.sum(terms, axis=-1, keepdims=True)
        probs = (terms / summed).astype(jnp.bfloat16)
        result = jnp.einsum("hik,kd->ihd", probs, values, preferred_element_type=jnp.float32)
        return (result, (peak + jnp.log(summed))[..., 0])

    blocks = queries.reshape(count_blocks, block_rows, queries.shape[1], queries.shape[2])
    results, log_totals = lax.map(one_block, (blocks, jnp.arange(count_blocks) * block_rows))
    return (results.reshape(queries.shape), log_totals)


def attend_back(queries, keys, values, log_totals, grad_out, mask_fn):
    group_rows = queries.shape[0]
    block_rows = min(512, group_rows)
    count_blocks = group_rows // block_rows

    def one_block(packed):
        query_block, grad_block, log_block, first_row = packed
        scores = score_block(query_block, keys, first_row + jnp.arange(block_rows), mask_fn)
        probs = jnp.exp(scores - log_block[..., None])
        grad_probs = jnp.einsum(
            "ihd,kd->hik", grad_block, values, preferred_element_type=jnp.float32
        )
        inner = jnp.sum(probs * grad_probs, axis=-1, keepdims=True)
        grad_scores = (probs * (grad_probs - inner)).astype(jnp.bfloat16)
        grad_query = jnp.einsum(
            "hik,kd->ihd", grad_scores, keys, preferred_element_type=jnp.float32
        ) * HEAD_SIZE ** (-0.5)
        grad_key = jnp.einsum(
            "hik,ihd->kd", grad_scores, query_block, preferred_element_type=jnp.float32
        ) * HEAD_SIZE ** (-0.5)
        grad_value = jnp.einsum(
            "hik,ihd->kd",
            probs.astype(jnp.bfloat16),
            grad_block,
            preferred_element_type=jnp.float32,
        )
        return (grad_query, grad_key, grad_value)

    shape_block = (count_blocks, block_rows, queries.shape[1], queries.shape[2])
    grad_queries, grad_keys, grad_values = lax.map(
        one_block,
        (
            queries.reshape(shape_block),
            grad_out.reshape(shape_block),
            log_totals,
            jnp.arange(count_blocks) * block_rows,
        ),
    )
    return (
        grad_queries.reshape(queries.shape),
        jnp.sum(grad_keys, axis=0),
        jnp.sum(grad_values, axis=0),
    )


def from_behind(value, axis, by):
    length = lax.axis_size(axis)
    pairs = [(i, i + by) for i in range(length) if 0 <= i + by < length]
    return lax.ppermute(value, axis, pairs)


def pass_halo(tail, source, seq_index):
    below = from_behind(tail, "seq", 1)
    above_one = from_behind(tail, "seq", -1)
    above_two = from_behind(tail, "seq", -2)
    return jnp.where(
        source == seq_index - 1,
        below,
        jnp.where(
            source == seq_index + 1, above_one, jnp.where(source == seq_index + 2, above_two, tail)
        ),
    )


def return_halo(grads, source, seq_index):
    kept = jnp.where(source == seq_index, grads, 0.0)
    lower = from_behind(jnp.where(source == seq_index - 1, grads, 0.0), "seq", -1)
    raised = from_behind(jnp.where(source == seq_index + 1, grads, 0.0), "seq", 1)
    further = from_behind(jnp.where(source == seq_index + 2, grads, 0.0), "seq", 2)
    return kept + lower + raised + further


def other_half(value):
    layer = lax.axis_size("vocab")
    return lax.ppermute(value, "vocab", [(i, (i + layer // MB) % layer) for i in range(layer)])


def owners_swap(value):
    seq_count, layer = lax.axis_size("seq"), lax.axis_size("vocab")
    team = layer // MB
    pairs = []
    for seq_at in range(seq_count):
        for batch in range(MB):
            for place in range(team):
                pairs.append(
                    (
                        seq_at * layer + batch * team + place,
                        place * layer + batch * team + seq_at,
                    )
                )
    return lax.ppermute(value, ("seq", "vocab"), pairs)


def on_device(
    token_identifiers,
    targets,
    row_group_index,
    answer_length,
    embedding,
    embedding_first_moment,
    embedding_second_moment,
    output_head_table,
    query_projection,
    keyval_projection,
    output_projection,
    gate_up_projection,
    down_projection,
    gains,
    gain_first_moment,
    gain_second_moment,
    adapter_input_maps,
    input_map_momentum,
    adapter_up_maps,
    up_momentum,
    adapter_keyval_maps,
    keyval_momentum,
):
    seq_count = lax.axis_size("seq")
    layer = lax.axis_size("vocab")
    team = layer // MB
    seq_index = lax.axis_index("seq")
    vocabulary_index = lax.axis_index("vocab")
    batch = vocabulary_index // team
    place = vocabulary_index % team
    other_index = (vocabulary_index + team) % layer
    group_rows = token_identifiers.shape[1]
    half_group = group_rows // 2
    width = MODEL_WIDTH // team
    table_width = output_head_table.shape[1]
    head_width = query_projection.shape[2]
    heads = head_width // HEAD_SIZE
    hidden = gate_up_projection.shape[2]
    plain_keys = KEY_HEADS // 2

    def move(name, collective, **options):
        return move_tokens(name, collective, team, layer, group_rows, width, **options)

    def gathered(piece):
        return lax.all_gather(piece, "seq", axis=0, tiled=True)

    tokens_all = lax.all_gather(token_identifiers, "seq")
    keyval_rows = keyval_projection.shape[0] // layer
    keyval_piece = gathered(
        lax.dynamic_slice_in_dim(keyval_projection, vocabulary_index * keyval_rows, keyval_rows, 0)
    )
    query_own = gathered(query_projection.reshape(-1, 2 * head_width))
    out_own = gathered(output_projection.reshape(-1, 2 * head_width))
    gate_own = gathered(gate_up_projection.reshape(-1, 2 * hidden))
    down_own = gathered(down_projection)
    head_parts = 2
    part_width = table_width // head_parts
    head_pieces = [
        gathered(output_head_table[:, part * part_width : (part + 1) * part_width])
        for part in range(head_parts)
    ]
    query_weights = (query_own, other_half(query_own))
    out_weights = (out_own, other_half(out_own))
    gate_weights = (gate_own, other_half(gate_own))
    down_weights = (down_own, other_half(down_own))

    tokens_flat = jnp.swapaxes(tokens_all, 0, 1).reshape(-1)
    local_ids = tokens_flat - vocabulary_index * table_width
    token_rows = (jnp.arange(table_width)[None, :] == local_ids[:, None]).astype(jnp.bfloat16)
    looked = jnp.einsum(
        "tv,dv->td",
        token_rows,
        embedding.astype(jnp.bfloat16),
        preferred_element_type=jnp.float32,
    ).astype(jnp.bfloat16)
    (looked,) = move("sum_lookup", 1, part=looked, reduce="stack")
    residual_in = owners_swap(looked).astype(jnp.float32)
    gain_local = lax.dynamic_slice_in_dim(gains, place * width, width, 1)
    residual_in, scale_in, normed_full = move(
        "norm_in", 2, added=residual_in, gain=gain_local[0:1], middle="forward", gather="team"
    )

    keyval_full = spread("gather_keyval", 3, layer, keyval_piece)
    keyval_full = jnp.swapaxes(
        keyval_full.reshape(layer, seq_count, keyval_rows, 2 * KEY_HEADS * HEAD_SIZE), 0, 1
    ).reshape(MODEL_WIDTH, 2, KEY_HEADS, HEAD_SIZE)

    def chosen(values, axis):
        heads_of = lambda first: jnp.concatenate(
            [
                lax.slice_in_dim(values, index, index + 1, axis=axis)
                for index in (first, plain_keys + first, 1 - first, plain_keys + 1 - first)
            ],
            axis=axis,
        )
        return jnp.where(batch == 0, heads_of(0), heads_of(1))

    keyval_weight = chosen(keyval_full, 2).reshape(MODEL_WIDTH, 8 * HEAD_SIZE)
    input_map_lowrank = adapter_input_maps.astype(jnp.bfloat16)
    down_qkv = jnp.swapaxes(input_map_lowrank[:3], 0, 1).reshape(MODEL_WIDTH, 3 * ADAPTER_RANK)

    def of_slices(values, axis):
        return jnp.stack(
            [
                lax.dynamic_slice_in_dim(values, index * head_width, head_width, axis)
                for index in (vocabulary_index, other_index)
            ],
            axis=axis - 1,
        )

    down_out = of_slices(
        input_map_lowrank[3].reshape(2, QUERY_HEADS // 2 * HEAD_SIZE, ADAPTER_RANK), 1
    ).reshape(4 * head_width, ADAPTER_RANK)
    up_query_map = (
        of_slices(adapter_up_maps[0].reshape(ADAPTER_RANK, 2, QUERY_HEADS // 2 * HEAD_SIZE), 2)
        .reshape(ADAPTER_RANK, 4 * head_width)
        .astype(jnp.bfloat16)
    )
    up_output_map = adapter_up_maps[1].astype(jnp.bfloat16)
    keyval_up = (
        chosen(adapter_keyval_maps.reshape(2, ADAPTER_RANK, KEY_HEADS, HEAD_SIZE), 2)
        .astype(jnp.bfloat16)
        .reshape(2, ADAPTER_RANK, 4 * HEAD_SIZE)
    )

    row_of, row_start, length, source_all = layout(row_group_index[batch], seq_count)
    positions = (seq_index - row_start[seq_index]) * group_rows + jnp.arange(group_rows)
    source = source_all[seq_index]
    adapter_result = jnp.dot(
        normed_full, down_qkv, preferred_element_type=jnp.float32
    ).astype(jnp.bfloat16)
    adapter_parts = [
        adapter_result[:, ADAPTER_RANK * which : ADAPTER_RANK * (which + 1)] for which in range(3)
    ]
    query_linear = jnp.concatenate(
        [
            jnp.dot(normed_full, weight, preferred_element_type=jnp.float32)
            for weight in query_weights
        ],
        axis=1,
    ) + ADAPTER_SCALE * jnp.dot(
        adapter_parts[0], up_query_map, preferred_element_type=jnp.float32
    )
    keyval_linear = jnp.dot(normed_full, keyval_weight, preferred_element_type=jnp.float32)
    key_linear = keyval_linear[:, : 4 * HEAD_SIZE] + ADAPTER_SCALE * jnp.dot(
        adapter_parts[1], keyval_up[0], preferred_element_type=jnp.float32
    )
    value_linear = keyval_linear[:, 4 * HEAD_SIZE :] + ADAPTER_SCALE * jnp.dot(
        adapter_parts[2], keyval_up[1], preferred_element_type=jnp.float32
    )
    queries = (
        rotate(query_linear.reshape(group_rows, 4 * heads, HEAD_SIZE), positions)
        .astype(jnp.bfloat16)
        .reshape(group_rows, 2, 2, heads, HEAD_SIZE)
    )
    keys = (
        rotate(key_linear.reshape(group_rows, 4, HEAD_SIZE), positions)
        .astype(jnp.bfloat16)
        .reshape(group_rows, 2, 2, HEAD_SIZE)
    )
    values = value_linear.reshape(group_rows, 2, 2, HEAD_SIZE).astype(jnp.bfloat16)
    borrowed = pass_halo(
        jnp.stack([keys[half_group:, :, 1], values[half_group:, :, 1]]), source, seq_index
    )
    keys_shifted = jnp.concatenate([borrowed[0], keys[:, :, 1]], axis=0)
    values_shifted = jnp.concatenate([borrowed[1], values[:, :, 1]], axis=0)
    attended, kept = [], []
    for part in range(2):
        plain = (queries[:, part, 0], keys[:, part, 0], values[:, part, 0])
        shifted = (queries[:, part, 1], keys_shifted[:, part], values_shifted[:, part])
        plain_out, plain_log = attend(*plain, plain_mask)
        shifted_out, shifted_log = attend(*shifted, shifted_mask)
        attended += [plain_out, shifted_out]
        kept.append((plain, plain_log, shifted, shifted_log))
    combined_heads = (
        jnp.stack(attended, axis=1).reshape(group_rows, 4 * head_width).astype(jnp.bfloat16)
    )
    combined_parts = (combined_heads[:, : 2 * head_width], combined_heads[:, 2 * head_width :])
    adapter_out_part = jnp.dot(
        combined_heads, down_out, preferred_element_type=jnp.float32
    ).astype(jnp.bfloat16)
    branch_part = ADAPTER_SCALE * jnp.dot(
        adapter_out_part, up_output_map, preferred_element_type=jnp.float32
    )
    for piece, weight in zip(combined_parts, out_weights):
        branch_part = branch_part + jnp.einsum(
            "tc,dc->td", piece, weight, preferred_element_type=jnp.float32
        )
    residual_mid, scale_mid, mid_full = move(
        "sum_attended",
        4,
        part=branch_part.astype(jnp.bfloat16),
        reduce="team",
        added=residual_in,
        gain=gain_local[1:2],
        middle="forward",
        gather="team",
    )

    gate_parts, up_parts, ffn_part = [], [], 0.0
    for gate_weight, down_weight in zip(gate_weights, down_weights):
        gate_pre = jnp.dot(mid_full, gate_weight, preferred_element_type=jnp.float32)
        gate_part, up_part = (gate_pre[:, :hidden], gate_pre[:, hidden:])
        mixed = (gate_part * jax.nn.sigmoid(gate_part) * up_part).astype(jnp.bfloat16)
        gate_parts.append(gate_part)
        up_parts.append(up_part)
        ffn_part = ffn_part + jnp.einsum(
            "tf,df->td", mixed, down_weight, preferred_element_type=jnp.float32
        )
    residual_out, scale_out, out_full_rows = move(
        "sum_hidden",
        5,
        part=ffn_part.astype(jnp.bfloat16),
        reduce="team",
        added=residual_mid,
        gain=gain_local[2:3],
        middle="forward",
        gather="layer",
    )

    counted = []
    for each in range(MB):
        row_each, start_each, length_each, _ = layout(row_group_index[each], seq_count)
        places = (seq_index - start_each[seq_index]) * group_rows + jnp.arange(group_rows)
        limit = length_each[seq_index] * group_rows - answer_length[each, row_each[seq_index]]
        counted.append((places >= limit).astype(jnp.float32))
    counted = jnp.concatenate(counted)
    local_targets = targets.reshape(-1) - vocabulary_index * table_width
    logit_parts, matched_parts, stats = [], [], []
    for part in range(head_parts):
        logits = jnp.dot(out_full_rows, head_pieces[part], preferred_element_type=jnp.float32)
        matched = (
            jnp.arange(part * part_width, (part + 1) * part_width)[None, :]
            == local_targets[:, None]
        )
        peak = jnp.max(logits, axis=1)
        exp_total = jnp.sum(jnp.exp(logits - peak[:, None]), axis=1)
        picked = jnp.sum(jnp.where(matched, logits, 0.0), axis=1)
        logit_parts.append(logits)
        matched_parts.append(matched)
        stats += [peak, exp_total, picked]
    stats += [jnp.zeros_like(stats[0])] * (8 - len(stats))
    stats = spread("gather_stats", 6, layer, jnp.stack(stats))
    peaks = jnp.concatenate([stats[:, 3 * part] for part in range(head_parts)])
    sums = jnp.concatenate([stats[:, 3 * part + 1] for part in range(head_parts)])
    picked = sum(jnp.sum(stats[:, 3 * part + 2], axis=0) for part in range(head_parts))
    peak = jnp.max(peaks, axis=0)
    log_total = peak + jnp.log(jnp.sum(sums * jnp.exp(peaks - peak[None, :]), axis=0))
    loss_total_sum = jnp.sum(
        counted * (log_total - picked + Z_WEIGHT * log_total * log_total)
    )
    token_count = jnp.sum(counted)
    head_grad = 0.0
    for part in range(head_parts):
        grad_logits = counted[:, None] * (
            jnp.exp(logit_parts[part] - log_total[:, None])
            * (1.0 + 2.0 * Z_WEIGHT * log_total)[:, None]
            - matched_parts[part].astype(jnp.float32)
        )
        head_grad = head_grad + jnp.einsum(
            "tv,dv->td",
            grad_logits.astype(jnp.bfloat16),
            head_pieces[part],
            preferred_element_type=jnp.float32,
        )
    grad_out_res, gain_grad_out, grad_ffn = move(
        "sum_head_grad",
        7,
        part=head_grad.astype(jnp.bfloat16),
        reduce="layer",
        values=residual_out,
        scale=scale_out,
        gain=gain_local[2:3],
        middle="backward",
        gather="team",
    )

    ffn_part = 0.0
    for part in range(2):
        grad_hidden = jnp.dot(
            grad_ffn, down_weights[part], preferred_element_type=jnp.float32
        )
        gate_part, up_part = gate_parts[part], up_parts[part]
        sigmoid_gate = jax.nn.sigmoid(gate_part)
        grad_gate = grad_hidden * up_part * sigmoid_gate * (1.0 + gate_part * (1.0 - sigmoid_gate))
        grad_up = grad_hidden * gate_part * sigmoid_gate
        grad_gate_up = jnp.concatenate([grad_gate, grad_up], axis=1).astype(jnp.bfloat16)
        ffn_part = ffn_part + jnp.einsum(
            "tc,dc->td", grad_gate_up, gate_weights[part], preferred_element_type=jnp.float32
        )
    grad_mid, gain_grad_mid, branch_grad = move(
        "sum_hidden_grad",
        8,
        part=ffn_part.astype(jnp.bfloat16),
        reduce="team",
        values=residual_mid,
        scale=scale_mid,
        gain=gain_local[1:2],
        added=grad_out_res,
        middle="backward",
        gather="team",
    )

    adapter_out_grad = ADAPTER_SCALE * jnp.einsum(
        "td,rd->tr", branch_grad, up_output_map, preferred_element_type=jnp.float32
    )
    up_out_grad = ADAPTER_SCALE * jnp.einsum(
        "tr,td->rd", adapter_out_part, branch_grad, preferred_element_type=jnp.float32
    )
    grad_mixed = jnp.concatenate(
        [
            jnp.dot(branch_grad, weight, preferred_element_type=jnp.float32)
            for weight in out_weights
        ],
        axis=1,
    ) + precise_product(adapter_out_grad, down_out.astype(jnp.float32).T)
    down_out_grad = precise_product(combined_heads.astype(jnp.float32).T, adapter_out_grad)
    grad_heads = grad_mixed.reshape(group_rows, 2, 2, heads, HEAD_SIZE).astype(jnp.bfloat16)
    query_grads, key_grads, value_grads, returning = [], [], [], []
    for part in range(2):
        plain, plain_log, shifted, shifted_log = kept[part]
        grad_q, grad_k, grad_v = attend_back(
            *plain, plain_log, grad_heads[:, part, 0], plain_mask
        )
        shift_q, shift_k, shift_v = attend_back(
            *shifted, shifted_log, grad_heads[:, part, 1], shifted_mask
        )
        query_grads += [grad_q, shift_q]
        key_grads += [grad_k, shift_k[half_group:]]
        value_grads += [grad_v, shift_v[half_group:]]
        returning.append(jnp.stack([shift_k[:half_group], shift_v[:half_group]]))
    returned = return_halo(jnp.stack(returning), source, seq_index)
    padding = jnp.zeros((half_group, HEAD_SIZE), jnp.float32)
    for part in range(2):
        for which, grads in ((0, key_grads), (1, value_grads)):
            grads[2 * part + 1] = grads[2 * part + 1] + jnp.concatenate(
                [padding, returned[part, which]], axis=0
            )
    grad_query = (
        rotate_back(
            jnp.stack(query_grads, axis=1).reshape(group_rows, 4 * heads, HEAD_SIZE), positions
        )
        .astype(jnp.bfloat16)
        .reshape(group_rows, 4 * head_width)
    )
    grad_key = (
        rotate_back(jnp.stack(key_grads, axis=1), positions)
        .astype(jnp.bfloat16)
        .reshape(group_rows, 4 * HEAD_SIZE)
    )
    grad_value = (
        jnp.stack(value_grads, axis=1).astype(jnp.bfloat16).reshape(group_rows, 4 * HEAD_SIZE)
    )
    pulls = ((grad_query, up_query_map), (grad_key, keyval_up[0]), (grad_value, keyval_up[1]))
    adapter_grad = ADAPTER_SCALE * jnp.concatenate(
        [
            jnp.einsum("tc,rc->tr", grad, up_map, preferred_element_type=jnp.float32)
            for grad, up_map in pulls
        ],
        axis=1,
    )
    up_grads = [
        ADAPTER_SCALE
        * jnp.einsum("tr,tc->rc", low, grad, preferred_element_type=jnp.float32)
        for low, (grad, _) in zip(adapter_parts, pulls)
    ]
    in_part = (
        jnp.einsum(
            "tc,dc->td",
            grad_query[:, : 2 * head_width],
            query_weights[0],
            preferred_element_type=jnp.float32,
        )
        + jnp.einsum(
            "tc,dc->td",
            grad_query[:, 2 * head_width :],
            query_weights[1],
            preferred_element_type=jnp.float32,
        )
        + jnp.einsum(
            "tc,dc->td",
            jnp.concatenate([grad_key, grad_value], axis=1),
            keyval_weight,
            preferred_element_type=jnp.float32,
        )
        + jnp.einsum(
            "tr,dr->td", adapter_grad, down_qkv.astype(jnp.float32), precision=PRECISE
        )
    )
    down_qkv_grad = jnp.einsum(
        "td,tr->rd", normed_full.astype(jnp.float32), adapter_grad, precision=PRECISE
    )
    _, gain_grad_in, grad_in = move(
        "sum_in_grad",
        9,
        part=in_part.astype(jnp.bfloat16),
        reduce="team",
        values=residual_in,
        scale=scale_in,
        gain=gain_local[0:1],
        added=grad_mid,
        middle="backward",
    )

    (grad_rows,) = move("gather_rows", 10, payload=owners_swap(grad_in), gather="stack")
    table_grad = jnp.einsum("td,tv->dv", grad_rows, token_rows, preferred_element_type=jnp.float32)

    def placed(pieces, shape, axis):
        whole = jnp.zeros(shape, jnp.float32)
        for piece, index in zip(pieces, (vocabulary_index, other_index)):
            start = [0] * len(shape)
            start[axis] = index * head_width
            whole = lax.dynamic_update_slice(whole, piece, start)
        return whole

    out_pieces = down_out_grad.T.reshape(ADAPTER_RANK, 2, 2, head_width)
    down_out_full = placed(
        [out_pieces[:, 0], out_pieces[:, 1]],
        (ADAPTER_RANK, 2, QUERY_HEADS // 2 * HEAD_SIZE),
        2,
    ).reshape(ADAPTER_RANK, MODEL_WIDTH)
    query_pieces = up_grads[0].reshape(ADAPTER_RANK, 2, 2, head_width)
    up_query_full = placed(
        [query_pieces[:, 0], query_pieces[:, 1]],
        (ADAPTER_RANK, 2, QUERY_HEADS // 2 * HEAD_SIZE),
        2,
    ).reshape(ADAPTER_RANK, MODEL_WIDTH)

    def key_heads_back(grads):
        first, first_shifted, second, second_shifted = jnp.split(grads, 4, axis=1)
        kept_order = jnp.concatenate([first, second, first_shifted, second_shifted], axis=1)
        swapped = jnp.concatenate([second, first, second_shifted, first_shifted], axis=1)
        return jnp.where(batch == 0, kept_order, swapped)

    gain_grad = lax.dynamic_update_slice(
        jnp.zeros((3, MODEL_WIDTH), jnp.float32),
        jnp.concatenate([gain_grad_in[:1], gain_grad_mid[:1], gain_grad_out[:1]]),
        (0, place * width),
    )
    owner = (vocabulary_index == 0).astype(jnp.float32)
    loss_row = jnp.zeros((1, MODEL_WIDTH), jnp.float32)
    loss_row = loss_row.at[0, 0].set(loss_total_sum * owner).at[0, 1].set(token_count * owner)
    keyval_grads = jnp.concatenate([key_heads_back(up_grads[1]), key_heads_back(up_grads[2])])
    small = jnp.concatenate(
        [
            down_qkv_grad,
            down_out_full,
            up_query_full,
            up_out_grad,
            keyval_grads.reshape(-1, MODEL_WIDTH),
            gain_grad,
            loss_row,
        ]
    )
    small = lax.psum(small, ("seq", "vocab"))
    rank = ADAPTER_RANK
    keyval_rows_small = 2 * rank * KEY_HEADS * HEAD_SIZE // MODEL_WIDTH
    input_map_gradient = jnp.swapaxes(small[: 4 * rank].reshape(4, rank, MODEL_WIDTH), 1, 2)
    up_gradient = small[4 * rank : 6 * rank].reshape(2, rank, MODEL_WIDTH)
    at = 6 * rank + keyval_rows_small
    keyval_gradient = small[6 * rank : at].reshape(2, rank, KEY_HEADS * HEAD_SIZE)
    gain_grad = small[at : at + 3]
    loss_pair = small[at + 3, :2]
    table_squares = total_over_all(
        "sum_squares",
        11,
        seq_count,
        layer,
        jnp.full((8, 128), jnp.sum(table_grad * table_grad), jnp.float32),
    )[0, 0]
    squares = table_squares + jnp.sum(small[: at + 3] * small[: at + 3])
    gradient_norm = jnp.sqrt(squares)
    multiplier = jnp.minimum(1.0, CLIP_NORM / (gradient_norm + 1e-06))
    embedding_first_next, embedding_second_next, embedding_next = adamw_step(
        embedding, embedding_first_moment, embedding_second_moment, table_grad * multiplier
    )
    gain_first_next, gain_second_next, gains_next = adamw_step(
        gains, gain_first_moment, gain_second_moment, gain_grad * multiplier
    )
    input_map_momentum_next, adapter_input_next = momentum_orthogonal_step(
        adapter_input_maps, input_map_momentum, input_map_gradient * multiplier
    )
    up_momentum_next, adapter_up_next = momentum_orthogonal_step(
        adapter_up_maps, up_momentum, up_gradient * multiplier
    )
    keyval_momentum_next, adapter_keyval_next = momentum_orthogonal_step(
        adapter_keyval_maps, keyval_momentum, keyval_gradient * multiplier
    )
    return (
        loss_pair[0],
        loss_pair[1],
        gradient_norm,
        embedding_first_next,
        embedding_second_next,
        embedding_next,
        gain_first_next,
        gain_second_next,
        gains_next,
        input_map_momentum_next,
        adapter_input_next,
        up_momentum_next,
        adapter_up_next,
        keyval_momentum_next,
        adapter_keyval_next,
    )


def solution(mesh):
    placed = (
        P(None, "seq"),
        P(None, "seq"),
        P(),
        P(),
        P("seq", "vocab"),
        P("seq", "vocab"),
        P("seq", "vocab"),
        P("seq", "vocab"),
        P("seq", None, "vocab"),
        P("seq", None),
        P("seq", None, "vocab"),
        P("seq", None, "vocab"),
        P("seq", "vocab"),
        P(),
        P(),
        P(),
        P(),
        P(),
        P(),
        P(),
        P(),
        P(),
    )
    return jax.shard_map(
        on_device,
        mesh=mesh,
        in_specs=placed,
        out_specs=(
            P(),
            P(),
            P(),
            P("seq", "vocab"),
            P("seq", "vocab"),
            P("seq", "vocab"),
            P(),
            P(),
            P(),
            P(),
            P(),
            P(),
            P(),
            P(),
            P(),
        ),
        check_vma=False,
    )
```

```python
import functools
import math

import jax
import jax.numpy as jnp
from jax import lax
from jax.experimental import pallas as pl
from jax.experimental.pallas import tpu as pltpu
from jax.sharding import PartitionSpec as P

MODEL_WIDTH = 2048
QUERY_HEADS = 32
KEY_HEADS = 4
HEAD_SIZE = 64
ADAPTER_RANK = 8
MB = 2
STEP = 10


ADAPTER_SCALE = 2.0
NORM_EPS = 1e-05
Z_WEIGHT = 0.0001
CLIP_NORM = 1.0
ROPE_BASE = 10000.0
MASKED = -1e30
MUON_MOMENTUM = 0.95
MUON_RATE = 0.1
ADAM_RATE = 0.3
BETA_FIRST = 0.9
BETA_SECOND = 0.999
ADAM_EPS = 1e-08
DECAY_RATE = 0.01
SCHULZ = (3.4445, -4.775, 2.0315)
PRECISE = lax.Precision.HIGHEST
MESH = pl.DeviceIdType.MESH


def flip(index, mask):
    result = index
    bit = 1
    while bit <= mask:
        if mask & bit:
            result = result + bit * (1 - 2 * lax.rem(lax.div(index, jnp.int32(bit)), jnp.int32(2)))
        bit *= 2
    return result


def against(left, right):
    return lax.dot_general(
        left, right, (((1,), (1,)), ((), ())), preferred_element_type=jnp.float32
    )


class Links:
    def __init__(self, sent, got):
        self.sent, self.got, self.started = sent, got, []
        self.seq_index = lax.axis_index("seq")
        self.me = lax.axis_index("vocab")

    def layer_peer(self, mask):
        return (self.seq_index, flip(self.me, mask))

    def column_peer(self, step):
        count = jnp.int32(lax.axis_size("seq"))
        return (lax.rem(self.seq_index + step, count), self.me)

    def meet(self, peers):
        barrier = pltpu.get_barrier_semaphore()
        for peer in peers:
            pl.semaphore_signal(barrier, inc=1, device_id=peer, device_id_type=MESH)
        pl.semaphore_wait(barrier, len(peers))

    def send(self, source, target, peer):
        at = len(self.started)
        copy = pltpu.make_async_remote_copy(
            src_ref=source,
            dst_ref=target,
            send_sem=self.sent.at[at],
            recv_sem=self.got.at[at],
            device_id=peer,
            device_id_type=MESH,
        )
        copy.start()
        self.started.append(copy)
        return copy

    def along(self, source, target, steps):
        count = jnp.int32(lax.axis_size("seq"))
        waits = []
        for at, step in enumerate(steps):
            place = len(self.started)
            copy = pltpu.make_async_remote_copy(
                src_ref=source,
                dst_ref=target.at[at],
                send_sem=self.sent.at[place],
                recv_sem=self.got.at[place],
                device_id=self.column_peer(step % lax.axis_size("seq")),
                device_id_type=MESH,
            )
            there = self.seq_index + step
            giver = self.seq_index - step
            to_send = (there >= 0) & (there < count)
            to_take = (giver >= 0) & (giver < count)
            pl.when(to_send)(copy.start)
            self.started.append((to_send, copy))
            waits.append(functools.partial(pl.when(to_take), copy.wait_recv))
        return waits

    def finish(self):
        for copy in self.started:
            if isinstance(copy, tuple):
                pl.when(copy[0])(copy[1].wait_send)
            else:
                copy.wait_send()


def group_masks(size):
    if size == 8:
        return [2, 4], True
    return list(range(2, size, 2)), False


def sum_blocks(links, size, produce, near_in, far_out, far_in, side_in, mine):
    masks, routed = group_masks(size)
    half = mine.shape[0] // 2
    sides, fars = [], []
    for step, mask in enumerate(([6] if routed else []) + masks + [0]):
        source = produce(step, mask)
        near = links.send(source, near_in.at[step], links.layer_peer(1))
        near.wait_recv()
        if routed and mask == 6:
            far_out[step] = (mine[...] + near_in[step].astype(jnp.float32)).astype(jnp.bfloat16)
            for at, over in enumerate(masks):
                sides.append(
                    links.send(
                        far_out.at[step, pl.ds(at * half, half)],
                        side_in.at[at],
                        links.layer_peer(over),
                    )
                )
        elif mask:
            both = mine[...] + near_in[step].astype(jnp.float32)
            if routed:
                mine[...] = both
                at = 1 if mask == 2 else 0
                sides[at].wait_recv()
                rows = pl.ds(at * half, half)
                mine[rows, :] = mine[rows, :] + side_in[at].astype(jnp.float32)
                both = mine[...]
            far_out[step] = both.astype(jnp.bfloat16)
            fars.append(
                links.send(far_out.at[step], far_in.at[len(fars)], links.layer_peer(mask))
            )
        else:
            mine[...] = mine[...] + near_in[step].astype(jnp.float32)
    for at, copy in enumerate(fars):
        copy.wait_recv()
        mine[...] = mine[...] + far_in[at].astype(jnp.float32)


def gather_blocks(links, size, block, write, parts=2):
    masks, routed = group_masks(size)
    out, on, over = {}, {}, {}
    for part in range(parts):
        write(part)
        for mask in [1] + masks:
            out[mask, part] = links.send(
                block(0, part), block(0, part), links.layer_peer(mask)
            )
    for part in range(parts):
        for at, mask in enumerate(masks):
            out[mask, part].wait_recv()
            if routed and part == at:
                over[part] = links.send(
                    block(mask, part), block(mask, part), links.layer_peer(masks[1 - at])
                )
            on[mask, part] = links.send(
                block(mask, part), block(mask, part), links.layer_peer(1)
            )
    for part, copy in over.items():
        copy.wait_recv()
        on[6, part] = links.send(block(6, part), block(6, part), links.layer_peer(1))
    for part in range(parts):
        out[1, part].wait_recv()
    for copy in on.values():
        copy.wait_recv()


def token_kernel(settings, *refs):
    team, layer, reduce, middle, added, gather, source, column_swap = settings
    refs = list(refs)
    take = lambda: refs.pop(0)
    source_refs = [take() for _ in range(source[1])]
    added_ref = take() if added else None
    values_ref, scale_in = (take(), take()) if middle == "backward" else (None, None)
    gain_ref = take()
    new_ref = take()
    scale_ref = take() if middle == "forward" else None
    gain_grad_ref = take() if middle == "backward" else None
    last_ref = take()
    near_in, far_out, far_in, side_in, mine, sent, got = [take() for _ in range(7)]
    links = Links(sent, got)
    size = layer if reduce == "layer" else team
    spread = layer if gather == "layer" else team
    masks = set(range(2, max(size, spread) if gather else size, 2)) | {1}
    if max(size, spread if gather else 0) == 8:
        masks -= {6}
    seq_count = lax.axis_size("seq")
    column = list(range(1, seq_count)) if column_swap else []
    links.meet(
        [links.layer_peer(mask) for mask in sorted(masks)]
        + [links.column_peer(step) for step in column]
    )
    sum_blocks(
        links, size, source[0](links, size, mine, source_refs, refs), near_in, far_out, far_in, side_in, mine
    )
    rows = new_ref.shape[0]
    if column_swap:
        narrow, wide = refs[:2]
        width = mine.shape[1]
        narrow[...] = mine[...].astype(jnp.bfloat16)
        here = pl.ds(pl.multiple_of(links.seq_index * width, 128), width)
        rows_of = lambda index: pl.ds(pl.multiple_of(index * rows, 16), rows)
        swaps = [
            links.send(narrow.at[rows_of(peer[0])], wide.at[:, here], peer)
            for peer in [links.column_peer(step) for step in column]
        ]
        wide[:, here] = narrow[rows_of(links.seq_index), :]
        for copy in swaps:
            copy.wait_recv()
    parts = 2
    count = rows // parts

    few = 16

    def write(part):
        start = last_rows(0, part)

        def some_rows(at, pulls):
            first = pl.multiple_of(part * count + at * few, few)
            spot = pl.ds(first, few)
            if column_swap:
                total = wide[spot, :].astype(jnp.float32)
            else:
                total = mine[spot, :]
            if middle == "forward":
                fresh = total + added_ref[spot, :] if added else total
                new_ref[spot, :] = fresh
                mean = jnp.sum(fresh * fresh, axis=1, keepdims=True) / MODEL_WIDTH
                scale = lax.rsqrt(mean + NORM_EPS)
                scale_ref[spot, :] = jnp.broadcast_to(scale, (few, 128))
                payload = fresh * scale * gain_ref[...]
            else:
                values = values_ref[spot, :]
                scale = scale_in[spot, :1]
                weighted = total * gain_ref[...]
                dots = jnp.sum(values * weighted, axis=1, keepdims=True)
                payload = scale * weighted - values * (scale * scale * scale * dots / MODEL_WIDTH)
                pull = total * values * scale
                pulls = pulls + pull[:8] + pull[8:]
                if added:
                    payload = payload + added_ref[spot, :]
                new_ref[spot, :] = payload
            if gather:
                here = pl.ds(pl.multiple_of(start + at * few, few), few)
                last_ref[here, :] = payload.astype(jnp.bfloat16)
            return pulls

        nothing = jnp.zeros((8, MODEL_WIDTH), jnp.float32) if middle == "backward" else 0
        pulls = lax.fori_loop(0, count // few, some_rows, nothing)
        if middle == "backward":
            pull = jnp.broadcast_to(jnp.sum(pulls, axis=0, keepdims=True), gain_grad_ref.shape)
            gain_grad_ref[...] = pull if part == 0 else gain_grad_ref[...] + pull
        if not gather:
            spot = pl.ds(part * count, count)
            last_ref[:, spot] = new_ref[spot, :].T.astype(jnp.bfloat16)

    def last_rows(mask, part):
        owner = flip(links.me, mask)
        if gather == "team":
            owner = lax.rem(owner, jnp.int32(team))
        return pl.multiple_of(owner * rows + part * count, 16)

    def block_rows(mask, part):
        return pl.ds(last_rows(mask, part), count)

    if gather:
        gather_blocks(
            links, spread, lambda mask, part: last_ref.at[block_rows(mask, part)], write, parts
        )
    else:
        for part in range(parts):
            write(part)
    links.finish()


def by_pairs(links, size, mine, near_out, total, work):
    rows = mine.shape[0]

    def produce(step, mask):
        owner = lax.rem(flip(links.me, mask), jnp.int32(size))
        work(step, mask, pl.multiple_of(lax.div(owner, jnp.int32(2)) * 2 * rows, 128))
        own = lax.rem(links.me, jnp.int32(2))
        mine[...] = total[pl.ds(pl.multiple_of(own * rows, 16), rows), :]
        near_out[step] = total[pl.ds(pl.multiple_of((1 - own) * rows, 16), rows), :].astype(
            jnp.bfloat16
        )
        return near_out.at[step]

    return produce


def add_product(total, left, right_ref, first):
    width = total.shape[1] // 2
    for start in (0, width):
        spot = slice(start, start + width)
        part = against(left, right_ref[spot, :])
        total[:, spot] = part if first else total[:, spot] + part


def from_product(links, size, mine, source_refs, scratch):
    total, near_out = scratch

    def work(step, mask, first):
        rows = pl.ds(first, total.shape[0])
        for at, (left, right) in enumerate(zip(source_refs[::2], source_refs[1::2])):
            add_product(total, left[rows, :], right, at == 0)

    return by_pairs(links, size, mine, near_out, total, work)


def from_gates(links, size, mine, source_refs, scratch):
    total, near_out, gates, gate_sem = scratch
    grad_ref = source_refs[2]

    def work(step, mask, first):
        rows = pl.ds(first, total.shape[0])
        copies = [
            pltpu.make_async_copy(source_refs[at].at[rows], gates.at[at], gate_sem.at[at])
            for at in range(2)
        ]
        for copy in copies:
            copy.start()
        grads = grad_ref[rows, :]
        for at in range(2):
            down_ref, weight_ref = source_refs[3 + 2 * at : 5 + 2 * at]
            hidden = down_ref.shape[1]
            grad_hidden = jnp.dot(grads, down_ref[...], preferred_element_type=jnp.float32)
            copies[at].wait()
            gate, up = gates[at, :, :hidden], gates[at, :, hidden:]
            sigmoid = jax.nn.sigmoid(gate)
            grad_gate = grad_hidden * up * sigmoid * (1.0 + gate * (1.0 - sigmoid))
            grad_up = grad_hidden * gate * sigmoid
            both = jnp.concatenate([grad_gate, grad_up], axis=1).astype(jnp.bfloat16)
            add_product(total, both, weight_ref, at == 0)

    return by_pairs(links, size, mine, near_out, total, work)


def from_table(links, size, mine, source_refs, scratch):
    ids_ref, table_ref = source_refs
    near_out = scratch[2]
    tokens = mine.shape[0]
    count = min(512, tokens)
    depth = min(2048, table_ref.shape[1])

    def block(mask, store):
        owner = flip(links.me, mask)

        def one(at, _):
            first = pl.multiple_of(at * count, count)
            spot = pl.ds(first, count)
            ids = jnp.broadcast_to(ids_ref[pl.ds(owner, 1), spot], (8, count)).T[:, :1]
            ids = ids.astype(jnp.int32)
            found = None
            for start in range(0, table_ref.shape[1], depth):
                names = lax.broadcasted_iota(jnp.int32, (count, depth), 1) + start
                chosen = jnp.where(names == ids, 1.0, 0.0).astype(jnp.bfloat16)
                part = against(chosen, table_ref[:, start : start + depth])
                found = part if found is None else found + part
            store(spot, found)
            return 0

        lax.fori_loop(0, tokens // count, one, 0)

    def produce(step, mask):
        def keep_near(spot, found):
            near_out[step, spot, :] = found.astype(jnp.bfloat16)

        def keep_mine(spot, found):
            mine[spot, :] = found

        block(mask ^ 1, keep_near)
        block(mask, keep_mine)
        return near_out.at[step]

    return produce


def from_logits(links, size, mine, source_refs, scratch):
    parts = (len(source_refs) - 1) // 2
    logit_refs, head_refs, row_ref = source_refs[:parts], source_refs[parts:-1], source_refs[-1]
    tiles, total, near_out, tile_sem = scratch
    rows = mine.shape[0]
    width = tiles.shape[2]
    pieces = [
        (part, at) for part in range(parts) for at in range(logit_refs[part].shape[1] // width)
    ]
    order = ([6] if size == 8 else []) + group_masks(size)[0] + [0]
    work_list = [(mask, part, at) for mask in order for part, at in pieces]

    def pair_rows(mask):
        first = lax.div(flip(links.me, mask), jnp.int32(2)) * 2 * rows
        return pl.ds(pl.multiple_of(first, 128), 2 * rows)

    def fetch(index):
        mask, part, at = work_list[index]
        return pltpu.make_async_copy(
            logit_refs[part].at[pair_rows(mask), pl.ds(at * width, width)],
            tiles.at[index % 2],
            tile_sem.at[index % 2],
        )

    def work(step, mask, first_row):
        if step == 0:
            fetch(0).start()
        columns = row_ref[:, pl.ds(first_row, 2 * rows)].T
        log_total, factor, counted = columns[:, 0:1], columns[:, 1:2], columns[:, 2:3]
        wanted = columns[:, 3:4].astype(jnp.int32)
        for place, (part, at) in enumerate(pieces):
            index = step * len(pieces) + place
            if index + 1 < len(work_list):
                fetch(index + 1).start()
            fetch(index).wait()
            step_width = min(1024, width)

            def one(turn, _, part=part, at=at, index=index, place=place):
                first = pl.multiple_of(turn * step_width, step_width)
                spot = pl.ds(first, step_width)
                logits = tiles[index % 2, :, spot]
                names = lax.broadcasted_iota(jnp.int32, logits.shape, 1) + (
                    first + at * width + sum(ref.shape[1] for ref in logit_refs[:part])
                )
                grads = factor * jnp.exp(logits - log_total) - jnp.where(
                    names == wanted, counted, 0.0
                )
                weights = head_refs[part][
                    :, pl.ds(pl.multiple_of(first + at * width, step_width), step_width)
                ]
                total[...] += against(grads.astype(jnp.bfloat16), weights)
                return 0

            if place == 0:
                total[...] = jnp.zeros_like(total)
            lax.fori_loop(0, width // step_width, one, 0)

    return by_pairs(links, size, mine, near_out, total, work)


def move_tokens(
    name, collective, team, layer, rows, source, operands, *, reduce, middle, gain,
    added=None, values=None, scale=None, gather=None, column_swap=0, extra=(), any_operands=0, vmem_mib=44, us=1
):
    vmem = pl.BlockSpec(memory_space=pltpu.VMEM)
    rest = [item for item in (added, values, scale, gain) if item is not None]
    wide = jax.ShapeDtypeStruct((rows, MODEL_WIDTH), jnp.float32)
    results = [wide]
    if middle == "forward":
        results.append(jax.ShapeDtypeStruct((rows, 128), jnp.float32))
    else:
        results.append(jax.ShapeDtypeStruct((8, MODEL_WIDTH), jnp.float32))
    tall = {None: None, "team": team * rows, "layer": layer * rows}[gather]
    results.append(
        jax.ShapeDtypeStruct((tall, MODEL_WIDTH) if gather else (MODEL_WIDTH, rows), jnp.bfloat16)
    )
    size = layer if reduce == "layer" else team
    seq_count = column_swap or 1
    block = (rows * seq_count, MODEL_WIDTH // seq_count)
    masks, routed = group_masks(size)
    steps = len(masks) + 1 + routed
    copies = steps + len(masks) + 2 * routed + (seq_count - 1)
    if gather:
        masks_out, routed_out = group_masks(layer if gather == "layer" else team)
        copies += 2 * (1 + 2 * len(masks_out)) + 4 * routed_out
    scratch = [
        pltpu.VMEM((steps, *block), jnp.bfloat16),
        pltpu.VMEM((max(steps - 1, 1), *block), jnp.bfloat16),
        pltpu.VMEM((len(masks), *block), jnp.bfloat16),
        pltpu.VMEM((2, block[0] // 2, block[1]) if routed else (2, 16, 128), jnp.bfloat16),
        pltpu.VMEM(block, jnp.float32),
        pltpu.SemaphoreType.DMA((copies,)),
        pltpu.SemaphoreType.DMA((copies,)),
    ]
    if column_swap:
        scratch += [
            pltpu.VMEM(block, jnp.bfloat16),
            pltpu.VMEM((rows, MODEL_WIDTH), jnp.bfloat16),
        ]
    scratch += list(extra)
    settings = (
        team, layer, reduce, middle, added is not None, gather, (source, len(operands)), column_swap
    )
    return pl.pallas_call(
        functools.partial(token_kernel, settings),
        name=name,
        out_shape=results,
        in_specs=[pl.BlockSpec(memory_space=pl.ANY)] * any_operands
        + [vmem] * (len(operands) + len(rest) - any_operands),
        out_specs=[vmem] * len(results),
        scratch_shapes=scratch,
        cost_estimate=pl.CostEstimate(
            flops=0, bytes_accessed=us * 3_700_000, transcendentals=0
        ),
        compiler_params=pltpu.CompilerParams(
            collective_id=collective, has_side_effects=True, vmem_limit_bytes=vmem_mib * 2**20
        ),
    )(*operands, *rest)


def spread_kernel(layer, item_ref, all_ref, sent, got):
    links = Links(sent, got)
    peers = [links.layer_peer(mask) for mask in range(1, layer)]
    links.meet(peers)
    all_ref[links.me] = item_ref[...]
    copies = [links.send(item_ref, all_ref.at[links.me], peer) for peer in peers]
    for copy in copies:
        copy.wait_recv()
    links.finish()


def spread(name, collective, layer, item):
    vmem = pl.BlockSpec(memory_space=pltpu.VMEM)
    return pl.pallas_call(
        functools.partial(spread_kernel, layer),
        name=name,
        out_shape=jax.ShapeDtypeStruct((layer, *item.shape), item.dtype),
        in_specs=[vmem],
        out_specs=vmem,
        scratch_shapes=[pltpu.SemaphoreType.DMA((layer - 1,))] * 2,
        cost_estimate=pl.CostEstimate(flops=0, bytes_accessed=3_700_000, transcendentals=0),
        compiler_params=pltpu.CompilerParams(collective_id=collective, has_side_effects=True),
    )(item)


def layout(groups, count):
    ends = jnp.cumsum(groups)
    index = jnp.arange(count, dtype=jnp.int32)
    row_of = jnp.sum((ends[None, :] <= index[:, None]).astype(jnp.int32), axis=1)
    length = groups[row_of]
    row_start = ends[row_of] - length
    source = jnp.where(index > row_start, index - 1, row_start + length - 1)
    return (row_of, row_start, length, source)


def spread_lanes(values, head, heads):
    if heads == 1:
        return values
    zeros = jnp.zeros_like(values)
    return jnp.concatenate([values if index == head else zeros for index in range(heads)], axis=1)


def turned(values, cosine, sine):
    pieces = []
    for first in range(0, values.shape[1], 128):
        piece = values[:, first : first + 128]
        lane = lax.broadcasted_iota(jnp.int32, piece.shape, 1)
        partner = jnp.where(
            lax.rem(lane, jnp.int32(HEAD_SIZE)) < HEAD_SIZE // 2,
            pltpu.roll(piece, 128 - HEAD_SIZE // 2, 1),
            pltpu.roll(piece, HEAD_SIZE // 2, 1),
        )
        pieces.append(piece * cosine + partner * sine)
    return jnp.concatenate(pieces, axis=1)


def head_columns(values, head):
    return values[:, head * HEAD_SIZE : (head + 1) * HEAD_SIZE]


def of_batch(batch, values, first, second):
    return jnp.where(batch == 0, head_columns(values, first), head_columns(values, second))


UNIT_HEADS = ((0, 1), (2, 3), (1, 0), (3, 2))


def project_kernel(
    team, query_width, linear_ref, up_ref, cosine_ref, sine_ref, choice_ref, ready_ref,
    query_ref, key_ref, value_ref, low_ref, tail, borrowed, arrived, sent, got,
):
    links = Links(sent, got)
    seq_count = lax.axis_size("seq")
    arrived[...] = jnp.zeros_like(arrived)
    team_peers = [links.layer_peer(mask) for mask in range(1, team)]
    steps = sorted({1, 2, seq_count - 1, seq_count - 2})
    links.meet(team_peers + [links.column_peer(step) for step in steps])
    batch = lax.div(links.me, jnp.int32(team))
    group_rows = query_ref.shape[0]
    half = group_rows // 2
    chunk = half // 2
    kv_width = KEY_HEADS * HEAD_SIZE

    def rows_of(at, _):
        first = pl.multiple_of(at * chunk, chunk)
        rows = pl.ds(first, chunk)
        low = linear_ref[rows, query_width + 2 * kv_width : query_width + 2 * kv_width + 128]
        low = low.astype(jnp.bfloat16)
        low_ref[rows, :] = low
        linear = linear_ref[rows, : query_width + 2 * kv_width] + ADAPTER_SCALE * jnp.dot(
            low, up_ref[...], preferred_element_type=jnp.float32
        )
        cosine, sine = cosine_ref[rows, :], sine_ref[rows, :]
        query_ref[rows, :] = turned(linear[:, :query_width], cosine, sine).astype(jnp.bfloat16)
        keys = turned(linear[:, query_width : query_width + kv_width], cosine, sine)
        keys = keys.astype(jnp.bfloat16)
        values = linear[:, query_width + kv_width :].astype(jnp.bfloat16)
        later = pl.ds(pl.multiple_of(half + first, chunk), chunk)
        for unit, pair in enumerate(UNIT_HEADS):
            key_ref[unit, later, :] = of_batch(batch, keys, *pair)
            value_ref[unit, later, :] = of_batch(batch, values, *pair)

        @pl.when(at >= 2)
        def _():
            spot = pl.ds(pl.multiple_of(first - half, chunk), chunk)
            tail[spot, :] = jnp.concatenate(
                [keys[:, kv_width // 2 :], values[:, kv_width // 2 :]], axis=1
            )

        return 0

    lax.fori_loop(0, 2, lambda at, _: rows_of(at + 2, 0), 0)
    count = half // team
    mine = pl.ds(pl.multiple_of(lax.rem(links.me, jnp.int32(team)) * count, 16), count)
    copies = links.along(tail.at[mine], arrived, (1, -1, -2))
    lax.fori_loop(0, 2, rows_of, 0)
    for wait in copies:
        wait()
    chosen = tail[mine, :].astype(jnp.float32) * choice_ref[3:4, :1]
    for at in range(3):
        chosen = chosen + arrived[at].astype(jnp.float32) * choice_ref[at : at + 1, :1]
    borrowed[mine, :] = chosen.astype(jnp.bfloat16)
    copies = [links.send(borrowed.at[mine], borrowed.at[mine], peer) for peer in team_peers]
    for copy in copies:
        copy.wait_recv()
    before = borrowed[...]
    for unit, (first, second) in enumerate(UNIT_HEADS):
        if unit % 2:
            key_ref[unit, :half, :] = of_batch(batch, before, first - 2, second - 2)
            value_ref[unit, :half, :] = of_batch(batch, before, first, second)
        else:
            key_ref[unit, :half, :] = jnp.zeros((half, HEAD_SIZE), jnp.bfloat16)
            value_ref[unit, :half, :] = jnp.zeros((half, HEAD_SIZE), jnp.bfloat16)
    links.finish()


def project(collective, team, query_width, linear, up, cosine, sine, choice, ready):
    vmem = pl.BlockSpec(memory_space=pltpu.VMEM)
    group_rows = linear.shape[0]
    half, width = group_rows // 2, KEY_HEADS * HEAD_SIZE
    copies = 3 + team - 1
    units = jax.ShapeDtypeStruct((4, half + group_rows, HEAD_SIZE), jnp.bfloat16)
    return pl.pallas_call(
        functools.partial(project_kernel, team, query_width),
        name="project",
        out_shape=[
            jax.ShapeDtypeStruct((group_rows, query_width), jnp.bfloat16),
            units,
            units,
            jax.ShapeDtypeStruct((group_rows, 128), jnp.bfloat16),
        ],
        in_specs=[vmem] * 5 + [pl.BlockSpec(memory_space=pl.ANY)],
        out_specs=[vmem] * 4,
        scratch_shapes=[
            pltpu.VMEM((half, width), jnp.bfloat16),
            pltpu.VMEM((half, width), jnp.bfloat16),
            pltpu.VMEM((3, half // team, width), jnp.bfloat16),
            pltpu.SemaphoreType.DMA((copies,)),
            pltpu.SemaphoreType.DMA((copies,)),
        ],
        cost_estimate=pl.CostEstimate(flops=0, bytes_accessed=3_700_000, transcendentals=0),
        compiler_params=pltpu.CompilerParams(
            collective_id=collective, has_side_effects=True, vmem_limit_bytes=40 * 2**20
        ),
    )(linear, up, cosine, sine, choice, ready)


def unit_halves(unit, half):
    if unit % 2:
        return ((0, (0, half)), (half, (2 * half,)))
    return ((half, (half, 2 * half)), (0, (half,)))


def block_scores(queries, keys, causal):
    scores = against(queries, keys) * HEAD_SIZE ** (-0.5)
    if causal:
        seen = lax.broadcasted_iota(jnp.int32, scores.shape, 1) <= lax.broadcasted_iota(
            jnp.int32, scores.shape, 0
        )
        scores = jnp.where(seen, scores, MASKED)
    return scores


def attend_kernel(heads, query_ref, key_ref, value_ref, down_ref, out_ref, log_ref):
    head_width = heads * HEAD_SIZE
    half = query_ref.shape[0] // 2
    for unit in range(4):
        lanes = slice(unit * head_width, (unit + 1) * head_width)
        for first_row, blocks in unit_halves(unit, half):
            rows = slice(first_row, first_row + half)
            queries = query_ref[rows, lanes]
            result = None
            for head in range(heads):
                scores = [
                    block_scores(
                        queries,
                        spread_lanes(key_ref[unit, start : start + half, :], head, heads),
                        index == len(blocks) - 1,
                    )
                    for index, start in enumerate(blocks)
                ]
                peak = functools.reduce(
                    jnp.maximum, [jnp.max(item, axis=1, keepdims=True) for item in scores]
                )
                terms = [jnp.exp(item - peak) for item in scores]
                summed = sum(jnp.sum(item, axis=1, keepdims=True) for item in terms)
                share = 1.0 / summed
                for item, start in zip(terms, blocks):
                    part = jnp.dot(
                        (item * share).astype(jnp.bfloat16),
                        spread_lanes(value_ref[unit, start : start + half, :], head, heads),
                        preferred_element_type=jnp.float32,
                    )
                    result = part if result is None else result + part
                log_ref[unit, rows, head : head + 1] = peak + jnp.log(summed)
            out_ref[rows, lanes] = result.astype(jnp.bfloat16)
    out_ref[:, 4 * head_width :] = jnp.dot(
        out_ref[:, : 4 * head_width], down_ref[...], preferred_element_type=jnp.float32
    ).astype(jnp.bfloat16)


def attend(heads, queries, keys, values, down):
    vmem = pl.BlockSpec(memory_space=pltpu.VMEM)
    group_rows, query_width = queries.shape
    return pl.pallas_call(
        functools.partial(attend_kernel, heads),
        name="attend",
        out_shape=[
            jax.ShapeDtypeStruct((group_rows, query_width + 128), jnp.bfloat16),
            jax.ShapeDtypeStruct((4, group_rows, heads), jnp.float32),
        ],
        in_specs=[vmem] * 4,
        out_specs=[vmem] * 2,
        cost_estimate=pl.CostEstimate(flops=0, bytes_accessed=3_700_000, transcendentals=0),
        compiler_params=pltpu.CompilerParams(vmem_limit_bytes=48 * 2**20),
    )(queries, keys, values, down)


def attend_back_kernel(
    heads, query_ref, key_ref, value_ref, log_ref, grad_ref, down_ref, cosine_ref, sine_ref,
    grad_query_ref, grad_key_ref, grad_value_ref, wide,
):
    head_width = heads * HEAD_SIZE
    query_width = 4 * head_width
    half = query_ref.shape[0] // 2
    grad_key_ref[...] = jnp.zeros_like(grad_key_ref)
    grad_value_ref[...] = jnp.zeros_like(grad_value_ref)
    scale = HEAD_SIZE ** (-0.5)
    over_rows = (((0,), (0,)), ((), ()))
    for unit in range(4):
        lanes = slice(unit * head_width, (unit + 1) * head_width)
        for first_row, blocks in unit_halves(unit, half):
            rows = slice(first_row, first_row + half)
            queries = query_ref[rows, lanes]
            low = grad_ref[rows, query_width:]
            low_first = low.astype(jnp.bfloat16)
            low_rest = (low - low_first.astype(jnp.float32)).astype(jnp.bfloat16)
            grads = grad_ref[rows, lanes] + against(low_first, down_ref[lanes, :])
            grads = (grads + against(low_rest, down_ref[lanes, :])).astype(jnp.bfloat16)
            grad_query = None
            for head in range(heads):
                own = slice(head * HEAD_SIZE, (head + 1) * HEAD_SIZE)
                keys = [
                    spread_lanes(key_ref[unit, start : start + half, :], head, heads)
                    for start in blocks
                ]
                probs, pulls = [], []
                for index, start in enumerate(blocks):
                    scores = block_scores(queries, keys[index], index == len(blocks) - 1)
                    probs.append(jnp.exp(scores - log_ref[unit, rows, head : head + 1]))
                    values = spread_lanes(value_ref[unit, start : start + half, :], head, heads)
                    pulls.append(against(grads, values))
                inner = sum(
                    jnp.sum(prob * pull, axis=1, keepdims=True)
                    for prob, pull in zip(probs, pulls)
                )
                for prob, pull, key, start in zip(probs, pulls, keys, blocks):
                    grad_scores = (prob * (pull - inner)).astype(jnp.bfloat16)
                    part = jnp.dot(grad_scores, key, preferred_element_type=jnp.float32)
                    grad_query = part if grad_query is None else grad_query + part
                    grad_key = lax.dot_general(
                        grad_scores, queries, over_rows, preferred_element_type=jnp.float32
                    )
                    grad_value = lax.dot_general(
                        prob.astype(jnp.bfloat16),
                        grads,
                        over_rows,
                        preferred_element_type=jnp.float32,
                    )
                    spot = slice(start, start + half)
                    grad_key_ref[unit, spot, :] += grad_key[:, own] * scale
                    grad_value_ref[unit, spot, :] += grad_value[:, own]
            wide[rows, lanes] = grad_query * scale
    grad_query_ref[...] = turned(wide[...], cosine_ref[...], -sine_ref[...]).astype(jnp.bfloat16)


def attend_back(heads, queries, keys, values, log_totals, grads, down, cosine, sine):
    vmem = pl.BlockSpec(memory_space=pltpu.VMEM)
    units = jax.ShapeDtypeStruct(keys.shape, jnp.float32)
    return pl.pallas_call(
        functools.partial(attend_back_kernel, heads),
        name="attend_back",
        out_shape=[jax.ShapeDtypeStruct(queries.shape, jnp.bfloat16), units, units],
        in_specs=[vmem] * 8,
        out_specs=[vmem] * 3,
        scratch_shapes=[pltpu.VMEM(queries.shape, jnp.float32)],
        cost_estimate=pl.CostEstimate(flops=0, bytes_accessed=3_700_000, transcendentals=0),
        compiler_params=pltpu.CompilerParams(vmem_limit_bytes=52 * 2**20),
    )(queries, keys, values, log_totals, grads, down, cosine, sine)


def give_back_kernel(
    team, query_ref, key_ref, value_ref, up_ref, cosine_ref, sine_ref, choice_ref, out_ref,
    tail, arrived, sent, got,
):
    links = Links(sent, got)
    seq_count = lax.axis_size("seq")
    steps = sorted({1, 2, seq_count - 1, seq_count - 2})
    arrived[...] = jnp.zeros_like(arrived)
    links.meet([links.column_peer(step) for step in steps])
    batch = lax.div(links.me, jnp.int32(team))
    group_rows, query_width = query_ref.shape
    half = group_rows // 2
    kv_width = KEY_HEADS * HEAD_SIZE

    def natural(ref, rows, heads):
        units = {0: (0, 2), 1: (2, 0), 2: (1, 3), 3: (3, 1)}
        return jnp.concatenate(
            [
                jnp.where(batch == 0, ref[units[head][0], rows, :], ref[units[head][1], rows, :])
                for head in heads
            ],
            axis=1,
        )

    before = slice(0, half)
    own = jnp.concatenate(
        [natural(key_ref, before, (2, 3)), natural(value_ref, before, (2, 3))], axis=1
    )
    tail[...] = own.astype(jnp.bfloat16)
    copies = links.along(tail, arrived, (-1, 1, 2))
    middle, last = slice(half, 2 * half), slice(2 * half, 3 * half)

    def write(first, keys, values):
        rows = slice(first, first + half)
        cosine, sine = cosine_ref[rows, :], sine_ref[rows, :]
        out_ref[rows, :query_width] = query_ref[rows, :]
        out_ref[rows, query_width : query_width + kv_width] = turned(keys, cosine, -sine).astype(
            jnp.bfloat16
        )
        out_ref[rows, query_width + kv_width : query_width + 2 * kv_width] = values.astype(
            jnp.bfloat16
        )
        low = ADAPTER_SCALE * against(out_ref[rows, : query_width + 2 * kv_width], up_ref[...])
        first_part = low.astype(jnp.bfloat16)
        out_ref[rows, query_width + 2 * kv_width : query_width + 2 * kv_width + 128] = first_part
        out_ref[rows, query_width + 2 * kv_width + 128 :] = (
            low - first_part.astype(jnp.float32)
        ).astype(jnp.bfloat16)

    every = (0, 1, 2, 3)
    write(0, natural(key_ref, middle, every), natural(value_ref, middle, every))
    back = own * choice_ref[3:4, :1]
    for at, wait in enumerate(copies):
        wait()
        back = back + arrived[at].astype(jnp.float32) * choice_ref[at : at + 1, :1]
    keys, values = natural(key_ref, last, every), natural(value_ref, last, every)
    small = kv_width // 2
    keys = jnp.concatenate([keys[:, :small], keys[:, small:] + back[:, :small]], axis=1)
    values = jnp.concatenate([values[:, :small], values[:, small:] + back[:, small:]], axis=1)
    write(half, keys, values)
    links.finish()


def give_back(collective, team, grad_query, grad_key, grad_value, up, cosine, sine, choice):
    vmem = pl.BlockSpec(memory_space=pltpu.VMEM)
    group_rows, query_width = grad_query.shape
    half, width = group_rows // 2, KEY_HEADS * HEAD_SIZE
    return pl.pallas_call(
        functools.partial(give_back_kernel, team),
        name="give_back",
        out_shape=jax.ShapeDtypeStruct((group_rows, query_width + 2 * width + 256), jnp.bfloat16),
        in_specs=[vmem] * 7,
        out_specs=vmem,
        scratch_shapes=[
            pltpu.VMEM((half, width), jnp.bfloat16),
            pltpu.VMEM((3, half, width), jnp.bfloat16),
            pltpu.SemaphoreType.DMA((3,)),
            pltpu.SemaphoreType.DMA((3,)),
        ],
        cost_estimate=pl.CostEstimate(flops=0, bytes_accessed=3_700_000, transcendentals=0),
        compiler_params=pltpu.CompilerParams(
            collective_id=collective, has_side_effects=True, vmem_limit_bytes=40 * 2**20
        ),
    )(grad_query, grad_key, grad_value, up, cosine, sine, choice)


def start_kernel(ids_ref, piece_ref, ids_out, piece_out, sent, got):
    links = Links(sent, got)
    others = [links.column_peer(step) for step in range(1, lax.axis_size("seq"))]
    links.meet(others)
    copies = []
    for source, target in ((ids_ref, ids_out), (piece_ref, piece_out)):
        copies += [links.send(source, target.at[links.seq_index], other) for other in others]
        target[links.seq_index] = source[...]
    for copy in copies:
        copy.wait_recv()
    links.finish()


def start(collective, seq_count, ids, piece):
    vmem = pl.BlockSpec(memory_space=pltpu.VMEM)
    shape = lambda item: jax.ShapeDtypeStruct((seq_count, *item.shape), item.dtype)
    return pl.pallas_call(
        start_kernel,
        name="start",
        out_shape=[shape(ids), shape(piece)],
        in_specs=[vmem, vmem],
        out_specs=[vmem, vmem],
        scratch_shapes=[pltpu.SemaphoreType.DMA((2 * (seq_count - 1),))] * 2,
        cost_estimate=pl.CostEstimate(flops=0, bytes_accessed=3_700_000, transcendentals=0),
        compiler_params=pltpu.CompilerParams(collective_id=collective, has_side_effects=True),
    )(ids, piece)


def layer_rows_kernel(layer, item_ref, all_ref, sent, got):
    links = Links(sent, got)
    peers = [links.layer_peer(mask) for mask in range(1, layer)]
    links.meet(peers)
    all_ref[:, pl.ds(links.me, 1)] = item_ref[...][:, None]
    copies = [links.send(item_ref, all_ref.at[:, links.me], peer) for peer in peers]
    for copy in copies:
        copy.wait_recv()
    links.finish()


def layer_rows(collective, layer, item):
    vmem = pl.BlockSpec(memory_space=pltpu.VMEM)
    outer, rows, columns = item.shape
    return pl.pallas_call(
        functools.partial(layer_rows_kernel, layer),
        name="layer_rows",
        out_shape=jax.ShapeDtypeStruct((outer, layer, rows, columns), item.dtype),
        in_specs=[vmem],
        out_specs=vmem,
        scratch_shapes=[pltpu.SemaphoreType.DMA((layer - 1,))] * 2,
        cost_estimate=pl.CostEstimate(flops=0, bytes_accessed=3_700_000, transcendentals=0),
        compiler_params=pltpu.CompilerParams(collective_id=collective, has_side_effects=True),
    )(item)


def logits_kernel(first_name, rows_ref, head_ref, target_ref, logits_ref, stats_ref):
    count, columns = logits_ref.shape
    width = 1024 if columns % 1024 == 0 else 512
    wanted = target_ref[...].T[:, :1].astype(jnp.int32) - first_name

    def one(at, state):
        peak, summed, picked = state
        spot = pl.ds(pl.multiple_of(at * width, width), width)
        logits = jnp.dot(rows_ref[...], head_ref[:, spot], preferred_element_type=jnp.float32)
        logits_ref[:, spot] = logits
        higher = jnp.maximum(peak, jnp.max(logits, axis=1, keepdims=True))
        summed = summed * jnp.exp(peak - higher) + jnp.sum(
            jnp.exp(logits - higher), axis=1, keepdims=True
        )
        names = lax.broadcasted_iota(jnp.int32, logits.shape, 1) + at * width
        picked = picked + jnp.sum(
            jnp.where(names == wanted, logits, 0.0), axis=1, keepdims=True
        )
        return higher, summed, picked

    column = lambda value: jnp.full((count, 1), value, jnp.float32)
    peak, summed, picked = lax.fori_loop(
        0, columns // width, one, (column(MASKED), column(0.0), column(0.0))
    )
    lane = lax.broadcasted_iota(jnp.int32, (count, 128), 1)
    stats = jnp.where(lane == 0, peak, jnp.where(lane == 1, summed, picked))
    stats_ref[...] = stats.T[:8]


def head_logits(rows, head, targets, first_name):
    count, columns = rows.shape[0], head.shape[1]
    block = min(512, count)
    return pl.pallas_call(
        functools.partial(logits_kernel, first_name),
        name="head_logits",
        grid=(count // block,),
        out_shape=[
            jax.ShapeDtypeStruct((count, columns), jnp.float32),
            jax.ShapeDtypeStruct((8, count), jnp.float32),
        ],
        in_specs=[
            pl.BlockSpec((block, MODEL_WIDTH), lambda at: (at, 0)),
            pl.BlockSpec(head.shape, lambda at: (0, 0)),
            pl.BlockSpec((8, block), lambda at: (0, at)),
        ],
        out_specs=[
            pl.BlockSpec((block, columns), lambda at: (at, 0)),
            pl.BlockSpec((8, block), lambda at: (0, at)),
        ],
        cost_estimate=pl.CostEstimate(flops=0, bytes_accessed=90_000_000, transcendentals=0),
        compiler_params=pltpu.CompilerParams(vmem_limit_bytes=48 * 2**20),
    )(rows, head, targets)


def table_kernel(
    layer, tile, low_ref, ids_ref, small_ref, grad_ref, norm_ref, small_out, held,
    small_in, small_mid, small_up, squares, layer_in, between, seq_in, sent, got,
):
    links = Links(sent, got)
    seq_count = lax.axis_size("seq")
    peers = [links.layer_peer(mask) for mask in range(1, layer)]
    others = [links.column_peer(step) for step in range(1, seq_count)]
    links.meet(peers + others)
    width = held.shape[1]
    rows = low_ref.shape[1]
    tiles = grad_ref.shape[1] // tile
    masks, routed = group_masks(layer)
    half = width // 2

    features_of = lambda index: pl.ds(pl.multiple_of(index * width, 16), width)
    step_lanes = rows * seq_count // 2
    steps = seq_count // 2

    def block(mask, phase):
        return held.at[flip(links.me, mask), :, pl.ds(phase * step_lanes, step_lanes)]

    def half_block(mask, which, phase):
        return held.at[
            flip(links.me, mask), pl.ds(which * half, half), pl.ds(phase * step_lanes, step_lanes)
        ]

    swaps = [
        links.send(
            low_ref.at[features_of(peer[0])],
            held.at[links.me, :, pl.ds((at + 1) * rows, rows)],
            peer,
        )
        for at, peer in enumerate(others)
    ]
    held[links.me, :, :rows] = low_ref[features_of(links.seq_index), :]
    small_rows = small_ref.shape[0] // layer
    rows_of = lambda owner: pl.ds(pl.multiple_of(owner * small_rows, 8), small_rows)
    small_near = [
        links.send(small_ref.at[rows_of(peer[1])], small_in.at[links.me], peer) for peer in peers
    ]
    small_in[links.me] = small_ref[rows_of(links.me), :]

    def add(mask, phase, first=False, last=False):
        owner = flip(links.me, mask)
        lanes = slice(phase * step_lanes, (phase + 1) * step_lanes)

        def one(at, _):
            spot = pl.ds(pl.multiple_of(at * tile, tile), tile)
            ids = ids_ref[pl.ds(owner, 1), lanes]
            wanted = lax.broadcasted_iota(jnp.int32, (tile, step_lanes), 0) + at * tile
            chosen = jnp.where(wanted == ids, 1.0, 0.0).astype(jnp.bfloat16)
            part = against(held[owner, :, lanes], chosen)
            part = part if first else grad_ref[:, spot] + part
            grad_ref[:, spot] = part
            if last:
                squares[...] += jnp.sum((part * part).reshape(-1, 8, tile), axis=0)
            return 0

        lax.fori_loop(0, tiles, one, 0)

    near, out, on, over, last = {}, {}, {}, {}, {}

    def send_own(phase):
        near[phase] = links.send(block(0, phase), block(0, phase), links.layer_peer(1))
        for mask in masks:
            out[mask, phase] = links.send(
                block(0, phase), block(0, phase), links.layer_peer(mask)
            )

    def pass_on(phase):
        for at, mask in enumerate(masks):
            out[mask, phase].wait_recv()
            if routed:
                over[at, phase] = links.send(
                    half_block(mask, at, phase),
                    half_block(mask, at, phase),
                    links.layer_peer(masks[1 - at]),
                )
            on[mask, phase] = links.send(
                block(mask, phase), block(mask, phase), links.layer_peer(1)
            )

    def pass_last(phase):
        for at in range(2):
            over[at, phase].wait_recv()
            last[at, phase] = links.send(
                half_block(6, at, phase), half_block(6, at, phase), links.layer_peer(1)
            )

    def add_last(phase):
        add(6, phase)
        for at in range(2):
            last[at, phase].wait_recv()
        add(7, phase, last=phase == 1)

    squares[...] = jnp.zeros_like(squares)
    for copy in swaps[: steps - 1]:
        copy.wait_recv()
    send_own(0)
    add(0, 0, first=True)
    near[0].wait_recv()
    add(1, 0)
    pass_on(0)
    for mask in masks:
        add(mask, 0)
    for copy in swaps[steps - 1 :]:
        copy.wait_recv()
    send_own(1)
    for copy in small_near:
        copy.wait_recv()
    whole = small_in[0]
    for at in range(1, layer):
        whole = whole + small_in[at]
    small_mid[...] = whole
    small_up[links.seq_index] = whole
    small_ups = [
        links.send(small_mid, small_up.at[links.seq_index], other) for other in others
    ]
    if routed:
        pass_last(0)
    for mask in masks:
        on[mask, 0].wait_recv()
        add(mask ^ 1, 0)
    pass_on(1)
    for copy in small_ups:
        copy.wait_recv()
    whole = small_up[0]
    for at in range(1, seq_count):
        whole = whole + small_up[at]
    small_out[rows_of(links.me), :] = whole
    small_on = [
        links.send(small_out.at[rows_of(links.me)], small_out.at[rows_of(links.me)], peer)
        for peer in peers
    ]
    if routed:
        add_last(0)
    add(0, 1)
    near[1].wait_recv()
    add(1, 1)
    if routed:
        pass_last(1)
    for mask in masks:
        add(mask, 1)
    for mask in masks:
        on[mask, 1].wait_recv()
        add(mask ^ 1, 1, last=not routed and mask == masks[-1])
    if routed:
        add_last(1)
    for copy in small_on:
        copy.wait_recv()
    total = squares[...]
    between[0] = jnp.broadcast_to(jnp.sum(total), (8, 128))
    layer_in[links.me] = between[0]
    copies = [links.send(between.at[0], layer_in.at[links.me], peer) for peer in peers]
    for copy in copies:
        copy.wait_recv()
    whole = layer_in[0]
    for at in range(1, layer):
        whole = whole + layer_in[at]
    between[1] = whole
    seq_in[links.seq_index] = whole
    ups = [links.send(between.at[1], seq_in.at[links.seq_index], other) for other in others]
    for copy in ups:
        copy.wait_recv()
    whole = seq_in[0]
    for at in range(1, seq_count):
        whole = whole + seq_in[at]
    norm_ref[...] = whole
    links.finish()


def table_gradient(collective, seq_count, layer, low, ids, small, table_width):
    vmem = pl.BlockSpec(memory_space=pltpu.VMEM)
    width, rows = MODEL_WIDTH // seq_count, low.shape[1] * seq_count
    tile = min(1024, table_width)
    masks, routed = group_masks(layer)
    copies = (seq_count - 1) * 3 + 3 * (layer - 1) + 2 * (1 + 2 * len(masks) + 4 * routed)
    piece = (small.shape[0] // layer, small.shape[1])
    return pl.pallas_call(
        functools.partial(table_kernel, layer, tile),
        name="table_gradient",
        out_shape=[
            jax.ShapeDtypeStruct((width, table_width), jnp.float32),
            jax.ShapeDtypeStruct((8, 128), jnp.float32),
            jax.ShapeDtypeStruct(small.shape, jnp.float32),
        ],
        in_specs=[vmem] * 3,
        out_specs=[vmem] * 3,
        scratch_shapes=[
            pltpu.VMEM((layer, width, rows), jnp.bfloat16),
            pltpu.VMEM((layer, *piece), jnp.float32),
            pltpu.VMEM(piece, jnp.float32),
            pltpu.VMEM((seq_count, *piece), jnp.float32),
            pltpu.VMEM((8, tile), jnp.float32),
            pltpu.VMEM((layer, 8, 128), jnp.float32),
            pltpu.VMEM((2, 8, 128), jnp.float32),
            pltpu.VMEM((seq_count, 8, 128), jnp.float32),
            pltpu.SemaphoreType.DMA((copies,)),
            pltpu.SemaphoreType.DMA((copies,)),
        ],
        cost_estimate=pl.CostEstimate(flops=0, bytes_accessed=3_700_000, transcendentals=0),
        compiler_params=pltpu.CompilerParams(
            collective_id=collective, has_side_effects=True, vmem_limit_bytes=30 * 2**20
        ),
    )(low, ids, small)


def update_kernel(
    keyval_width, norm_ref, small_ref, moment_ref, weight_ref, gains_ref, gain_first_ref, gain_second_ref,
    grad_ref, table_ref, first_ref, second_ref,
    norm_out, moment_out, weight_out, gains_out, gain_first_out, gain_second_out,
    table_out, first_out, second_out, current, multiplier,
):
    step = pl.program_id(0)
    adapters = 8 * ADAPTER_RANK
    row = lax.broadcasted_iota(jnp.int32, (adapters, MODEL_WIDTH), 0)
    column = lax.broadcasted_iota(jnp.int32, (adapters, MODEL_WIDTH), 1)
    own = (row < 6 * ADAPTER_RANK) | (column < keyval_width)
    piece = 3 * MODEL_WIDTH // (2 * ADAPTER_RANK)
    side = lambda axis: lax.div(
        lax.broadcasted_iota(jnp.int32, (adapters, adapters), axis), jnp.int32(ADAPTER_RANK)
    )
    together = side(0) == side(1)

    def adamw(grad, weight, first, second):
        first = BETA_FIRST * first + (1.0 - BETA_FIRST) * grad
        second = BETA_SECOND * second + (1.0 - BETA_SECOND) * grad * grad
        fixed_second = second * (1.0 / (1.0 - BETA_SECOND**STEP))
        low = fixed_second * lax.rsqrt(fixed_second) + ADAM_EPS
        inverse = pl.reciprocal(low, approx=True)
        inverse = inverse * (2.0 - low * inverse)
        fresh = weight * (1.0 - ADAM_RATE * DECAY_RATE) - (
            ADAM_RATE / (1.0 - BETA_FIRST**STEP)
        ) * (first * inverse)
        return first, second, fresh

    @pl.when(step == 0)
    def _():
        small = small_ref[...]
        loss_spot = (lax.broadcasted_iota(jnp.int32, small.shape, 0) >= 6 * ADAPTER_RANK) & (
            lax.broadcasted_iota(jnp.int32, small.shape, 1) >= keyval_width + piece
        )
        counted = jnp.where(loss_spot, 0.0, small * small)
        norm = jnp.sqrt(norm_ref[...] + jnp.sum(counted))
        norm_out[...] = norm
        multiplier[...] = jnp.minimum(1.0, CLIP_NORM / (norm + 1e-06))
        factor = multiplier[0:1, 0:1]
        grad = jnp.where(own, small[:adapters], 0.0)
        fresh = MUON_MOMENTUM * moment_ref[...] + grad * factor
        moment_out[...] = fresh
        sums = jnp.broadcast_to(jnp.sum(fresh * fresh, axis=1, keepdims=True), (adapters, 128))
        sums = jnp.dot(
            jnp.where(together, 1.0, 0.0), sums, precision=PRECISE, preferred_element_type=jnp.float32
        )
        current[...] = fresh / (jnp.sqrt(sums[:, :1]) + 1e-07)

    @pl.when((step >= 1) & (step <= 5))
    def _():
        now = current[...]
        gram = lax.dot_general(
            now, now, (((1,), (1,)), ((), ())), precision=PRECISE, preferred_element_type=jnp.float32
        )
        gram = jnp.where(together, gram, 0.0)
        square = jnp.dot(gram, gram, precision=PRECISE, preferred_element_type=jnp.float32)
        current[...] = SCHULZ[0] * now + jnp.dot(
            SCHULZ[1] * gram + SCHULZ[2] * square,
            now,
            precision=PRECISE,
            preferred_element_type=jnp.float32,
        )

    @pl.when(step == 6)
    def _():
        stretch = jnp.where(
            row < 6 * ADAPTER_RANK,
            0.2 * math.sqrt(MODEL_WIDTH),
            0.2 * math.sqrt(keyval_width),
        )
        weight_out[...] = (
            weight_ref[...] * (1.0 - MUON_RATE * DECAY_RATE) - MUON_RATE * (current[...] * stretch)
        )

    @pl.when(step == 7)
    def _():
        factor = multiplier[0:1, 0:1]
        base = 6 * ADAPTER_RANK
        grad = small_ref[base : base + 2 * ADAPTER_RANK, keyval_width : keyval_width + piece]
        first, second, fresh = adamw(
            grad * factor, gains_ref[...], gain_first_ref[...], gain_second_ref[...]
        )
        gain_first_out[...] = first
        gain_second_out[...] = second
        gains_out[...] = fresh

    count, columns = table_out.shape
    factor = multiplier[0:1, 0:1]
    wide = min(1024, columns)

    def eight_rows(at, _):
        rows = pl.ds(pl.multiple_of(at * 8, 8), 8)
        here = pl.ds(pl.multiple_of(step * count + at * 8, 8), 8)
        for start in range(0, columns, wide):
            spot = slice(start, start + wide)
            first, second, fresh = adamw(
                grad_ref[here, spot] * factor,
                table_ref[rows, spot],
                first_ref[rows, spot],
                second_ref[rows, spot],
            )
            first_out[rows, spot] = first
            second_out[rows, spot] = second
            table_out[rows, spot] = fresh
        return 0

    lax.fori_loop(0, count // 8, eight_rows, 0)


def update(keyval_width, norm, small, moment, weight, gains, gain_first, gain_second, grad, table, first, second):
    steps = 8
    rows, columns = table.shape
    whole = lambda item: pl.BlockSpec(item.shape, lambda step: (0, 0))
    block = pl.BlockSpec((rows // steps, columns), lambda step: (step, 0))
    vmem = pl.BlockSpec(memory_space=pltpu.VMEM)
    fixed = (norm, small, moment, weight, gains, gain_first, gain_second)
    shape = lambda item: jax.ShapeDtypeStruct(item.shape, jnp.float32)
    kept = (norm, moment, weight, gains, gain_first, gain_second)
    return pl.pallas_call(
        functools.partial(update_kernel, keyval_width),
        name="update",
        grid=(steps,),
        out_shape=[shape(item) for item in kept + (table, first, second)],
        in_specs=[whole(item) for item in fixed]
        + [vmem]
        + [block] * 3,
        out_specs=[whole(item) for item in kept] + [block] * 3,
        scratch_shapes=[
            pltpu.VMEM(moment.shape, jnp.float32),
            pltpu.VMEM((8, 128), jnp.float32),
        ],
        cost_estimate=pl.CostEstimate(flops=0, bytes_accessed=70_000_000, transcendentals=0),
        compiler_params=pltpu.CompilerParams(vmem_limit_bytes=52 * 2**20),
    )(*fixed, grad, table, first, second)


def other_half(value):
    layer = lax.axis_size("vocab")
    return lax.ppermute(value, "vocab", [(i, (i + layer // MB) % layer) for i in range(layer)])


def on_device(
    token_identifiers,
    targets,
    row_group_index,
    answer_length,
    embedding,
    embedding_first_moment,
    embedding_second_moment,
    output_head_table,
    query_projection,
    keyval_projection,
    output_projection,
    gate_up_projection,
    down_projection,
    gains,
    gain_first_moment,
    gain_second_moment,
    adapter_input_maps,
    input_map_momentum,
    adapter_up_maps,
    up_momentum,
    adapter_keyval_maps,
    keyval_momentum,
):
    seq_count = lax.axis_size("seq")
    layer = lax.axis_size("vocab")
    team = layer // MB
    seq_index = lax.axis_index("seq")
    vocabulary_index = lax.axis_index("vocab")
    batch = vocabulary_index // team
    place = vocabulary_index % team
    other_index = (vocabulary_index + team) % layer
    group_rows = token_identifiers.shape[1]
    half_group = group_rows // 2
    rows = group_rows // team
    table_width = output_head_table.shape[1]
    head_width = query_projection.shape[2]
    heads = head_width // HEAD_SIZE
    hidden = gate_up_projection.shape[2]
    query_width = 4 * head_width

    def move(name, collective, source, *operands, **options):
        return move_tokens(name, collective, team, layer, rows, source, operands, **options)

    def gathered(piece):
        return lax.all_gather(piece, "seq", axis=0, tiled=True)

    keyval_rows = keyval_projection.shape[0] // layer
    keyval_width = KEY_HEADS * HEAD_SIZE
    tokens_all, keyval_piece = start(
        2,
        seq_count,
        token_identifiers.reshape(-1, 128),
        lax.dynamic_slice_in_dim(keyval_projection, vocabulary_index * keyval_rows, keyval_rows, 0),
    )
    keyval_full = layer_rows(3, layer, keyval_piece).reshape(MODEL_WIDTH, 2 * keyval_width)
    near_own = gathered(
        jnp.concatenate(
            [item.reshape(-1, 2 * head_width) for item in (query_projection, output_projection)],
            axis=1,
        )
    )
    feed = gathered(
        jnp.concatenate([gate_up_projection.reshape(-1, 2 * hidden), down_projection], axis=1)
    )
    part_widths = (3 * table_width // 4, table_width // 4)
    part_starts = (0, part_widths[0])

    tokens_flat = tokens_all.reshape(seq_count, MB, team, rows).transpose(1, 2, 0, 3)
    local_ids = tokens_flat.reshape(-1) - vocabulary_index * table_width
    local_ids, keyval_full, near_own = lax.optimization_barrier(
        (local_ids.reshape(layer, -1), keyval_full, near_own)
    )
    near_other = other_half(near_own)
    query_weights = [item[:, : 2 * head_width] for item in (near_own, near_other)]
    out_weights = [item[:, 2 * head_width :] for item in (near_own, near_other)]
    block = (seq_count * rows, MODEL_WIDTH // seq_count)
    residual_in, scale_in, normed_full = move(
        "look_up",
        1,
        from_table,
        local_ids.astype(jnp.float32),
        embedding.astype(jnp.bfloat16),
        reduce="layer",
        middle="forward",
        gain=gains[0:1],
        gather="team",
        column_swap=seq_count,
        extra=(pltpu.VMEM((layer // 2, *block), jnp.bfloat16),),
    )

    (
        normed_full,
        row_group_index,
        adapter_input_maps,
        adapter_up_maps,
        adapter_keyval_maps,
        feed,
    ) = lax.optimization_barrier(
        (
            normed_full,
            row_group_index,
            adapter_input_maps,
            adapter_up_maps,
            adapter_keyval_maps,
            feed,
        )
    )
    gate_own, down_own = feed[:, : 2 * hidden], feed[:, 2 * hidden :]
    gate_weights = (gate_own, other_half(gate_own))
    down_weights = (down_own, other_half(down_own))

    def padded(values, columns=128):
        return jnp.pad(values, ((0, 0), (0, columns - values.shape[1])))

    def of_slices(values, axis):
        return jnp.stack(
            [
                lax.dynamic_slice_in_dim(values, index * head_width, head_width, axis)
                for index in (vocabulary_index, other_index)
            ],
            axis=axis - 1,
        )

    rank = ADAPTER_RANK
    input_map_lowrank = adapter_input_maps.astype(jnp.bfloat16)
    down_qkv = padded(
        jnp.swapaxes(input_map_lowrank[:3], 0, 1).reshape(MODEL_WIDTH, 3 * rank)
    )
    down_out = padded(
        of_slices(
            input_map_lowrank[3].reshape(2, QUERY_HEADS // 2 * HEAD_SIZE, rank), 1
        ).reshape(query_width, rank)
    )
    up_query_map = (
        of_slices(adapter_up_maps[0].reshape(rank, 2, QUERY_HEADS // 2 * HEAD_SIZE), 2)
        .reshape(rank, query_width)
        .astype(jnp.bfloat16)
    )
    keyval_up = adapter_keyval_maps.astype(jnp.bfloat16)
    linear_width = query_width + 2 * keyval_width
    up_maps = jnp.zeros((128, linear_width), jnp.bfloat16)
    up_maps = up_maps.at[:rank, :query_width].set(up_query_map)
    for which in range(2):
        first = query_width + which * keyval_width
        up_maps = up_maps.at[
            (1 + which) * rank : (2 + which) * rank, first : first + keyval_width
        ].set(keyval_up[which])
    up_output_map = padded(ADAPTER_SCALE * adapter_up_maps[1].astype(jnp.bfloat16).T)
    in_weights = jnp.concatenate([*query_weights, keyval_full, down_qkv, down_qkv], axis=1)
    out_weight = jnp.concatenate([*out_weights, up_output_map], axis=1)

    row_of, row_start, length, source_all = layout(row_group_index[batch], seq_count)
    positions = (seq_index - row_start[seq_index]) * group_rows + jnp.arange(group_rows)
    freqs = ROPE_BASE ** (
        -2.0 * jnp.arange(HEAD_SIZE // 2, dtype=jnp.float32) / HEAD_SIZE
    )
    angles = positions.astype(jnp.float32)[:, None] * freqs[None, :]
    cosine = jnp.tile(jnp.cos(angles), (1, 4))
    sine = jnp.sin(angles)
    sine = jnp.concatenate([-sine, sine, -sine, sine], axis=1)

    def weighed(found):
        choice = jnp.zeros((8, 128), jnp.float32)
        return choice.at[:4].set(jnp.stack(found).astype(jnp.float32)[:, None])

    source = source_all[seq_index]
    taken = weighed([source == seq_index + away for away in (-1, 1, 2, 0)])

    def gives(away):
        giver = seq_index + away
        inside = (giver >= 0) & (giver < seq_count)
        return inside & (source_all[jnp.clip(giver, 0, seq_count - 1)] == seq_index)

    given = weighed([gives(away) for away in (1, -1, -2, 0)])
    linear = jnp.dot(normed_full, in_weights, preferred_element_type=jnp.float32)
    queries, keys, values, adapter_result = project(
        13, team, query_width, linear, up_maps, cosine, sine, taken, feed
    )
    attended, log_totals = attend(heads, queries, keys, values, down_out)
    products = (
        pltpu.VMEM((2 * rows, MODEL_WIDTH), jnp.float32),
        pltpu.VMEM((team // 2, rows, MODEL_WIDTH), jnp.bfloat16),
    )
    residual_mid, scale_mid, mid_full = move(
        "sum_attended",
        4,
        from_product,
        attended,
        out_weight,
        extra=products,
        reduce="team",
        added=residual_in,
        gain=gains[1:2],
        middle="forward",
        gather="team",
    )

    last_piece, mid_full = lax.optimization_barrier(
        (output_head_table[:, part_starts[1] :], mid_full)
    )
    head_pieces = (
        gathered(output_head_table[:, : part_starts[1]]),
        gathered(last_piece),
    )

    gate_parts, mixed = [], []
    for gate_weight in gate_weights:
        gate_pre = jnp.dot(mid_full, gate_weight, preferred_element_type=jnp.float32)
        gate_part, up_part = (gate_pre[:, :hidden], gate_pre[:, hidden:])
        mixed.append((gate_part * jax.nn.sigmoid(gate_part) * up_part).astype(jnp.bfloat16))
        gate_parts.append(gate_pre)
    residual_out, scale_out, out_full_rows = move(
        "sum_hidden",
        5,
        from_product,
        mixed[0],
        down_weights[0],
        mixed[1],
        down_weights[1],
        extra=products,
        reduce="team",
        added=residual_mid,
        gain=gains[2:3],
        middle="forward",
        gather="layer",
    )

    (
        out_full_rows,
        answer_length,
        input_map_momentum,
        up_momentum,
        keyval_momentum,
        gain_first_moment,
        gain_second_moment,
        local_ids,
    ) = lax.optimization_barrier(
        (
            out_full_rows,
            answer_length,
            input_map_momentum,
            up_momentum,
            keyval_momentum,
            gain_first_moment,
            gain_second_moment,
            local_ids,
        )
    )

    counted = []
    for each in range(MB):
        row_each, start_each, length_each, _ = layout(row_group_index[each], seq_count)
        places = (seq_index - start_each[seq_index]) * group_rows + jnp.arange(group_rows)
        limit = length_each[seq_index] * group_rows - answer_length[each, row_each[seq_index]]
        counted.append((places >= limit).astype(jnp.float32))
    counted = jnp.concatenate(counted)
    local_targets = targets.reshape(-1) - vocabulary_index * table_width
    target_rows = jnp.broadcast_to(
        local_targets.astype(jnp.float32)[None, :], (8, MB * group_rows)
    )
    logit_parts, stats = [], []
    head_parts = len(head_pieces)
    for first, piece in zip(part_starts, head_pieces):
        logits, each = head_logits(out_full_rows, piece, target_rows, first)
        logit_parts.append(logits)
        stats.append(each[:3])
    stats.append(jnp.zeros((8 - 3 * head_parts, MB * group_rows), jnp.float32))
    stats = spread("gather_stats", 6, layer, jnp.concatenate(stats))
    peaks = jnp.concatenate([stats[:, 3 * part] for part in range(head_parts)])
    sums = jnp.concatenate([stats[:, 3 * part + 1] for part in range(head_parts)])
    picked = sum(jnp.sum(stats[:, 3 * part + 2], axis=0) for part in range(head_parts))
    peak = jnp.max(peaks, axis=0)
    log_total = peak + jnp.log(jnp.sum(sums * jnp.exp(peaks - peak[None, :]), axis=0))
    loss_total_sum = jnp.sum(
        counted * (log_total - picked + Z_WEIGHT * log_total * log_total)
    )
    token_count = jnp.sum(counted)
    row_facts = jnp.stack(
        [
            log_total,
            counted * (1.0 + 2.0 * Z_WEIGHT * log_total),
            counted,
            local_targets.astype(jnp.float32),
        ]
        + [jnp.zeros_like(log_total)] * 4
    )
    tile = min(1024, part_widths[1])
    block = (rows, MODEL_WIDTH)
    pairs = layer // 2
    grad_out_res, gain_grad_out, grad_ffn = move(
        "sum_head_grad",
        7,
        from_logits,
        *logit_parts,
        *head_pieces,
        row_facts,
        any_operands=head_parts,
        vmem_mib=56,
        extra=(
            pltpu.VMEM((2, 2 * rows, tile), jnp.float32),
            pltpu.VMEM((2 * rows, MODEL_WIDTH), jnp.float32),
            pltpu.VMEM((pairs, *block), jnp.bfloat16),
            pltpu.SemaphoreType.DMA((2,)),
        ),
        reduce="layer",
        values=residual_out,
        scale=scale_out,
        gain=gains[2:3],
        middle="backward",
        gather="team",
    )

    grad_mid, gain_grad_mid, branch_grad = move(
        "sum_hidden_grad",
        8,
        from_gates,
        *gate_parts,
        grad_ffn,
        down_weights[0],
        gate_weights[0],
        down_weights[1],
        gate_weights[1],
        any_operands=2,
        extra=products
        + (
            pltpu.VMEM((2, 2 * rows, 2 * hidden), jnp.float32),
            pltpu.SemaphoreType.DMA((2,)),
        ),
        vmem_mib=56,
        reduce="team",
        values=residual_mid,
        scale=scale_mid,
        gain=gains[1:2],
        added=grad_out_res,
        middle="backward",
        gather="team",
    )

    grad_mixed = jnp.dot(branch_grad, out_weight, preferred_element_type=jnp.float32)
    grad_query, grad_keys, grad_values = attend_back(
        heads, queries, keys, values, log_totals, grad_mixed, down_out, cosine, sine
    )
    grads = give_back(
        12, team, grad_query, grad_keys, grad_values, up_maps, cosine, sine, given
    )
    _, gain_grad_in, grad_in = move(
        "sum_in_grad",
        9,
        from_product,
        grads,
        in_weights,
        extra=products,
        reduce="team",
        values=residual_in,
        scale=scale_in,
        gain=gains[0:1],
        added=grad_mid,
        middle="backward",
    )

    over_rows = (((0,), (0,)), ((), ()))
    product = lambda left, right: lax.dot_general(
        left, right, over_rows, preferred_element_type=jnp.float32
    )
    down_qkv_grad = product(grads[:, linear_width:], normed_full)
    down_qkv_grad = down_qkv_grad[: 3 * rank] + down_qkv_grad[128 : 128 + 3 * rank]
    up_grads = ADAPTER_SCALE * product(adapter_result, grads[:, :linear_width])
    up_grads = lax.optimization_barrier(
        [
            up_grads[:rank, :query_width],
            up_grads[rank : 2 * rank, query_width : query_width + keyval_width],
            up_grads[2 * rank : 3 * rank, query_width + keyval_width :],
        ]
    )
    adapter_out_grad = grad_mixed[:, query_width : query_width + rank]
    adapter_out_first = adapter_out_grad.astype(jnp.bfloat16)
    adapter_out_rest = (adapter_out_grad - adapter_out_first.astype(jnp.float32)).astype(
        jnp.bfloat16
    )
    down_out_grad = product(
        jnp.concatenate([adapter_out_first, adapter_out_rest], axis=1), attended[:, :query_width]
    )
    down_out_grad = down_out_grad[:rank] + down_out_grad[rank:]
    up_out_grad = ADAPTER_SCALE * product(
        attended[:, query_width : query_width + rank], branch_grad
    )

    def placed(pieces, shape, axis):
        whole = jnp.zeros(shape, jnp.float32)
        for piece, index in zip(pieces, (vocabulary_index, other_index)):
            start = [0] * len(shape)
            start[axis] = index * head_width
            whole = lax.dynamic_update_slice(whole, piece, start)
        return whole

    out_pieces = down_out_grad.reshape(ADAPTER_RANK, 2, 2, head_width)
    down_out_full = placed(
        [out_pieces[:, 0], out_pieces[:, 1]],
        (ADAPTER_RANK, 2, QUERY_HEADS // 2 * HEAD_SIZE),
        2,
    ).reshape(ADAPTER_RANK, MODEL_WIDTH)
    query_pieces = up_grads[0].reshape(ADAPTER_RANK, 2, 2, head_width)
    up_query_full = placed(
        [query_pieces[:, 0], query_pieces[:, 1]],
        (ADAPTER_RANK, 2, QUERY_HEADS // 2 * HEAD_SIZE),
        2,
    ).reshape(ADAPTER_RANK, MODEL_WIDTH)

    gain_grad = jnp.concatenate([gain_grad_in[:1], gain_grad_mid[:1], gain_grad_out[:1]])
    owner = (vocabulary_index == 0).astype(jnp.float32)
    keyval_grads = jnp.concatenate([up_grads[1], up_grads[2]])
    rank = ADAPTER_RANK
    gain_shape = (2 * rank, 3 * MODEL_WIDTH // (2 * rank))
    loss_rows = jnp.zeros((2 * rank, 128), jnp.float32)
    loss_rows = loss_rows.at[0, 0].set(loss_total_sum * owner).at[0, 1].set(token_count * owner)

    def last_rows(*pieces):
        filled = sum(piece.shape[1] for piece in pieces)
        return jnp.concatenate(
            [*pieces, jnp.zeros((2 * rank, MODEL_WIDTH - filled), jnp.float32)], axis=1
        )

    small = jnp.concatenate(
        [
            down_qkv_grad,
            down_out_full,
            up_query_full,
            up_out_grad,
            last_rows(keyval_grads, gain_grad.reshape(gain_shape), loss_rows),
            jnp.zeros((max(0, 8 * layer - 8 * rank), MODEL_WIDTH), jnp.float32),
        ]
    )

    below = (seq_index - jnp.arange(seq_count)) % seq_count
    ids_by_step = jnp.take(local_ids.reshape(layer, seq_count, rows), below, axis=1).reshape(
        layer, -1
    )
    table_grad, table_squares, small = table_gradient(
        10, seq_count, layer, grad_in, ids_by_step, small, table_width
    )
    loss_at = keyval_width + gain_shape[1]
    loss_pair = small[6 * rank, loss_at : loss_at + 2]

    def stacked(input_maps, up_maps, keyval_maps):
        return jnp.concatenate(
            [
                jnp.swapaxes(input_maps, 1, 2).reshape(4 * rank, MODEL_WIDTH),
                up_maps.reshape(2 * rank, MODEL_WIDTH),
                last_rows(keyval_maps.reshape(2 * rank, keyval_width)),
            ]
        )

    def unstacked(rows):
        return (
            jnp.swapaxes(rows[: 4 * rank].reshape(4, rank, MODEL_WIDTH), 1, 2),
            rows[4 * rank : 6 * rank].reshape(2, rank, MODEL_WIDTH),
            rows[6 * rank :, :keyval_width].reshape(2, rank, keyval_width),
        )

    (
        gradient_norm,
        moments_next,
        weights_next,
        gains_next,
        gain_first_next,
        gain_second_next,
        embedding_next,
        embedding_first_next,
        embedding_second_next,
    ) = update(
        keyval_width,
        table_squares,
        small,
        stacked(input_map_momentum, up_momentum, keyval_momentum),
        stacked(adapter_input_maps, adapter_up_maps, adapter_keyval_maps),
        gains.reshape(gain_shape),
        gain_first_moment.reshape(gain_shape),
        gain_second_moment.reshape(gain_shape),
        table_grad,
        embedding,
        embedding_first_moment,
        embedding_second_moment,
    )
    gradient_norm = gradient_norm[0, 0]
    gains_next, gain_first_next, gain_second_next = (
        item.reshape(3, MODEL_WIDTH) for item in (gains_next, gain_first_next, gain_second_next)
    )
    input_map_momentum_next, up_momentum_next, keyval_momentum_next = unstacked(moments_next)
    adapter_input_next, adapter_up_next, adapter_keyval_next = unstacked(weights_next)
    return (
        loss_pair[0],
        loss_pair[1],
        gradient_norm,
        embedding_first_next,
        embedding_second_next,
        embedding_next,
        gain_first_next,
        gain_second_next,
        gains_next,
        input_map_momentum_next,
        adapter_input_next,
        up_momentum_next,
        adapter_up_next,
        keyval_momentum_next,
        adapter_keyval_next,
    )


def solution(mesh):
    placed = (
        P(None, "seq"),
        P(None, "seq"),
        P(),
        P(),
        P("seq", "vocab"),
        P("seq", "vocab"),
        P("seq", "vocab"),
        P("seq", "vocab"),
        P("seq", None, "vocab"),
        P("seq", None),
        P("seq", None, "vocab"),
        P("seq", None, "vocab"),
        P("seq", "vocab"),
        P(),
        P(),
        P(),
        P(),
        P(),
        P(),
        P(),
        P(),
        P(),
    )
    return jax.shard_map(
        on_device,
        mesh=mesh,
        in_specs=placed,
        out_specs=(
            P(),
            P(),
            P(),
            P("seq", "vocab"),
            P("seq", "vocab"),
            P("seq", "vocab"),
            P(),
            P(),
            P(),
            P(),
            P(),
            P(),
            P(),
            P(),
            P(),
        ),
        check_vma=False,
    )
```

```python
import functools
import math

import jax
import jax.numpy as jnp
from jax import lax
from jax.experimental import pallas as pl
from jax.experimental.pallas import tpu as pltpu
from jax.sharding import PartitionSpec as P

MODEL_WIDTH = 2048
QUERY_HEADS = 32
KEY_HEADS = 4
HEAD_SIZE = 64
ADAPTER_RANK = 8
MB = 2
STEP = 10


ADAPTER_SCALE = 2.0
NORM_EPS = 1e-05
Z_WEIGHT = 0.0001
CLIP_NORM = 1.0
ROPE_BASE = 10000.0
MASKED = -1e30
MUON_MOMENTUM = 0.95
MUON_RATE = 0.1
ADAM_RATE = 0.3
BETA_FIRST = 0.9
BETA_SECOND = 0.999
ADAM_EPS = 1e-08
DECAY_RATE = 0.01
SCHULZ = (3.4445, -4.775, 2.0315)
PRECISE = lax.Precision.HIGHEST
MESH = pl.DeviceIdType.MESH


def flip(index, mask):
    result = index
    bit = 1
    while bit <= mask:
        if mask & bit:
            result = result + bit * (1 - 2 * lax.rem(lax.div(index, jnp.int32(bit)), jnp.int32(2)))
        bit *= 2
    return result


def against(left, right):
    return lax.dot_general(
        left, right, (((1,), (1,)), ((), ())), preferred_element_type=jnp.float32
    )


class Links:
    def __init__(self, sent, got):
        self.sent, self.got, self.started = sent, got, []
        self.seq_index = lax.axis_index("seq")
        self.me = lax.axis_index("vocab")

    def layer_peer(self, mask):
        return (self.seq_index, flip(self.me, mask))

    def column_peer(self, step):
        count = jnp.int32(lax.axis_size("seq"))
        return (lax.rem(self.seq_index + step, count), self.me)

    def meet(self, peers):
        barrier = pltpu.get_barrier_semaphore()
        for peer in peers:
            pl.semaphore_signal(barrier, inc=1, device_id=peer, device_id_type=MESH)
        pl.semaphore_wait(barrier, len(peers))

    def send(self, source, target, peer):
        at = len(self.started)
        copy = pltpu.make_async_remote_copy(
            src_ref=source,
            dst_ref=target,
            send_sem=self.sent.at[at],
            recv_sem=self.got.at[at],
            device_id=peer,
            device_id_type=MESH,
        )
        copy.start()
        self.started.append(copy)
        return copy

    def along(self, source, target, steps):
        count = jnp.int32(lax.axis_size("seq"))
        waits = []
        for at, step in enumerate(steps):
            place = len(self.started)
            copy = pltpu.make_async_remote_copy(
                src_ref=source,
                dst_ref=target.at[at],
                send_sem=self.sent.at[place],
                recv_sem=self.got.at[place],
                device_id=self.column_peer(step % lax.axis_size("seq")),
                device_id_type=MESH,
            )
            there = self.seq_index + step
            giver = self.seq_index - step
            to_send = (there >= 0) & (there < count)
            to_take = (giver >= 0) & (giver < count)
            pl.when(to_send)(copy.start)
            self.started.append((to_send, copy))
            waits.append(functools.partial(pl.when(to_take), copy.wait_recv))
        return waits

    def finish(self):
        for copy in self.started:
            if isinstance(copy, tuple):
                pl.when(copy[0])(copy[1].wait_send)
            else:
                copy.wait_send()


def group_masks(size):
    if size == 8:
        return [2, 4], True
    return list(range(2, size, 2)), False


def sum_blocks(links, size, produce, near_in, far_out, far_in, side_in, mine):
    masks, routed = group_masks(size)
    half = mine.shape[0] // 2
    sides, fars = [], []
    for step, mask in enumerate(([6] if routed else []) + masks + [0]):
        source = produce(step, mask)
        near = links.send(source, near_in.at[step], links.layer_peer(1))
        near.wait_recv()
        if routed and mask == 6:
            far_out[step] = (mine[...] + near_in[step].astype(jnp.float32)).astype(jnp.bfloat16)
            for at, over in enumerate(masks):
                sides.append(
                    links.send(
                        far_out.at[step, pl.ds(at * half, half)],
                        side_in.at[at],
                        links.layer_peer(over),
                    )
                )
        elif mask:
            both = mine[...] + near_in[step].astype(jnp.float32)
            if routed:
                mine[...] = both
                at = 1 if mask == 2 else 0
                sides[at].wait_recv()
                rows = pl.ds(at * half, half)
                mine[rows, :] = mine[rows, :] + side_in[at].astype(jnp.float32)
                both = mine[...]
            far_out[step] = both.astype(jnp.bfloat16)
            fars.append(
                links.send(far_out.at[step], far_in.at[len(fars)], links.layer_peer(mask))
            )
        else:
            mine[...] = mine[...] + near_in[step].astype(jnp.float32)
    for at, copy in enumerate(fars):
        copy.wait_recv()
        mine[...] = mine[...] + far_in[at].astype(jnp.float32)


def gather_blocks(links, size, block, write, parts=2):
    masks, routed = group_masks(size)
    out, on, over = {}, {}, {}
    for part in range(parts):
        write(part)
        for mask in [1] + masks:
            out[mask, part] = links.send(
                block(0, part), block(0, part), links.layer_peer(mask)
            )
    for part in range(parts):
        for at, mask in enumerate(masks):
            out[mask, part].wait_recv()
            if routed and part == at:
                over[part] = links.send(
                    block(mask, part), block(mask, part), links.layer_peer(masks[1 - at])
                )
            on[mask, part] = links.send(
                block(mask, part), block(mask, part), links.layer_peer(1)
            )
    for part, copy in over.items():
        copy.wait_recv()
        on[6, part] = links.send(block(6, part), block(6, part), links.layer_peer(1))
    for part in range(parts):
        out[1, part].wait_recv()
    for copy in on.values():
        copy.wait_recv()


def token_kernel(settings, *refs):
    team, layer, reduce, middle, added, gather, source, column_swap = settings
    refs = list(refs)
    take = lambda: refs.pop(0)
    source_refs = [take() for _ in range(source[1])]
    added_ref = take() if added else None
    values_ref, scale_in = (take(), take()) if middle == "backward" else (None, None)
    gain_ref = take()
    new_ref = take()
    scale_ref = take() if middle == "forward" else None
    gain_grad_ref = take() if middle == "backward" else None
    last_ref = take()
    near_in, far_out, far_in, side_in, mine, sent, got = [take() for _ in range(7)]
    links = Links(sent, got)
    size = layer if reduce == "layer" else team
    spread = layer if gather == "layer" else team
    masks = set(range(2, max(size, spread) if gather else size, 2)) | {1}
    if max(size, spread if gather else 0) == 8:
        masks -= {6}
    seq_count = lax.axis_size("seq")
    column = list(range(1, seq_count)) if column_swap else []
    links.meet(
        [links.layer_peer(mask) for mask in sorted(masks)]
        + [links.column_peer(step) for step in column]
    )
    sum_blocks(
        links, size, source[0](links, size, mine, source_refs, refs), near_in, far_out, far_in, side_in, mine
    )
    rows = new_ref.shape[0]
    if column_swap:
        narrow, wide = refs[:2]
        width = mine.shape[1]
        narrow[...] = mine[...].astype(jnp.bfloat16)
        here = pl.ds(pl.multiple_of(links.seq_index * width, 128), width)
        rows_of = lambda index: pl.ds(pl.multiple_of(index * rows, 16), rows)
        swaps = [
            links.send(narrow.at[rows_of(peer[0])], wide.at[:, here], peer)
            for peer in [links.column_peer(step) for step in column]
        ]
        wide[:, here] = narrow[rows_of(links.seq_index), :]
        for copy in swaps:
            copy.wait_recv()
    parts = 2
    count = rows // parts

    few = 16

    def write(part):
        start = last_rows(0, part)

        def some_rows(at, pulls):
            first = pl.multiple_of(part * count + at * few, few)
            spot = pl.ds(first, few)
            if column_swap:
                total = wide[spot, :].astype(jnp.float32)
            else:
                total = mine[spot, :]
            if middle == "forward":
                fresh = total + added_ref[spot, :] if added else total
                new_ref[spot, :] = fresh
                mean = jnp.sum(fresh * fresh, axis=1, keepdims=True) / MODEL_WIDTH
                scale = lax.rsqrt(mean + NORM_EPS)
                scale_ref[spot, :] = jnp.broadcast_to(scale, (few, 128))
                payload = fresh * scale * gain_ref[...]
            else:
                values = values_ref[spot, :]
                scale = scale_in[spot, :1]
                weighted = total * gain_ref[...]
                dots = jnp.sum(values * weighted, axis=1, keepdims=True)
                payload = scale * weighted - values * (scale * scale * scale * dots / MODEL_WIDTH)
                pull = total * values * scale
                pulls = pulls + pull[:8] + pull[8:]
                if added:
                    payload = payload + added_ref[spot, :]
                new_ref[spot, :] = payload
            if gather:
                here = pl.ds(pl.multiple_of(start + at * few, few), few)
                last_ref[here, :] = payload.astype(jnp.bfloat16)
            return pulls

        nothing = jnp.zeros((8, MODEL_WIDTH), jnp.float32) if middle == "backward" else 0
        pulls = lax.fori_loop(0, count // few, some_rows, nothing)
        if middle == "backward":
            pull = jnp.broadcast_to(jnp.sum(pulls, axis=0, keepdims=True), gain_grad_ref.shape)
            gain_grad_ref[...] = pull if part == 0 else gain_grad_ref[...] + pull
        if not gather:
            spot = pl.ds(part * count, count)
            last_ref[:, spot] = new_ref[spot, :].T.astype(jnp.bfloat16)

    def last_rows(mask, part):
        owner = flip(links.me, mask)
        if gather == "team":
            owner = lax.rem(owner, jnp.int32(team))
        return pl.multiple_of(owner * rows + part * count, 16)

    def block_rows(mask, part):
        return pl.ds(last_rows(mask, part), count)

    if gather:
        gather_blocks(
            links, spread, lambda mask, part: last_ref.at[block_rows(mask, part)], write, parts
        )
    else:
        for part in range(parts):
            write(part)
    links.finish()


def by_pairs(links, size, mine, near_out, total, work):
    rows = mine.shape[0]

    def produce(step, mask):
        owner = lax.rem(flip(links.me, mask), jnp.int32(size))
        work(step, mask, pl.multiple_of(lax.div(owner, jnp.int32(2)) * 2 * rows, 128))
        own = lax.rem(links.me, jnp.int32(2))
        mine[...] = total[pl.ds(pl.multiple_of(own * rows, 16), rows), :]
        near_out[step] = total[pl.ds(pl.multiple_of((1 - own) * rows, 16), rows), :].astype(
            jnp.bfloat16
        )
        return near_out.at[step]

    return produce


def add_product(total, left, right_ref, first):
    width = total.shape[1] // 2
    for start in (0, width):
        spot = slice(start, start + width)
        part = against(left, right_ref[spot, :])
        total[:, spot] = part if first else total[:, spot] + part


def from_product(links, size, mine, source_refs, scratch):
    total, near_out = scratch

    def work(step, mask, first):
        rows = pl.ds(first, total.shape[0])
        for at, (left, right) in enumerate(zip(source_refs[::2], source_refs[1::2])):
            add_product(total, left[rows, :], right, at == 0)

    return by_pairs(links, size, mine, near_out, total, work)


def from_gates(links, size, mine, source_refs, scratch):
    total, near_out, gates, gate_sem = scratch
    grad_ref = source_refs[2]

    def work(step, mask, first):
        rows = pl.ds(first, total.shape[0])
        copies = [
            pltpu.make_async_copy(source_refs[at].at[rows], gates.at[at], gate_sem.at[at])
            for at in range(2)
        ]
        for copy in copies:
            copy.start()
        grads = grad_ref[rows, :]
        for at in range(2):
            down_ref, weight_ref = source_refs[3 + 2 * at : 5 + 2 * at]
            hidden = down_ref.shape[1]
            grad_hidden = jnp.dot(grads, down_ref[...], preferred_element_type=jnp.float32)
            copies[at].wait()
            gate, up = gates[at, :, :hidden], gates[at, :, hidden:]
            sigmoid = jax.nn.sigmoid(gate)
            grad_gate = grad_hidden * up * sigmoid * (1.0 + gate * (1.0 - sigmoid))
            grad_up = grad_hidden * gate * sigmoid
            both = jnp.concatenate([grad_gate, grad_up], axis=1).astype(jnp.bfloat16)
            add_product(total, both, weight_ref, at == 0)

    return by_pairs(links, size, mine, near_out, total, work)


def from_table(links, size, mine, source_refs, scratch):
    ids_ref, table_ref = source_refs
    near_out = scratch[2]
    tokens = mine.shape[0]
    count = min(512, tokens)
    depth = min(2048, table_ref.shape[1])

    def block(mask, store):
        owner = flip(links.me, mask)

        def one(at, _):
            first = pl.multiple_of(at * count, count)
            spot = pl.ds(first, count)
            ids = jnp.broadcast_to(ids_ref[pl.ds(owner, 1), spot], (8, count)).T[:, :1]
            ids = ids.astype(jnp.int32)
            found = None
            for start in range(0, table_ref.shape[1], depth):
                names = lax.broadcasted_iota(jnp.int32, (count, depth), 1) + start
                chosen = jnp.where(names == ids, 1.0, 0.0).astype(jnp.bfloat16)
                part = against(chosen, table_ref[:, start : start + depth])
                found = part if found is None else found + part
            store(spot, found)
            return 0

        lax.fori_loop(0, tokens // count, one, 0)

    def produce(step, mask):
        def keep_near(spot, found):
            near_out[step, spot, :] = found.astype(jnp.bfloat16)

        def keep_mine(spot, found):
            mine[spot, :] = found

        block(mask ^ 1, keep_near)
        block(mask, keep_mine)
        return near_out.at[step]

    return produce


def from_logits(links, size, mine, source_refs, scratch):
    parts = (len(source_refs) - 1) // 2
    logit_refs, head_refs, row_ref = source_refs[:parts], source_refs[parts:-1], source_refs[-1]
    tiles, total, near_out, tile_sem = scratch
    rows = mine.shape[0]
    width = tiles.shape[2]
    pieces = [
        (part, at) for part in range(parts) for at in range(logit_refs[part].shape[1] // width)
    ]
    order = ([6] if size == 8 else []) + group_masks(size)[0] + [0]
    work_list = [(mask, part, at) for mask in order for part, at in pieces]

    def pair_rows(mask):
        first = lax.div(flip(links.me, mask), jnp.int32(2)) * 2 * rows
        return pl.ds(pl.multiple_of(first, 128), 2 * rows)

    def fetch(index):
        mask, part, at = work_list[index]
        return pltpu.make_async_copy(
            logit_refs[part].at[pair_rows(mask), pl.ds(at * width, width)],
            tiles.at[index % 2],
            tile_sem.at[index % 2],
        )

    def work(step, mask, first_row):
        if step == 0:
            fetch(0).start()
        columns = row_ref[:, pl.ds(first_row, 2 * rows)].T
        log_total, factor, counted = columns[:, 0:1], columns[:, 1:2], columns[:, 2:3]
        wanted = columns[:, 3:4].astype(jnp.int32)
        for place, (part, at) in enumerate(pieces):
            index = step * len(pieces) + place
            if index + 1 < len(work_list):
                fetch(index + 1).start()
            fetch(index).wait()
            step_width = min(1024, width)

            def one(turn, _, part=part, at=at, index=index, place=place):
                first = pl.multiple_of(turn * step_width, step_width)
                spot = pl.ds(first, step_width)
                logits = tiles[index % 2, :, spot]
                names = lax.broadcasted_iota(jnp.int32, logits.shape, 1) + (
                    first + at * width + sum(ref.shape[1] for ref in logit_refs[:part])
                )
                grads = factor * jnp.exp(logits - log_total) - jnp.where(
                    names == wanted, counted, 0.0
                )
                weights = head_refs[part][
                    :, pl.ds(pl.multiple_of(first + at * width, step_width), step_width)
                ]
                total[...] += against(grads.astype(jnp.bfloat16), weights)
                return 0

            if place == 0:
                total[...] = jnp.zeros_like(total)
            lax.fori_loop(0, width // step_width, one, 0)

    return by_pairs(links, size, mine, near_out, total, work)


def move_tokens(
    name, collective, team, layer, rows, source, operands, *, reduce, middle, gain,
    added=None, values=None, scale=None, gather=None, column_swap=0, extra=(), any_operands=0, vmem_mib=44, us=1
):
    vmem = pl.BlockSpec(memory_space=pltpu.VMEM)
    rest = [item for item in (added, values, scale, gain) if item is not None]
    wide = jax.ShapeDtypeStruct((rows, MODEL_WIDTH), jnp.float32)
    results = [wide]
    if middle == "forward":
        results.append(jax.ShapeDtypeStruct((rows, 128), jnp.float32))
    else:
        results.append(jax.ShapeDtypeStruct((8, MODEL_WIDTH), jnp.float32))
    tall = {None: None, "team": team * rows, "layer": layer * rows}[gather]
    results.append(
        jax.ShapeDtypeStruct((tall, MODEL_WIDTH) if gather else (MODEL_WIDTH, rows), jnp.bfloat16)
    )
    size = layer if reduce == "layer" else team
    seq_count = column_swap or 1
    block = (rows * seq_count, MODEL_WIDTH // seq_count)
    masks, routed = group_masks(size)
    steps = len(masks) + 1 + routed
    copies = steps + len(masks) + 2 * routed + (seq_count - 1)
    if gather:
        masks_out, routed_out = group_masks(layer if gather == "layer" else team)
        copies += 2 * (1 + 2 * len(masks_out)) + 4 * routed_out
    scratch = [
        pltpu.VMEM((steps, *block), jnp.bfloat16),
        pltpu.VMEM((max(steps - 1, 1), *block), jnp.bfloat16),
        pltpu.VMEM((len(masks), *block), jnp.bfloat16),
        pltpu.VMEM((2, block[0] // 2, block[1]) if routed else (2, 16, 128), jnp.bfloat16),
        pltpu.VMEM(block, jnp.float32),
        pltpu.SemaphoreType.DMA((copies,)),
        pltpu.SemaphoreType.DMA((copies,)),
    ]
    if column_swap:
        scratch += [
            pltpu.VMEM(block, jnp.bfloat16),
            pltpu.VMEM((rows, MODEL_WIDTH), jnp.bfloat16),
        ]
    scratch += list(extra)
    settings = (
        team, layer, reduce, middle, added is not None, gather, (source, len(operands)), column_swap
    )
    return pl.pallas_call(
        functools.partial(token_kernel, settings),
        name=name,
        out_shape=results,
        in_specs=[pl.BlockSpec(memory_space=pl.ANY)] * any_operands
        + [vmem] * (len(operands) + len(rest) - any_operands),
        out_specs=[vmem] * len(results),
        scratch_shapes=scratch,
        cost_estimate=pl.CostEstimate(
            flops=0, bytes_accessed=us * 3_700_000, transcendentals=0
        ),
        compiler_params=pltpu.CompilerParams(
            collective_id=collective, has_side_effects=True, vmem_limit_bytes=vmem_mib * 2**20
        ),
    )(*operands, *rest)


def spread_kernel(layer, item_ref, all_ref, sent, got):
    links = Links(sent, got)
    peers = [links.layer_peer(mask) for mask in range(1, layer)]
    links.meet(peers)
    all_ref[links.me] = item_ref[...]
    copies = [links.send(item_ref, all_ref.at[links.me], peer) for peer in peers]
    for copy in copies:
        copy.wait_recv()
    links.finish()


def spread(name, collective, layer, item):
    vmem = pl.BlockSpec(memory_space=pltpu.VMEM)
    return pl.pallas_call(
        functools.partial(spread_kernel, layer),
        name=name,
        out_shape=jax.ShapeDtypeStruct((layer, *item.shape), item.dtype),
        in_specs=[vmem],
        out_specs=vmem,
        scratch_shapes=[pltpu.SemaphoreType.DMA((layer - 1,))] * 2,
        cost_estimate=pl.CostEstimate(flops=0, bytes_accessed=3_700_000, transcendentals=0),
        compiler_params=pltpu.CompilerParams(collective_id=collective, has_side_effects=True),
    )(item)


def spread_lanes(values, head, heads):
    if heads == 1:
        return values
    zeros = jnp.zeros_like(values)
    return jnp.concatenate([values if index == head else zeros for index in range(heads)], axis=1)


def turned(values, cosine, sine):
    pieces = []
    for first in range(0, values.shape[1], 128):
        piece = values[:, first : first + 128]
        lane = lax.broadcasted_iota(jnp.int32, piece.shape, 1)
        partner = jnp.where(
            lax.rem(lane, jnp.int32(HEAD_SIZE)) < HEAD_SIZE // 2,
            pltpu.roll(piece, 128 - HEAD_SIZE // 2, 1),
            pltpu.roll(piece, HEAD_SIZE // 2, 1),
        )
        pieces.append(piece * cosine + partner * sine)
    return jnp.concatenate(pieces, axis=1)


def head_columns(values, head):
    return values[:, head * HEAD_SIZE : (head + 1) * HEAD_SIZE]


def of_batch(batch, values, first, second):
    return jnp.where(batch == 0, head_columns(values, first), head_columns(values, second))


UNIT_HEADS = ((0, 1), (2, 3), (1, 0), (3, 2))


def project_kernel(
    team, query_width, linear_ref, up_ref, cosine_ref, sine_ref, choice_ref, ready_ref,
    query_ref, key_ref, value_ref, low_ref, tail, borrowed, arrived, sent, got,
):
    links = Links(sent, got)
    seq_count = lax.axis_size("seq")
    arrived[...] = jnp.zeros_like(arrived)
    team_peers = [links.layer_peer(mask) for mask in range(1, team)]
    steps = sorted({1, 2, seq_count - 1, seq_count - 2})
    links.meet(team_peers + [links.column_peer(step) for step in steps])
    batch = lax.div(links.me, jnp.int32(team))
    group_rows = query_ref.shape[0]
    half = group_rows // 2
    chunk = half // 2
    kv_width = KEY_HEADS * HEAD_SIZE

    def rows_of(at, _):
        first = pl.multiple_of(at * chunk, chunk)
        rows = pl.ds(first, chunk)
        low = linear_ref[rows, query_width + 2 * kv_width : query_width + 2 * kv_width + 128]
        low = low.astype(jnp.bfloat16)
        low_ref[rows, :] = low
        linear = linear_ref[rows, : query_width + 2 * kv_width] + ADAPTER_SCALE * jnp.dot(
            low, up_ref[...], preferred_element_type=jnp.float32
        )
        cosine, sine = cosine_ref[rows, :], sine_ref[rows, :]
        query_ref[rows, :] = turned(linear[:, :query_width], cosine, sine).astype(jnp.bfloat16)
        keys = turned(linear[:, query_width : query_width + kv_width], cosine, sine)
        keys = keys.astype(jnp.bfloat16)
        values = linear[:, query_width + kv_width :].astype(jnp.bfloat16)
        later = pl.ds(pl.multiple_of(half + first, chunk), chunk)
        for unit, pair in enumerate(UNIT_HEADS):
            key_ref[unit, later, :] = of_batch(batch, keys, *pair)
            value_ref[unit, later, :] = of_batch(batch, values, *pair)

        @pl.when(at >= 2)
        def _():
            spot = pl.ds(pl.multiple_of(first - half, chunk), chunk)
            tail[spot, :] = jnp.concatenate(
                [keys[:, kv_width // 2 :], values[:, kv_width // 2 :]], axis=1
            )

        return 0

    lax.fori_loop(0, 2, lambda at, _: rows_of(at + 2, 0), 0)
    count = half // team
    mine = pl.ds(pl.multiple_of(lax.rem(links.me, jnp.int32(team)) * count, 16), count)
    copies = links.along(tail.at[mine], arrived, (1, -1, -2))
    lax.fori_loop(0, 2, rows_of, 0)
    for wait in copies:
        wait()
    chosen = tail[mine, :].astype(jnp.float32) * choice_ref[3:4, :1]
    for at in range(3):
        chosen = chosen + arrived[at].astype(jnp.float32) * choice_ref[at : at + 1, :1]
    borrowed[mine, :] = chosen.astype(jnp.bfloat16)
    copies = [links.send(borrowed.at[mine], borrowed.at[mine], peer) for peer in team_peers]
    for copy in copies:
        copy.wait_recv()
    before = borrowed[...]
    for unit, (first, second) in enumerate(UNIT_HEADS):
        if unit % 2:
            key_ref[unit, :half, :] = of_batch(batch, before, first - 2, second - 2)
            value_ref[unit, :half, :] = of_batch(batch, before, first, second)
        else:
            key_ref[unit, :half, :] = jnp.zeros((half, HEAD_SIZE), jnp.bfloat16)
            value_ref[unit, :half, :] = jnp.zeros((half, HEAD_SIZE), jnp.bfloat16)
    links.finish()


def project(collective, team, query_width, linear, up, cosine, sine, choice, ready):
    vmem = pl.BlockSpec(memory_space=pltpu.VMEM)
    group_rows = linear.shape[0]
    half, width = group_rows // 2, KEY_HEADS * HEAD_SIZE
    copies = 3 + team - 1
    units = jax.ShapeDtypeStruct((4, half + group_rows, HEAD_SIZE), jnp.bfloat16)
    return pl.pallas_call(
        functools.partial(project_kernel, team, query_width),
        name="project",
        out_shape=[
            jax.ShapeDtypeStruct((group_rows, query_width), jnp.bfloat16),
            units,
            units,
            jax.ShapeDtypeStruct((group_rows, 128), jnp.bfloat16),
        ],
        in_specs=[vmem] * 5 + [pl.BlockSpec(memory_space=pl.ANY)],
        out_specs=[vmem] * 4,
        scratch_shapes=[
            pltpu.VMEM((half, width), jnp.bfloat16),
            pltpu.VMEM((half, width), jnp.bfloat16),
            pltpu.VMEM((3, half // team, width), jnp.bfloat16),
            pltpu.SemaphoreType.DMA((copies,)),
            pltpu.SemaphoreType.DMA((copies,)),
        ],
        cost_estimate=pl.CostEstimate(flops=0, bytes_accessed=3_700_000, transcendentals=0),
        compiler_params=pltpu.CompilerParams(
            collective_id=collective, has_side_effects=True, vmem_limit_bytes=40 * 2**20
        ),
    )(linear, up, cosine, sine, choice, ready)


def unit_halves(unit, half):
    if unit % 2:
        return ((0, (0, half)), (half, (2 * half,)))
    return ((half, (half, 2 * half)), (0, (half,)))


def block_scores(queries, keys, causal):
    scores = against(queries, keys) * HEAD_SIZE ** (-0.5)
    if causal:
        seen = lax.broadcasted_iota(jnp.int32, scores.shape, 1) <= lax.broadcasted_iota(
            jnp.int32, scores.shape, 0
        )
        scores = jnp.where(seen, scores, MASKED)
    return scores


def attend_kernel(heads, query_ref, key_ref, value_ref, down_ref, out_ref, log_ref):
    head_width = heads * HEAD_SIZE
    half = query_ref.shape[0] // 2
    for unit in range(4):
        lanes = slice(unit * head_width, (unit + 1) * head_width)
        for first_row, blocks in unit_halves(unit, half):
            rows = slice(first_row, first_row + half)
            queries = query_ref[rows, lanes]
            result = None
            for head in range(heads):
                scores = [
                    block_scores(
                        queries,
                        spread_lanes(key_ref[unit, start : start + half, :], head, heads),
                        index == len(blocks) - 1,
                    )
                    for index, start in enumerate(blocks)
                ]
                peak = functools.reduce(
                    jnp.maximum, [jnp.max(item, axis=1, keepdims=True) for item in scores]
                )
                terms = [jnp.exp(item - peak) for item in scores]
                summed = sum(jnp.sum(item, axis=1, keepdims=True) for item in terms)
                share = 1.0 / summed
                for item, start in zip(terms, blocks):
                    part = jnp.dot(
                        (item * share).astype(jnp.bfloat16),
                        spread_lanes(value_ref[unit, start : start + half, :], head, heads),
                        preferred_element_type=jnp.float32,
                    )
                    result = part if result is None else result + part
                log_ref[unit, rows, head : head + 1] = peak + jnp.log(summed)
            out_ref[rows, lanes] = result.astype(jnp.bfloat16)
    out_ref[:, 4 * head_width :] = jnp.dot(
        out_ref[:, : 4 * head_width], down_ref[...], preferred_element_type=jnp.float32
    ).astype(jnp.bfloat16)


def attend(heads, queries, keys, values, down):
    vmem = pl.BlockSpec(memory_space=pltpu.VMEM)
    group_rows, query_width = queries.shape
    return pl.pallas_call(
        functools.partial(attend_kernel, heads),
        name="attend",
        out_shape=[
            jax.ShapeDtypeStruct((group_rows, query_width + 128), jnp.bfloat16),
            jax.ShapeDtypeStruct((4, group_rows, heads), jnp.float32),
        ],
        in_specs=[vmem] * 4,
        out_specs=[vmem] * 2,
        cost_estimate=pl.CostEstimate(flops=0, bytes_accessed=3_700_000, transcendentals=0),
        compiler_params=pltpu.CompilerParams(vmem_limit_bytes=48 * 2**20),
    )(queries, keys, values, down)


def attend_back_kernel(
    heads, query_ref, key_ref, value_ref, log_ref, grad_ref, down_ref, cosine_ref, sine_ref,
    grad_query_ref, grad_key_ref, grad_value_ref, wide,
):
    head_width = heads * HEAD_SIZE
    query_width = 4 * head_width
    half = query_ref.shape[0] // 2
    grad_key_ref[...] = jnp.zeros_like(grad_key_ref)
    grad_value_ref[...] = jnp.zeros_like(grad_value_ref)
    scale = HEAD_SIZE ** (-0.5)
    over_rows = (((0,), (0,)), ((), ()))
    for unit in range(4):
        lanes = slice(unit * head_width, (unit + 1) * head_width)
        for first_row, blocks in unit_halves(unit, half):
            rows = slice(first_row, first_row + half)
            queries = query_ref[rows, lanes]
            low = grad_ref[rows, query_width:]
            low_first = low.astype(jnp.bfloat16)
            low_rest = (low - low_first.astype(jnp.float32)).astype(jnp.bfloat16)
            grads = grad_ref[rows, lanes] + against(low_first, down_ref[lanes, :])
            grads = (grads + against(low_rest, down_ref[lanes, :])).astype(jnp.bfloat16)
            grad_query = None
            for head in range(heads):
                own = slice(head * HEAD_SIZE, (head + 1) * HEAD_SIZE)
                keys = [
                    spread_lanes(key_ref[unit, start : start + half, :], head, heads)
                    for start in blocks
                ]
                probs, pulls = [], []
                for index, start in enumerate(blocks):
                    scores = block_scores(queries, keys[index], index == len(blocks) - 1)
                    probs.append(jnp.exp(scores - log_ref[unit, rows, head : head + 1]))
                    values = spread_lanes(value_ref[unit, start : start + half, :], head, heads)
                    pulls.append(against(grads, values))
                inner = sum(
                    jnp.sum(prob * pull, axis=1, keepdims=True)
                    for prob, pull in zip(probs, pulls)
                )
                for prob, pull, key, start in zip(probs, pulls, keys, blocks):
                    grad_scores = (prob * (pull - inner)).astype(jnp.bfloat16)
                    part = jnp.dot(grad_scores, key, preferred_element_type=jnp.float32)
                    grad_query = part if grad_query is None else grad_query + part
                    grad_key = lax.dot_general(
                        grad_scores, queries, over_rows, preferred_element_type=jnp.float32
                    )
                    grad_value = lax.dot_general(
                        prob.astype(jnp.bfloat16),
                        grads,
                        over_rows,
                        preferred_element_type=jnp.float32,
                    )
                    spot = slice(start, start + half)
                    grad_key_ref[unit, spot, :] += grad_key[:, own] * scale
                    grad_value_ref[unit, spot, :] += grad_value[:, own]
            wide[rows, lanes] = grad_query * scale
    grad_query_ref[...] = turned(wide[...], cosine_ref[...], -sine_ref[...]).astype(jnp.bfloat16)


def attend_back(heads, queries, keys, values, log_totals, grads, down, cosine, sine):
    vmem = pl.BlockSpec(memory_space=pltpu.VMEM)
    units = jax.ShapeDtypeStruct(keys.shape, jnp.float32)
    return pl.pallas_call(
        functools.partial(attend_back_kernel, heads),
        name="attend_back",
        out_shape=[jax.ShapeDtypeStruct(queries.shape, jnp.bfloat16), units, units],
        in_specs=[vmem] * 8,
        out_specs=[vmem] * 3,
        scratch_shapes=[pltpu.VMEM(queries.shape, jnp.float32)],
        cost_estimate=pl.CostEstimate(flops=0, bytes_accessed=3_700_000, transcendentals=0),
        compiler_params=pltpu.CompilerParams(vmem_limit_bytes=52 * 2**20),
    )(queries, keys, values, log_totals, grads, down, cosine, sine)


def give_back_kernel(
    team, query_ref, key_ref, value_ref, up_ref, cosine_ref, sine_ref, choice_ref, out_ref,
    tail, arrived, sent, got,
):
    links = Links(sent, got)
    seq_count = lax.axis_size("seq")
    steps = sorted({1, 2, seq_count - 1, seq_count - 2})
    arrived[...] = jnp.zeros_like(arrived)
    links.meet([links.column_peer(step) for step in steps])
    batch = lax.div(links.me, jnp.int32(team))
    group_rows, query_width = query_ref.shape
    half = group_rows // 2
    kv_width = KEY_HEADS * HEAD_SIZE

    def natural(ref, rows, heads):
        units = {0: (0, 2), 1: (2, 0), 2: (1, 3), 3: (3, 1)}
        return jnp.concatenate(
            [
                jnp.where(batch == 0, ref[units[head][0], rows, :], ref[units[head][1], rows, :])
                for head in heads
            ],
            axis=1,
        )

    before = slice(0, half)
    own = jnp.concatenate(
        [natural(key_ref, before, (2, 3)), natural(value_ref, before, (2, 3))], axis=1
    )
    tail[...] = own.astype(jnp.bfloat16)
    copies = links.along(tail, arrived, (-1, 1, 2))
    middle, last = slice(half, 2 * half), slice(2 * half, 3 * half)

    def write(first, keys, values):
        rows = slice(first, first + half)
        cosine, sine = cosine_ref[rows, :], sine_ref[rows, :]
        out_ref[rows, :query_width] = query_ref[rows, :]
        out_ref[rows, query_width : query_width + kv_width] = turned(keys, cosine, -sine).astype(
            jnp.bfloat16
        )
        out_ref[rows, query_width + kv_width : query_width + 2 * kv_width] = values.astype(
            jnp.bfloat16
        )
        low = ADAPTER_SCALE * against(out_ref[rows, : query_width + 2 * kv_width], up_ref[...])
        first_part = low.astype(jnp.bfloat16)
        out_ref[rows, query_width + 2 * kv_width : query_width + 2 * kv_width + 128] = first_part
        out_ref[rows, query_width + 2 * kv_width + 128 :] = (
            low - first_part.astype(jnp.float32)
        ).astype(jnp.bfloat16)

    every = (0, 1, 2, 3)
    write(0, natural(key_ref, middle, every), natural(value_ref, middle, every))
    back = own * choice_ref[3:4, :1]
    for at, wait in enumerate(copies):
        wait()
        back = back + arrived[at].astype(jnp.float32) * choice_ref[at : at + 1, :1]
    keys, values = natural(key_ref, last, every), natural(value_ref, last, every)
    small = kv_width // 2
    keys = jnp.concatenate([keys[:, :small], keys[:, small:] + back[:, :small]], axis=1)
    values = jnp.concatenate([values[:, :small], values[:, small:] + back[:, small:]], axis=1)
    write(half, keys, values)
    links.finish()


def give_back(collective, team, grad_query, grad_key, grad_value, up, cosine, sine, choice):
    vmem = pl.BlockSpec(memory_space=pltpu.VMEM)
    group_rows, query_width = grad_query.shape
    half, width = group_rows // 2, KEY_HEADS * HEAD_SIZE
    return pl.pallas_call(
        functools.partial(give_back_kernel, team),
        name="give_back",
        out_shape=jax.ShapeDtypeStruct((group_rows, query_width + 2 * width + 256), jnp.bfloat16),
        in_specs=[vmem] * 7,
        out_specs=vmem,
        scratch_shapes=[
            pltpu.VMEM((half, width), jnp.bfloat16),
            pltpu.VMEM((3, half, width), jnp.bfloat16),
            pltpu.SemaphoreType.DMA((3,)),
            pltpu.SemaphoreType.DMA((3,)),
        ],
        cost_estimate=pl.CostEstimate(flops=0, bytes_accessed=3_700_000, transcendentals=0),
        compiler_params=pltpu.CompilerParams(
            collective_id=collective, has_side_effects=True, vmem_limit_bytes=40 * 2**20
        ),
    )(grad_query, grad_key, grad_value, up, cosine, sine, choice)


def start_kernel(ids_ref, piece_ref, ids_out, piece_out, sent, got):
    links = Links(sent, got)
    others = [links.column_peer(step) for step in range(1, lax.axis_size("seq"))]
    links.meet(others)
    copies = []
    for source, target in ((ids_ref, ids_out), (piece_ref, piece_out)):
        copies += [links.send(source, target.at[links.seq_index], other) for other in others]
        target[links.seq_index] = source[...]
    for copy in copies:
        copy.wait_recv()
    links.finish()


def start(collective, seq_count, ids, piece):
    vmem = pl.BlockSpec(memory_space=pltpu.VMEM)
    shape = lambda item: jax.ShapeDtypeStruct((seq_count, *item.shape), item.dtype)
    return pl.pallas_call(
        start_kernel,
        name="start",
        out_shape=[shape(ids), shape(piece)],
        in_specs=[vmem, vmem],
        out_specs=[vmem, vmem],
        scratch_shapes=[pltpu.SemaphoreType.DMA((2 * (seq_count - 1),))] * 2,
        cost_estimate=pl.CostEstimate(flops=0, bytes_accessed=3_700_000, transcendentals=0),
        compiler_params=pltpu.CompilerParams(collective_id=collective, has_side_effects=True),
    )(ids, piece)


def layer_rows_kernel(layer, item_ref, all_ref, sent, got):
    links = Links(sent, got)
    masks, _ = group_masks(layer)
    links.meet([links.layer_peer(mask) for mask in [1] + masks])
    half = item_ref.shape[0] // 2

    def block(mask, part):
        return all_ref.at[pl.ds(part * half, half), flip(links.me, mask)]

    def write(part):
        outer = pl.ds(part * half, half)
        all_ref[outer, pl.ds(links.me, 1)] = item_ref[outer][:, None]

    gather_blocks(links, layer, block, write)
    links.finish()


def layer_rows(collective, layer, item):
    vmem = pl.BlockSpec(memory_space=pltpu.VMEM)
    outer, rows, columns = item.shape
    masks, routed = group_masks(layer)
    copies = 2 * (1 + 2 * len(masks)) + 4 * routed
    return pl.pallas_call(
        functools.partial(layer_rows_kernel, layer),
        name="layer_rows",
        out_shape=jax.ShapeDtypeStruct((outer, layer, rows, columns), item.dtype),
        in_specs=[vmem],
        out_specs=vmem,
        scratch_shapes=[pltpu.SemaphoreType.DMA((copies,))] * 2,
        cost_estimate=pl.CostEstimate(flops=0, bytes_accessed=3_700_000, transcendentals=0),
        compiler_params=pltpu.CompilerParams(collective_id=collective, has_side_effects=True),
    )(item)


def logits_kernel(first_name, rows_ref, head_ref, target_ref, logits_ref, stats_ref):
    count, columns = logits_ref.shape
    width = 1024 if columns % 1024 == 0 else 512
    wanted = target_ref[...].T[:, :1].astype(jnp.int32) - first_name

    def one(at, state):
        peak, summed, picked = state
        spot = pl.ds(pl.multiple_of(at * width, width), width)
        logits = jnp.dot(rows_ref[...], head_ref[:, spot], preferred_element_type=jnp.float32)
        logits_ref[:, spot] = logits
        higher = jnp.maximum(peak, jnp.max(logits, axis=1, keepdims=True))
        summed = summed * jnp.exp(peak - higher) + jnp.sum(
            jnp.exp(logits - higher), axis=1, keepdims=True
        )
        names = lax.broadcasted_iota(jnp.int32, logits.shape, 1) + at * width
        picked = picked + jnp.sum(
            jnp.where(names == wanted, logits, 0.0), axis=1, keepdims=True
        )
        return higher, summed, picked

    column = lambda value: jnp.full((count, 1), value, jnp.float32)
    peak, summed, picked = lax.fori_loop(
        0, columns // width, one, (column(MASKED), column(0.0), column(0.0))
    )
    lane = lax.broadcasted_iota(jnp.int32, (count, 128), 1)
    stats = jnp.where(lane == 0, peak, jnp.where(lane == 1, summed, picked))
    stats_ref[...] = stats.T[:8]


def head_logits(rows, head, targets, first_name):
    count, columns = rows.shape[0], head.shape[1]
    block = min(512, count)
    return pl.pallas_call(
        functools.partial(logits_kernel, first_name),
        name="head_logits",
        grid=(count // block,),
        out_shape=[
            jax.ShapeDtypeStruct((count, columns), jnp.float32),
            jax.ShapeDtypeStruct((8, count), jnp.float32),
        ],
        in_specs=[
            pl.BlockSpec((block, MODEL_WIDTH), lambda at: (at, 0)),
            pl.BlockSpec(head.shape, lambda at: (0, 0)),
            pl.BlockSpec((8, block), lambda at: (0, at)),
        ],
        out_specs=[
            pl.BlockSpec((block, columns), lambda at: (at, 0)),
            pl.BlockSpec((8, block), lambda at: (0, at)),
        ],
        cost_estimate=pl.CostEstimate(flops=0, bytes_accessed=90_000_000, transcendentals=0),
        compiler_params=pltpu.CompilerParams(vmem_limit_bytes=48 * 2**20),
    )(rows, head, targets)


def table_kernel(
    layer, tile, low_ref, ids_ref, small_ref, grad_ref, norm_ref, small_out, held,
    small_in, small_mid, small_up, squares, layer_in, between, seq_in, sent, got,
):
    links = Links(sent, got)
    seq_count = lax.axis_size("seq")
    peers = [links.layer_peer(mask) for mask in range(1, layer)]
    others = [links.column_peer(step) for step in range(1, seq_count)]
    links.meet(peers + others)
    width = held.shape[1]
    rows = low_ref.shape[1]
    tiles = grad_ref.shape[1] // tile
    masks, routed = group_masks(layer)
    half = width // 2

    features_of = lambda index: pl.ds(pl.multiple_of(index * width, 16), width)
    step_lanes = rows * seq_count // 2
    steps = seq_count // 2

    def block(mask, phase):
        return held.at[flip(links.me, mask), :, pl.ds(phase * step_lanes, step_lanes)]

    def half_block(mask, which, phase):
        return held.at[
            flip(links.me, mask), pl.ds(which * half, half), pl.ds(phase * step_lanes, step_lanes)
        ]

    swaps = [
        links.send(
            low_ref.at[features_of(peer[0])],
            held.at[links.me, :, pl.ds((at + 1) * rows, rows)],
            peer,
        )
        for at, peer in enumerate(others)
    ]
    held[links.me, :, :rows] = low_ref[features_of(links.seq_index), :]
    small_rows = small_ref.shape[0] // layer
    rows_of = lambda owner: pl.ds(pl.multiple_of(owner * small_rows, 8), small_rows)
    small_near = [
        links.send(small_ref.at[rows_of(peer[1])], small_in.at[links.me], peer) for peer in peers
    ]
    small_in[links.me] = small_ref[rows_of(links.me), :]

    def add(mask, phase, first=False, last=False):
        owner = flip(links.me, mask)
        lanes = slice(phase * step_lanes, (phase + 1) * step_lanes)

        def one(at, _):
            spot = pl.ds(pl.multiple_of(at * tile, tile), tile)
            ids = ids_ref[pl.ds(owner, 1), lanes]
            wanted = lax.broadcasted_iota(jnp.int32, (tile, step_lanes), 0) + at * tile
            chosen = jnp.where(wanted == ids, 1.0, 0.0).astype(jnp.bfloat16)
            part = against(held[owner, :, lanes], chosen)
            part = part if first else grad_ref[:, spot] + part
            grad_ref[:, spot] = part
            if last:
                squares[...] += jnp.sum((part * part).reshape(-1, 8, tile), axis=0)
            return 0

        lax.fori_loop(0, tiles, one, 0)

    near, out, on, over, last = {}, {}, {}, {}, {}

    def send_own(phase):
        near[phase] = links.send(block(0, phase), block(0, phase), links.layer_peer(1))
        for mask in masks:
            out[mask, phase] = links.send(
                block(0, phase), block(0, phase), links.layer_peer(mask)
            )

    def pass_on(phase):
        for at, mask in enumerate(masks):
            out[mask, phase].wait_recv()
            if routed:
                over[at, phase] = links.send(
                    half_block(mask, at, phase),
                    half_block(mask, at, phase),
                    links.layer_peer(masks[1 - at]),
                )
            on[mask, phase] = links.send(
                block(mask, phase), block(mask, phase), links.layer_peer(1)
            )

    def pass_last(phase):
        for at in range(2):
            over[at, phase].wait_recv()
            last[at, phase] = links.send(
                half_block(6, at, phase), half_block(6, at, phase), links.layer_peer(1)
            )

    def add_last(phase):
        add(6, phase)
        for at in range(2):
            last[at, phase].wait_recv()
        add(7, phase, last=phase == 1)

    squares[...] = jnp.zeros_like(squares)
    for copy in swaps[: steps - 1]:
        copy.wait_recv()
    send_own(0)
    add(0, 0, first=True)
    near[0].wait_recv()
    add(1, 0)
    pass_on(0)
    for mask in masks:
        add(mask, 0)
    for copy in swaps[steps - 1 :]:
        copy.wait_recv()
    send_own(1)
    for copy in small_near:
        copy.wait_recv()
    whole = small_in[0]
    for at in range(1, layer):
        whole = whole + small_in[at]
    small_mid[...] = whole
    small_up[links.seq_index] = whole
    small_ups = [
        links.send(small_mid, small_up.at[links.seq_index], other) for other in others
    ]
    if routed:
        pass_last(0)
    for mask in masks:
        on[mask, 0].wait_recv()
        add(mask ^ 1, 0)
    pass_on(1)
    for copy in small_ups:
        copy.wait_recv()
    whole = small_up[0]
    for at in range(1, seq_count):
        whole = whole + small_up[at]
    small_out[rows_of(links.me), :] = whole
    small_on = [
        links.send(small_out.at[rows_of(links.me)], small_out.at[rows_of(links.me)], peer)
        for peer in peers
    ]
    if routed:
        add_last(0)
    add(0, 1)
    near[1].wait_recv()
    add(1, 1)
    if routed:
        pass_last(1)
    for mask in masks:
        add(mask, 1)
    for mask in masks:
        on[mask, 1].wait_recv()
        add(mask ^ 1, 1, last=not routed and mask == masks[-1])
    if routed:
        add_last(1)
    for copy in small_on:
        copy.wait_recv()
    total = squares[...]
    between[0] = jnp.broadcast_to(jnp.sum(total), (8, 128))
    layer_in[links.me] = between[0]
    copies = [links.send(between.at[0], layer_in.at[links.me], peer) for peer in peers]
    for copy in copies:
        copy.wait_recv()
    whole = layer_in[0]
    for at in range(1, layer):
        whole = whole + layer_in[at]
    between[1] = whole
    seq_in[links.seq_index] = whole
    ups = [links.send(between.at[1], seq_in.at[links.seq_index], other) for other in others]
    for copy in ups:
        copy.wait_recv()
    whole = seq_in[0]
    for at in range(1, seq_count):
        whole = whole + seq_in[at]
    norm_ref[...] = whole
    links.finish()


def table_gradient(collective, seq_count, layer, low, ids, small, table_width):
    vmem = pl.BlockSpec(memory_space=pltpu.VMEM)
    width, rows = MODEL_WIDTH // seq_count, low.shape[1] * seq_count
    tile = min(1024, table_width)
    masks, routed = group_masks(layer)
    copies = (seq_count - 1) * 3 + 3 * (layer - 1) + 2 * (1 + 2 * len(masks) + 4 * routed)
    piece = (small.shape[0] // layer, small.shape[1])
    return pl.pallas_call(
        functools.partial(table_kernel, layer, tile),
        name="table_gradient",
        out_shape=[
            jax.ShapeDtypeStruct((width, table_width), jnp.float32),
            jax.ShapeDtypeStruct((8, 128), jnp.float32),
            jax.ShapeDtypeStruct(small.shape, jnp.float32),
        ],
        in_specs=[vmem] * 3,
        out_specs=[vmem] * 3,
        scratch_shapes=[
            pltpu.VMEM((layer, width, rows), jnp.bfloat16),
            pltpu.VMEM((layer, *piece), jnp.float32),
            pltpu.VMEM(piece, jnp.float32),
            pltpu.VMEM((seq_count, *piece), jnp.float32),
            pltpu.VMEM((8, tile), jnp.float32),
            pltpu.VMEM((layer, 8, 128), jnp.float32),
            pltpu.VMEM((2, 8, 128), jnp.float32),
            pltpu.VMEM((seq_count, 8, 128), jnp.float32),
            pltpu.SemaphoreType.DMA((copies,)),
            pltpu.SemaphoreType.DMA((copies,)),
        ],
        cost_estimate=pl.CostEstimate(flops=0, bytes_accessed=3_700_000, transcendentals=0),
        compiler_params=pltpu.CompilerParams(
            collective_id=collective, has_side_effects=True, vmem_limit_bytes=30 * 2**20
        ),
    )(low, ids, small)


def update_kernel(
    keyval_width, norm_ref, small_ref, moment_ref, weight_ref, gains_ref, gain_first_ref, gain_second_ref,
    grad_ref, table_ref, first_ref, second_ref,
    norm_out, moment_out, weight_out, gains_out, gain_first_out, gain_second_out,
    table_out, first_out, second_out, current, multiplier,
):
    step = pl.program_id(0)
    adapters = 8 * ADAPTER_RANK
    row = lax.broadcasted_iota(jnp.int32, (adapters, MODEL_WIDTH), 0)
    column = lax.broadcasted_iota(jnp.int32, (adapters, MODEL_WIDTH), 1)
    own = (row < 6 * ADAPTER_RANK) | (column < keyval_width)
    piece = 3 * MODEL_WIDTH // (2 * ADAPTER_RANK)
    side = lambda axis: lax.div(
        lax.broadcasted_iota(jnp.int32, (adapters, adapters), axis), jnp.int32(ADAPTER_RANK)
    )
    together = side(0) == side(1)

    def adamw(grad, weight, first, second):
        first = BETA_FIRST * first + (1.0 - BETA_FIRST) * grad
        second = BETA_SECOND * second + (1.0 - BETA_SECOND) * grad * grad
        fixed_second = second * (1.0 / (1.0 - BETA_SECOND**STEP))
        low = fixed_second * lax.rsqrt(fixed_second) + ADAM_EPS
        inverse = pl.reciprocal(low, approx=True)
        inverse = inverse * (2.0 - low * inverse)
        fresh = weight * (1.0 - ADAM_RATE * DECAY_RATE) - (
            ADAM_RATE / (1.0 - BETA_FIRST**STEP)
        ) * (first * inverse)
        return first, second, fresh

    @pl.when(step == 0)
    def _():
        small = small_ref[...]
        loss_spot = (lax.broadcasted_iota(jnp.int32, small.shape, 0) >= 6 * ADAPTER_RANK) & (
            lax.broadcasted_iota(jnp.int32, small.shape, 1) >= keyval_width + piece
        )
        counted = jnp.where(loss_spot, 0.0, small * small)
        norm = jnp.sqrt(norm_ref[...] + jnp.sum(counted))
        norm_out[...] = norm
        multiplier[...] = jnp.minimum(1.0, CLIP_NORM / (norm + 1e-06))
        factor = multiplier[0:1, 0:1]
        grad = jnp.where(own, small[:adapters], 0.0)
        fresh = MUON_MOMENTUM * moment_ref[...] + grad * factor
        moment_out[...] = fresh
        sums = jnp.broadcast_to(jnp.sum(fresh * fresh, axis=1, keepdims=True), (adapters, 128))
        sums = jnp.dot(
            jnp.where(together, 1.0, 0.0), sums, precision=PRECISE, preferred_element_type=jnp.float32
        )
        current[...] = fresh / (jnp.sqrt(sums[:, :1]) + 1e-07)

    @pl.when((step >= 1) & (step <= 5))
    def _():
        now = current[...]
        gram = lax.dot_general(
            now, now, (((1,), (1,)), ((), ())), precision=PRECISE, preferred_element_type=jnp.float32
        )
        gram = jnp.where(together, gram, 0.0)
        square = jnp.dot(gram, gram, precision=PRECISE, preferred_element_type=jnp.float32)
        current[...] = SCHULZ[0] * now + jnp.dot(
            SCHULZ[1] * gram + SCHULZ[2] * square,
            now,
            precision=PRECISE,
            preferred_element_type=jnp.float32,
        )

    @pl.when(step == 6)
    def _():
        stretch = jnp.where(
            row < 6 * ADAPTER_RANK,
            0.2 * math.sqrt(MODEL_WIDTH),
            0.2 * math.sqrt(keyval_width),
        )
        weight_out[...] = (
            weight_ref[...] * (1.0 - MUON_RATE * DECAY_RATE) - MUON_RATE * (current[...] * stretch)
        )

    @pl.when(step == 7)
    def _():
        factor = multiplier[0:1, 0:1]
        base = 6 * ADAPTER_RANK
        grad = small_ref[base : base + 2 * ADAPTER_RANK, keyval_width : keyval_width + piece]
        first, second, fresh = adamw(
            grad * factor, gains_ref[...], gain_first_ref[...], gain_second_ref[...]
        )
        gain_first_out[...] = first
        gain_second_out[...] = second
        gains_out[...] = fresh

    count, columns = table_out.shape
    factor = multiplier[0:1, 0:1]
    wide = min(1024, columns)

    def eight_rows(at, _):
        rows = pl.ds(pl.multiple_of(at * 8, 8), 8)
        here = pl.ds(pl.multiple_of(step * count + at * 8, 8), 8)
        for start in range(0, columns, wide):
            spot = slice(start, start + wide)
            first, second, fresh = adamw(
                grad_ref[here, spot] * factor,
                table_ref[rows, spot],
                first_ref[rows, spot],
                second_ref[rows, spot],
            )
            first_out[rows, spot] = first
            second_out[rows, spot] = second
            table_out[rows, spot] = fresh
        return 0

    lax.fori_loop(0, count // 8, eight_rows, 0)


def update(keyval_width, norm, small, moment, weight, gains, gain_first, gain_second, grad, table, first, second):
    steps = 8
    rows, columns = table.shape
    whole = lambda item: pl.BlockSpec(item.shape, lambda step: (0, 0))
    block = pl.BlockSpec((rows // steps, columns), lambda step: (step, 0))
    vmem = pl.BlockSpec(memory_space=pltpu.VMEM)
    fixed = (norm, small, moment, weight, gains, gain_first, gain_second)
    shape = lambda item: jax.ShapeDtypeStruct(item.shape, jnp.float32)
    kept = (norm, moment, weight, gains, gain_first, gain_second)
    return pl.pallas_call(
        functools.partial(update_kernel, keyval_width),
        name="update",
        grid=(steps,),
        out_shape=[shape(item) for item in kept + (table, first, second)],
        in_specs=[whole(item) for item in fixed]
        + [vmem]
        + [block] * 3,
        out_specs=[whole(item) for item in kept] + [block] * 3,
        scratch_shapes=[
            pltpu.VMEM(moment.shape, jnp.float32),
            pltpu.VMEM((8, 128), jnp.float32),
        ],
        cost_estimate=pl.CostEstimate(flops=0, bytes_accessed=70_000_000, transcendentals=0),
        compiler_params=pltpu.CompilerParams(vmem_limit_bytes=34 * 2**20),
    )(*fixed, grad, table, first, second)


def places(groups, index):
    rows = jnp.arange(groups.shape[0])
    ends = jnp.sum(jnp.where(rows[None, :] <= rows[:, None], groups[None, :], 0), axis=1)
    row_of = jnp.sum((ends[None, :] <= index[:, None]).astype(jnp.int32), axis=1)
    inside = row_of[:, None] == rows[None, :]
    length = jnp.sum(jnp.where(inside, groups[None, :], 0), axis=1)
    row_start = jnp.sum(jnp.where(inside, ends[None, :], 0), axis=1) - length
    source = jnp.where(index > row_start, index - 1, row_start + length - 1)
    return (inside, row_start, length, source)


def other_half(value):
    layer = lax.axis_size("vocab")
    return lax.ppermute(value, "vocab", [(i, (i + layer // MB) % layer) for i in range(layer)])


def on_device(
    token_identifiers,
    targets,
    row_group_index,
    answer_length,
    embedding,
    embedding_first_moment,
    embedding_second_moment,
    output_head_table,
    query_projection,
    keyval_projection,
    output_projection,
    gate_up_projection,
    down_projection,
    gains,
    gain_first_moment,
    gain_second_moment,
    adapter_input_maps,
    input_map_momentum,
    adapter_up_maps,
    up_momentum,
    adapter_keyval_maps,
    keyval_momentum,
):
    seq_count = lax.axis_size("seq")
    layer = lax.axis_size("vocab")
    team = layer // MB
    seq_index = lax.axis_index("seq")
    vocabulary_index = lax.axis_index("vocab")
    batch = vocabulary_index // team
    place = vocabulary_index % team
    other_index = (vocabulary_index + team) % layer
    group_rows = token_identifiers.shape[1]
    half_group = group_rows // 2
    rows = group_rows // team
    table_width = output_head_table.shape[1]
    head_width = query_projection.shape[2]
    heads = head_width // HEAD_SIZE
    hidden = gate_up_projection.shape[2]
    query_width = 4 * head_width

    def move(name, collective, source, *operands, **options):
        return move_tokens(name, collective, team, layer, rows, source, operands, **options)

    def gathered(piece):
        return lax.all_gather(piece, "seq", axis=0, tiled=True)

    keyval_rows = keyval_projection.shape[0] // layer
    keyval_width = KEY_HEADS * HEAD_SIZE
    tokens_all, keyval_piece = start(
        2,
        seq_count,
        token_identifiers.reshape(-1, 128),
        lax.dynamic_slice_in_dim(keyval_projection, vocabulary_index * keyval_rows, keyval_rows, 0),
    )
    keyval_full = layer_rows(3, layer, keyval_piece).reshape(MODEL_WIDTH, 2 * keyval_width)
    near_own = gathered(
        jnp.concatenate(
            [item.reshape(-1, 2 * head_width) for item in (query_projection, output_projection)],
            axis=1,
        )
    )
    feed = gathered(
        jnp.concatenate([gate_up_projection.reshape(-1, 2 * hidden), down_projection], axis=1)
    )
    part_widths = (3 * table_width // 4, table_width // 4)
    part_starts = (0, part_widths[0])

    tokens_flat = tokens_all.reshape(seq_count, MB, team, rows).transpose(1, 2, 0, 3)
    local_ids = tokens_flat.reshape(-1) - vocabulary_index * table_width
    local_ids, keyval_full, near_own = lax.optimization_barrier(
        (local_ids.reshape(layer, -1), keyval_full, near_own)
    )
    near_other = other_half(near_own)
    query_weights = [item[:, : 2 * head_width] for item in (near_own, near_other)]
    out_weights = [item[:, 2 * head_width :] for item in (near_own, near_other)]
    block = (seq_count * rows, MODEL_WIDTH // seq_count)
    residual_in, scale_in, normed_full = move(
        "look_up",
        1,
        from_table,
        local_ids.astype(jnp.float32),
        embedding.astype(jnp.bfloat16),
        reduce="layer",
        middle="forward",
        gain=gains[0:1],
        gather="team",
        column_swap=seq_count,
        extra=(pltpu.VMEM((layer // 2, *block), jnp.bfloat16),),
    )

    (
        normed_full,
        row_group_index,
        adapter_input_maps,
        adapter_up_maps,
        adapter_keyval_maps,
        feed,
    ) = lax.optimization_barrier(
        (
            normed_full,
            row_group_index,
            adapter_input_maps,
            adapter_up_maps,
            adapter_keyval_maps,
            feed,
        )
    )
    gate_own, down_own = feed[:, : 2 * hidden], feed[:, 2 * hidden :]
    gate_weights = (gate_own, other_half(gate_own))

    def padded(values, columns=128):
        return jnp.pad(values, ((0, 0), (0, columns - values.shape[1])))

    def of_slices(values, axis):
        return jnp.stack(
            [
                lax.dynamic_slice_in_dim(values, index * head_width, head_width, axis)
                for index in (vocabulary_index, other_index)
            ],
            axis=axis - 1,
        )

    rank = ADAPTER_RANK
    input_map_lowrank = adapter_input_maps.astype(jnp.bfloat16)
    down_qkv = padded(
        jnp.swapaxes(input_map_lowrank[:3], 0, 1).reshape(MODEL_WIDTH, 3 * rank)
    )
    down_out = padded(
        of_slices(
            input_map_lowrank[3].reshape(2, QUERY_HEADS // 2 * HEAD_SIZE, rank), 1
        ).reshape(query_width, rank)
    )
    up_query_map = (
        of_slices(adapter_up_maps[0].reshape(rank, 2, QUERY_HEADS // 2 * HEAD_SIZE), 2)
        .reshape(rank, query_width)
        .astype(jnp.bfloat16)
    )
    keyval_up = adapter_keyval_maps.astype(jnp.bfloat16)
    linear_width = query_width + 2 * keyval_width
    up_maps = jnp.zeros((128, linear_width), jnp.bfloat16)
    up_maps = up_maps.at[:rank, :query_width].set(up_query_map)
    for which in range(2):
        first = query_width + which * keyval_width
        up_maps = up_maps.at[
            (1 + which) * rank : (2 + which) * rank, first : first + keyval_width
        ].set(keyval_up[which])
    up_output_map = padded(ADAPTER_SCALE * adapter_up_maps[1].astype(jnp.bfloat16).T)
    in_weights = jnp.concatenate([*query_weights, keyval_full, down_qkv, down_qkv], axis=1)
    out_weight = jnp.concatenate([*out_weights, up_output_map], axis=1)

    groups = jnp.where(batch == 0, row_group_index[0], row_group_index[1])
    near = seq_index + jnp.array([0, 1, -1, -2], jnp.int32)
    _, row_start, _, source = places(groups, near)
    positions = (seq_index - row_start[0]) * group_rows + jnp.arange(group_rows)
    lane = jnp.arange(128)
    freqs = ROPE_BASE ** (
        -2.0 * (lane % (HEAD_SIZE // 2)).astype(jnp.float32) / HEAD_SIZE
    )
    angles = positions.astype(jnp.float32)[:, None] * freqs[None, :]
    cosine = jnp.cos(angles)
    sine = jnp.sin(angles) * jnp.where(lane % HEAD_SIZE < HEAD_SIZE // 2, -1.0, 1.0)

    def weighed(found):
        found = jnp.concatenate([found, jnp.zeros((4,), bool)]).astype(jnp.float32)
        return jnp.broadcast_to(found[:, None], (8, 128))

    taken = weighed(source[0] == seq_index + jnp.array([-1, 1, 2, 0], jnp.int32))
    inside = (near >= 0) & (near < seq_count)
    given = weighed(jnp.roll(inside & (source == seq_index), -1))
    linear = jnp.dot(normed_full, in_weights, preferred_element_type=jnp.float32)
    queries, keys, values, adapter_result = project(
        13, team, query_width, linear, up_maps, cosine, sine, taken, feed
    )
    attended, log_totals = attend(heads, queries, keys, values, down_out)
    products = (
        pltpu.VMEM((2 * rows, MODEL_WIDTH), jnp.float32),
        pltpu.VMEM((team // 2, rows, MODEL_WIDTH), jnp.bfloat16),
    )
    residual_mid, scale_mid, mid_full = move(
        "sum_attended",
        4,
        from_product,
        attended,
        out_weight,
        extra=products,
        reduce="team",
        added=residual_in,
        gain=gains[1:2],
        middle="forward",
        gather="team",
    )

    last_piece, down_own, mid_full = lax.optimization_barrier(
        (output_head_table[:, part_starts[1] :], down_own, mid_full)
    )
    down_weights = (down_own, other_half(down_own))
    head_pieces = (
        gathered(output_head_table[:, : part_starts[1]]),
        gathered(last_piece),
    )

    gate_parts, mixed = [], []
    for gate_weight in gate_weights:
        gate_pre = jnp.dot(mid_full, gate_weight, preferred_element_type=jnp.float32)
        gate_part, up_part = (gate_pre[:, :hidden], gate_pre[:, hidden:])
        mixed.append((gate_part * jax.nn.sigmoid(gate_part) * up_part).astype(jnp.bfloat16))
        gate_parts.append(gate_pre)
    mixed, down_other = lax.optimization_barrier((mixed, down_weights[1]))
    down_weights = (down_own, down_other)
    residual_out, scale_out, out_full_rows = move(
        "sum_hidden",
        5,
        from_product,
        mixed[0],
        down_weights[0],
        mixed[1],
        down_weights[1],
        extra=products,
        reduce="team",
        added=residual_mid,
        gain=gains[2:3],
        middle="forward",
        gather="layer",
    )

    (
        out_full_rows,
        answer_length,
        input_map_momentum,
        up_momentum,
        keyval_momentum,
        gain_first_moment,
        gain_second_moment,
        local_ids,
    ) = lax.optimization_barrier(
        (
            out_full_rows,
            answer_length,
            input_map_momentum,
            up_momentum,
            keyval_momentum,
            gain_first_moment,
            gain_second_moment,
            local_ids,
        )
    )

    counted = []
    for each in range(MB):
        inside_row, start_each, length_each, _ = places(row_group_index[each], seq_index[None])
        spots = (seq_index - start_each[0]) * group_rows + jnp.arange(group_rows)
        answers = jnp.sum(jnp.where(inside_row[0], answer_length[each], 0))
        counted.append((spots >= length_each[0] * group_rows - answers).astype(jnp.float32))
    counted = jnp.concatenate(counted)
    local_targets = targets.reshape(-1) - vocabulary_index * table_width
    target_rows = jnp.broadcast_to(
        local_targets.astype(jnp.float32)[None, :], (8, MB * group_rows)
    )
    logit_parts, stats = [], []
    head_parts = len(head_pieces)
    for first, piece in zip(part_starts, head_pieces):
        logits, each = head_logits(out_full_rows, piece, target_rows, first)
        logit_parts.append(logits)
        stats.append(each[:3])
    stats.append(jnp.zeros((8 - 3 * head_parts, MB * group_rows), jnp.float32))
    stats = spread("gather_stats", 6, layer, jnp.concatenate(stats))
    peaks = jnp.concatenate([stats[:, 3 * part] for part in range(head_parts)])
    sums = jnp.concatenate([stats[:, 3 * part + 1] for part in range(head_parts)])
    picked = sum(jnp.sum(stats[:, 3 * part + 2], axis=0) for part in range(head_parts))
    peak = jnp.max(peaks, axis=0)
    log_total = peak + jnp.log(jnp.sum(sums * jnp.exp(peaks - peak[None, :]), axis=0))
    loss_total_sum = jnp.sum(
        counted * (log_total - picked + Z_WEIGHT * log_total * log_total)
    )
    token_count = jnp.sum(counted)
    row_facts = jnp.stack(
        [
            log_total,
            counted * (1.0 + 2.0 * Z_WEIGHT * log_total),
            counted,
            local_targets.astype(jnp.float32),
        ]
        + [jnp.zeros_like(log_total)] * 4
    )
    tile = min(1024, part_widths[1])
    block = (rows, MODEL_WIDTH)
    pairs = layer // 2
    grad_out_res, gain_grad_out, grad_ffn = move(
        "sum_head_grad",
        7,
        from_logits,
        *logit_parts,
        *head_pieces,
        row_facts,
        any_operands=head_parts,
        vmem_mib=56,
        extra=(
            pltpu.VMEM((2, 2 * rows, tile), jnp.float32),
            pltpu.VMEM((2 * rows, MODEL_WIDTH), jnp.float32),
            pltpu.VMEM((pairs, *block), jnp.bfloat16),
            pltpu.SemaphoreType.DMA((2,)),
        ),
        reduce="layer",
        values=residual_out,
        scale=scale_out,
        gain=gains[2:3],
        middle="backward",
        gather="team",
    )

    grad_mid, gain_grad_mid, branch_grad = move(
        "sum_hidden_grad",
        8,
        from_gates,
        *gate_parts,
        grad_ffn,
        down_weights[0],
        gate_weights[0],
        down_weights[1],
        gate_weights[1],
        any_operands=2,
        extra=products
        + (
            pltpu.VMEM((2, 2 * rows, 2 * hidden), jnp.float32),
            pltpu.SemaphoreType.DMA((2,)),
        ),
        vmem_mib=56,
        reduce="team",
        values=residual_mid,
        scale=scale_mid,
        gain=gains[1:2],
        added=grad_out_res,
        middle="backward",
        gather="team",
    )

    grad_mixed = jnp.dot(branch_grad, out_weight, preferred_element_type=jnp.float32)
    grad_query, grad_keys, grad_values = attend_back(
        heads, queries, keys, values, log_totals, grad_mixed, down_out, cosine, sine
    )
    grads = give_back(
        12, team, grad_query, grad_keys, grad_values, up_maps, cosine, sine, given
    )
    _, gain_grad_in, grad_in = move(
        "sum_in_grad",
        9,
        from_product,
        grads,
        in_weights,
        extra=products,
        reduce="team",
        values=residual_in,
        scale=scale_in,
        gain=gains[0:1],
        added=grad_mid,
        middle="backward",
    )

    over_rows = (((0,), (0,)), ((), ()))
    product = lambda left, right: lax.dot_general(
        left, right, over_rows, preferred_element_type=jnp.float32
    )
    down_qkv_grad = product(grads[:, linear_width:], normed_full)
    down_qkv_grad = down_qkv_grad[: 3 * rank] + down_qkv_grad[128 : 128 + 3 * rank]
    up_grads = ADAPTER_SCALE * product(adapter_result, grads[:, :linear_width])
    up_grads = lax.optimization_barrier(
        [
            up_grads[:rank, :query_width],
            up_grads[rank : 2 * rank, query_width : query_width + keyval_width],
            up_grads[2 * rank : 3 * rank, query_width + keyval_width :],
        ]
    )
    adapter_out_grad = grad_mixed[:, query_width : query_width + rank]
    adapter_out_first = adapter_out_grad.astype(jnp.bfloat16)
    adapter_out_rest = (adapter_out_grad - adapter_out_first.astype(jnp.float32)).astype(
        jnp.bfloat16
    )
    down_out_grad = product(
        jnp.concatenate([adapter_out_first, adapter_out_rest], axis=1), attended[:, :query_width]
    )
    down_out_grad = down_out_grad[:rank] + down_out_grad[rank:]
    up_out_grad = ADAPTER_SCALE * product(
        attended[:, query_width : query_width + rank], branch_grad
    )

    def placed(pieces, shape, axis):
        whole = jnp.zeros(shape, jnp.float32)
        for piece, index in zip(pieces, (vocabulary_index, other_index)):
            start = [0] * len(shape)
            start[axis] = index * head_width
            whole = lax.dynamic_update_slice(whole, piece, start)
        return whole

    out_pieces = down_out_grad.reshape(ADAPTER_RANK, 2, 2, head_width)
    down_out_full = placed(
        [out_pieces[:, 0], out_pieces[:, 1]],
        (ADAPTER_RANK, 2, QUERY_HEADS // 2 * HEAD_SIZE),
        2,
    ).reshape(ADAPTER_RANK, MODEL_WIDTH)
    query_pieces = up_grads[0].reshape(ADAPTER_RANK, 2, 2, head_width)
    up_query_full = placed(
        [query_pieces[:, 0], query_pieces[:, 1]],
        (ADAPTER_RANK, 2, QUERY_HEADS // 2 * HEAD_SIZE),
        2,
    ).reshape(ADAPTER_RANK, MODEL_WIDTH)

    gain_grad = jnp.concatenate([gain_grad_in[:1], gain_grad_mid[:1], gain_grad_out[:1]])
    owner = (vocabulary_index == 0).astype(jnp.float32)
    keyval_grads = jnp.concatenate([up_grads[1], up_grads[2]])
    rank = ADAPTER_RANK
    gain_shape = (2 * rank, 3 * MODEL_WIDTH // (2 * rank))
    loss_rows = jnp.zeros((2 * rank, 128), jnp.float32)
    loss_rows = loss_rows.at[0, 0].set(loss_total_sum * owner).at[0, 1].set(token_count * owner)

    def last_rows(*pieces):
        filled = sum(piece.shape[1] for piece in pieces)
        return jnp.concatenate(
            [*pieces, jnp.zeros((2 * rank, MODEL_WIDTH - filled), jnp.float32)], axis=1
        )

    small = jnp.concatenate(
        [
            down_qkv_grad,
            down_out_full,
            up_query_full,
            up_out_grad,
            last_rows(keyval_grads, gain_grad.reshape(gain_shape), loss_rows),
            jnp.zeros((max(0, 8 * layer - 8 * rank), MODEL_WIDTH), jnp.float32),
        ]
    )

    layers = jnp.arange(seq_count)
    below = (seq_index - layers[:, None]) % seq_count == layers[None, :]
    ids_by_step = jnp.sum(
        jnp.where(
            below[None, :, :, None], local_ids.reshape(layer, 1, seq_count, rows), 0
        ),
        axis=2,
    ).reshape(layer, -1)
    table_grad, table_squares, small = table_gradient(
        10, seq_count, layer, grad_in, ids_by_step, small, table_width
    )
    loss_at = keyval_width + gain_shape[1]
    loss_pair = small[6 * rank, loss_at : loss_at + 2]

    def stacked(input_maps, up_maps, keyval_maps):
        return jnp.concatenate(
            [
                jnp.swapaxes(input_maps, 1, 2).reshape(4 * rank, MODEL_WIDTH),
                up_maps.reshape(2 * rank, MODEL_WIDTH),
                last_rows(keyval_maps.reshape(2 * rank, keyval_width)),
            ]
        )

    def unstacked(rows):
        return (
            jnp.swapaxes(rows[: 4 * rank].reshape(4, rank, MODEL_WIDTH), 1, 2),
            rows[4 * rank : 6 * rank].reshape(2, rank, MODEL_WIDTH),
            rows[6 * rank :, :keyval_width].reshape(2, rank, keyval_width),
        )

    (
        gradient_norm,
        moments_next,
        weights_next,
        gains_next,
        gain_first_next,
        gain_second_next,
        embedding_next,
        embedding_first_next,
        embedding_second_next,
    ) = update(
        keyval_width,
        table_squares,
        small,
        stacked(input_map_momentum, up_momentum, keyval_momentum),
        stacked(adapter_input_maps, adapter_up_maps, adapter_keyval_maps),
        gains.reshape(gain_shape),
        gain_first_moment.reshape(gain_shape),
        gain_second_moment.reshape(gain_shape),
        table_grad,
        embedding,
        embedding_first_moment,
        embedding_second_moment,
    )
    gradient_norm = gradient_norm[0, 0]
    gains_next, gain_first_next, gain_second_next = (
        item.reshape(3, MODEL_WIDTH) for item in (gains_next, gain_first_next, gain_second_next)
    )
    input_map_momentum_next, up_momentum_next, keyval_momentum_next = unstacked(moments_next)
    adapter_input_next, adapter_up_next, adapter_keyval_next = unstacked(weights_next)
    return (
        loss_pair[0],
        loss_pair[1],
        gradient_norm,
        embedding_first_next,
        embedding_second_next,
        embedding_next,
        gain_first_next,
        gain_second_next,
        gains_next,
        input_map_momentum_next,
        adapter_input_next,
        up_momentum_next,
        adapter_up_next,
        keyval_momentum_next,
        adapter_keyval_next,
    )


def solution(mesh):
    placed = (
        P(None, "seq"),
        P(None, "seq"),
        P(),
        P(),
        P("seq", "vocab"),
        P("seq", "vocab"),
        P("seq", "vocab"),
        P("seq", "vocab"),
        P("seq", None, "vocab"),
        P("seq", None),
        P("seq", None, "vocab"),
        P("seq", None, "vocab"),
        P("seq", "vocab"),
        P(),
        P(),
        P(),
        P(),
        P(),
        P(),
        P(),
        P(),
        P(),
    )
    return jax.shard_map(
        on_device,
        mesh=mesh,
        in_specs=placed,
        out_specs=(
            P(),
            P(),
            P(),
            P("seq", "vocab"),
            P("seq", "vocab"),
            P("seq", "vocab"),
            P(),
            P(),
            P(),
            P(),
            P(),
            P(),
            P(),
            P(),
            P(),
        ),
        check_vma=False,
    )
```
